32 devices in a mesh: row: 2 (over x), col: 4 (over z), layer: 4 (over y, core).
Axes of the slice: x: 2, y: 2, z: 4, core: 2. Of those that a mesh axis runs over, the one named last changes fastest.
Arguments:
- hamiltonian: bfloat16 [2048, 2048], P('row', ('col', 'layer')), as said below
- inv_root: bfloat16 [2048, 2048], P('row', 'col'), as said below
- h_pattern: int32 [8, 8], replicated, may hold values from 0 to 1, as said below
- z_pattern: int32 [8, 8], replicated, may hold values from 0 to 1, as said below
Outputs:
- transformed: bfloat16 [2048, 2048], P('row', ('col', 'layer'))
The draws below stay inside these ranges and needn't reach their ends.
Inputs may be any that keep to these rules, and one draw needn't show every extreme that they name: hamiltonian is symmetric. inv_root is symmetric. h_pattern is symmetric and every diagonal block is present. z_pattern is symmetric and every diagonal block is present.
All inputs are finite; a program needn't handle non-finite values.
Results may differ from the reference program's by a relative error of at most 0.005.
Values may be sent and summed in bfloat16 or wider, within the bound.
No kernel may reach another device: no remote copies, remote signals or barrier semaphores. Data moves between devices by JAX's collectives and lax.ppermute only.
A program may use at most 64 MiB of HBM per device.

```python
import math
import jax
import jax.numpy as jnp

BLOCKS = 8
ORDER = 2048


def symmetric_noise(key):
    base = jax.random.truncated_normal(key, -4.0, 4.0, (ORDER, ORDER), jnp.float32)
    return (base + base.T) * 0.70710678


def block_pattern(key):
    reach = BLOCKS // 8
    scores = jax.random.randint(key, (BLOCKS, BLOCKS), 0, 100)
    paired = jnp.minimum(scores, scores.T)
    first = jnp.arange(BLOCKS, dtype=jnp.int32)[:, None]
    second = jnp.arange(BLOCKS, dtype=jnp.int32)[None, :]
    near = jnp.abs(first - second) <= reach
    return jnp.where(near | (paired < 30), 1, 0).astype(jnp.int32)


def draw_hamiltonian(key, part):
    noise = symmetric_noise(jax.random.fold_in(key, 11))
    return (noise * (1.6 / math.sqrt(ORDER))).astype(jnp.bfloat16)


def draw_inv_root(key, part):
    noise = symmetric_noise(jax.random.fold_in(key, 23))
    unit = jnp.eye(ORDER, dtype=jnp.float32)
    return (unit + noise * (0.632 / math.sqrt(ORDER))).astype(jnp.bfloat16)


def draw_h_pattern(key, part):
    return block_pattern(jax.random.fold_in(key, 37))


def draw_z_pattern(key, part):
    return block_pattern(jax.random.fold_in(key, 41))


def setup_inputs(seed: int = 0) -> dict:
    key_list = jax.random.split(jax.random.key(seed), 5)
    return {
        "hamiltonian": draw_hamiltonian(jax.random.fold_in(key_list[4], 71), 0),
        "inv_root": draw_inv_root(jax.random.fold_in(key_list[4], 71), 0),
        "h_pattern": draw_h_pattern(jax.random.fold_in(key_list[4], 71), 0),
        "z_pattern": draw_z_pattern(jax.random.fold_in(key_list[4], 71), 0),
    }


def apply_pattern(matrix, pattern):
    blocks = pattern.shape[0]
    size = matrix.shape[0] // blocks
    shaped = matrix.reshape(blocks, size, blocks, size)
    keep = (pattern > 0)[:, None, :, None]
    kept = jnp.where(keep, shaped, jnp.zeros_like(shaped))
    return kept.reshape(matrix.shape)


def reference(hamiltonian, inv_root, h_pattern, z_pattern):
    masked_hamiltonian = apply_pattern(hamiltonian, h_pattern)
    masked_root = apply_pattern(inv_root, z_pattern)
    product = jnp.dot(masked_hamiltonian, masked_root, preferred_element_type=jnp.float32).astype(jnp.bfloat16)
    transformed = jnp.dot(masked_root.T, product, preferred_element_type=jnp.float32)
    return transformed.astype(jnp.bfloat16)
```

```python
import functools

import jax
import jax.numpy as jnp
from jax import lax
from jax.experimental import pallas as pl
from jax.experimental.pallas import tpu as pltpu
from jax.sharding import PartitionSpec as P

BS = 256
VMEM_LIMIT = 48 * 1024 * 1024


def bits_of(size):
    return [1 << b for b in reversed(range(size.bit_length() - 1))]


def flip(size, bit):
    return [(i, i ^ bit) for i in range(size)]


def mod(a, n):
    return lax.rem(a + n, n)


def keep_block(pattern, i, j, block):
    return jnp.where(pattern[i, j] > 0, block, jnp.zeros_like(block))


def first_kernel(sizes, h_offsets, *refs):
    rows, cols, layers, rows_here, cols_here = sizes
    hp, zp = refs[0], refs[1]
    z_slots = refs[2 : 2 + cols]
    h_pieces = refs[2 + cols : 2 + cols + len(h_offsets)]
    out_a, out_b, zm, hm, xs = refs[2 + cols + len(h_offsets) :]
    r, c, l = lax.axis_index("row"), lax.axis_index("col"), lax.axis_index("layer")
    quarter = cols_here // layers
    per_tile = cols_here // BS
    per_rows = rows_here // BS
    block_row = r * layers + l
    for s in range(cols):
        cc = mod(c - s, cols)
        for t in range(per_tile):
            j = cc * per_tile + t
            zm[:, pl.ds(pl.multiple_of(j * BS, BS), BS)] = keep_block(
                zp, block_row, j, z_slots[s][:, t * BS : (t + 1) * BS]
            )
    for (dr, dl), piece in zip(h_offsets, h_pieces):
        rr, ll = r ^ dr, l ^ dl
        block_col = (c * cols_here + ll * quarter) // BS
        for q in range(per_rows):
            j = rr * per_rows + q
            hm[
                pl.ds(pl.multiple_of(j * BS, BS), BS),
                pl.ds(pl.multiple_of(ll * quarter, quarter), quarter),
            ] = keep_block(hp, j, block_col, piece[q * BS : (q + 1) * BS, :])
    total = None
    order = zm.shape[1]
    chunk = min(order, 2048)
    for k in range(0, order, chunk):
        part = jnp.dot(
            zm[:, k : k + chunk], hm[k : k + chunk, :], preferred_element_type=jnp.float32
        )
        total = part if total is None else total + part
    xs[...] = total.astype(jnp.bfloat16)
    half = lax.rem(c, 2)
    out_a[...] = xs[pl.ds(pl.multiple_of(half * quarter, quarter), quarter), :]
    out_b[...] = xs[pl.ds(pl.multiple_of((1 - half) * quarter, quarter), quarter), :]


def second_kernel(sizes, z_offsets, *refs):
    rows, cols, layers, rows_here, cols_here = sizes
    zp, z_tile = refs[0], refs[1]
    n_slots = len(z_offsets) * (cols - 1)
    slots = refs[2 : 2 + n_slots]
    messages = refs[2 + n_slots : 2 + n_slots + cols]
    out, xm = refs[2 + n_slots + cols :]
    r, c, l = lax.axis_index("row"), lax.axis_index("col"), lax.axis_index("layer")
    per_tile = cols_here // BS
    index = r * 2 + lax.rem(l, 2)
    for j in range(cols):
        xm[mod(index - j, cols)] = messages[j][...]
    for n, dl in enumerate(z_offsets):
        ll = l ^ dl
        block_row = r * layers + ll
        total = None
        for s in range(cols):
            cc = mod(c - s, cols)
            if s == 0:
                piece = z_tile[pl.ds(pl.multiple_of(ll * BS, BS), BS), :]
            else:
                piece = slots[n * (cols - 1) + s - 1][...]
            masked = jnp.concatenate(
                [
                    keep_block(zp, block_row, cc * per_tile + t, piece[:, t * BS : (t + 1) * BS])
                    for t in range(per_tile)
                ],
                axis=1,
            )
            part = lax.dot_general(
                masked, xm[cc], (((1,), (1,)), ((), ())), preferred_element_type=jnp.float32
            )
            total = part if total is None else total + part
        out[pl.ds(pl.multiple_of(ll * BS, BS), BS), :] = total.astype(out.dtype)


def local(sizes, hamiltonian, inv_root, h_pattern, z_pattern):
    rows, cols, layers, rows_here, cols_here = sizes
    quarter = cols_here // layers
    order = rows * rows_here
    l = lax.axis_index("layer")
    smem = pl.BlockSpec(memory_space=pltpu.SMEM)
    vmem = pl.BlockSpec(memory_space=pltpu.VMEM)

    own = lax.dynamic_slice_in_dim(inv_root, l * BS, BS, 0)
    ring = [(i, (i + 1) % cols) for i in range(cols)]
    z_slots = [own]
    for _ in range(1, cols):
        z_slots.append(lax.ppermute(z_slots[-1], "col", ring))

    h_pieces = {(0, 0): hamiltonian}
    row_bits, layer_bits = bits_of(rows), bits_of(layers)
    steps = [("layer", layers, layer_bits[0])]
    steps += [("row", rows, b) for b in row_bits]
    steps += [("layer", layers, b) for b in layer_bits[1:]]
    for axis, size, bit in steps:
        for (dr, dl), piece in list(h_pieces.items()):
            there = (dr ^ bit, dl) if axis == "row" else (dr, dl ^ bit)
            h_pieces[there] = lax.ppermute(piece, axis, flip(size, bit))
    h_offsets = list(h_pieces)

    shared = {0: z_slots[1:]}
    for bit in layer_bits:
        for dl, pieces in list(shared.items()):
            shared[dl ^ bit] = [lax.ppermute(p, "layer", flip(layers, bit)) for p in pieces]
    z_offsets = list(shared)

    half = jax.ShapeDtypeStruct((quarter, cols_here), jnp.bfloat16)
    x_a, x_b = pl.pallas_call(
        functools.partial(first_kernel, sizes, h_offsets),
        out_shape=[half, half],
        in_specs=[smem, smem] + [vmem] * (cols + len(h_offsets)),
        out_specs=[vmem, vmem],
        scratch_shapes=[
            pltpu.VMEM((BS, order), jnp.bfloat16),
            pltpu.VMEM((order, cols_here), jnp.bfloat16),
            pltpu.VMEM((BS, cols_here), jnp.bfloat16),
        ],
        compiler_params=pltpu.CompilerParams(vmem_limit_bytes=VMEM_LIMIT),
        name="first_product",
    )(h_pattern, z_pattern, *z_slots, *[h_pieces[o] for o in h_offsets])

    per_tile = cols_here // BS
    messages = []
    for j in range(cols):
        perm = []
        for r in range(rows):
            for c in range(cols):
                for l_ in range(layers):
                    block = r * layers + l_
                    there_r, there_half = divmod((c + j) % cols, 2)
                    b, y = divmod(block, per_tile)
                    there_l = y * 2 + there_half
                    perm.append(
                        ((r * cols + c) * layers + l_, (there_r * cols + b) * layers + there_l)
                    )
        messages.append(lax.ppermute(x_b if j % 2 else x_a, ("row", "col", "layer"), perm))

    flat = [p for o in z_offsets for p in shared[o]]
    return pl.pallas_call(
        functools.partial(second_kernel, sizes, z_offsets),
        out_shape=jax.ShapeDtypeStruct(hamiltonian.shape, jnp.bfloat16),
        in_specs=[smem] + [vmem] * (1 + len(flat) + cols),
        out_specs=vmem,
        scratch_shapes=[pltpu.VMEM((cols, quarter, cols_here), jnp.bfloat16)],
        compiler_params=pltpu.CompilerParams(vmem_limit_bytes=VMEM_LIMIT),
        name="second_product",
    )(z_pattern, inv_root, *flat, *messages)


def solution(mesh):
    rows, cols, layers = (mesh.shape[a] for a in ("row", "col", "layer"))

    def whole(hamiltonian, inv_root, h_pattern, z_pattern):
        order = hamiltonian.shape[0]
        sizes = (rows, cols, layers, order // rows, order // cols)
        return jax.shard_map(
            functools.partial(local, sizes),
            mesh=mesh,
            in_specs=(P("row", ("col", "layer")), P("row", "col"), P(), P()),
            out_specs=P("row", ("col", "layer")),
            check_vma=False,
        )(hamiltonian, inv_root, h_pattern, z_pattern)

    return whole
```

```python
import functools
from typing import NamedTuple

import jax
import jax.numpy as jnp
from jax import lax
from jax.experimental import pallas as pl
from jax.experimental.pallas import tpu as pltpu
from jax.sharding import PartitionSpec as P

BS = 256
VMEM_LIMIT = 48 * 1024 * 1024


class Sizes(NamedTuple):
    rows: int
    cols: int
    layers: int
    rows_here: int
    cols_here: int
    quarter: int
    per: int


def bits_of(size):
    return [1 << b for b in reversed(range(size.bit_length() - 1))]


def flip(size, bit):
    return [(i, i ^ bit) for i in range(size)]


def mod(a, n):
    return lax.rem(a + n, n)


def keep_block(pattern, i, j, block):
    return jnp.where(pattern[i, j] > 0, block, jnp.zeros_like(block))


def strip_rows(r, l, half, sizes):
    return pl.multiple_of(half * sizes.cols_here + l * sizes.quarter, sizes.quarter)


def strip_block(r, l, half, sizes):
    return (r * sizes.rows_here + half * sizes.cols_here + l * sizes.quarter) // BS


def mask_row(zp, block_row, first_block, piece):
    parts = [
        keep_block(zp, block_row, first_block + t, piece[:, t * BS : (t + 1) * BS])
        for t in range(piece.shape[1] // BS)
    ]
    return jnp.concatenate(parts, axis=1)


def first_kernel(sizes, h_offsets, *refs):
    cols, layers, quarter = sizes.cols, sizes.layers, sizes.quarter
    hp, zp = refs[0], refs[1]
    z_slots = refs[2 : 2 + cols]
    h_pieces = refs[2 + cols : 2 + cols + len(h_offsets)]
    out, zm, hm = refs[2 + cols + len(h_offsets) :]
    r, c, l = lax.axis_index("row"), lax.axis_index("col"), lax.axis_index("layer")
    per_tile = sizes.cols_here // BS
    per_rows = sizes.rows_here // BS
    for s in range(cols):
        cc = mod(c - s, cols)
        for half in range(sizes.per):
            rows = slice(half * quarter, (half + 1) * quarter)
            block_row = strip_block(r, l, half, sizes)
            zm[
                rows, pl.ds(pl.multiple_of(cc * sizes.cols_here, sizes.cols_here), sizes.cols_here)
            ] = mask_row(zp, block_row, cc * per_tile, z_slots[s][rows, :])
    for (dr, dl), piece in zip(h_offsets, h_pieces):
        rr, ll = r ^ dr, l ^ dl
        block_col = (c * sizes.cols_here + ll * quarter) // BS
        for q in range(per_rows):
            j = rr * per_rows + q
            hm[
                pl.ds(pl.multiple_of(j * BS, BS), BS),
                pl.ds(pl.multiple_of(ll * quarter, quarter), quarter),
            ] = keep_block(hp, j, block_col, piece[q * BS : (q + 1) * BS, :])
    total = None
    order = zm.shape[1]
    chunk = min(order, 2048)
    for k in range(0, order, chunk):
        part = jnp.dot(
            zm[:, k : k + chunk], hm[k : k + chunk, :], preferred_element_type=jnp.float32
        )
        total = part if total is None else total + part
    out[...] = total.astype(jnp.bfloat16)


def route_kernel(sizes, row_offsets, *refs):
    n = len(row_offsets)
    pieces, outs, table = refs[:n], refs[n:-1], refs[-1]
    r, c = lax.axis_index("row"), lax.axis_index("col")
    for dr, piece in zip(row_offsets, pieces):
        for half in range(sizes.per):
            table[(r ^ dr) * sizes.per + half] = piece[
                half * sizes.quarter : (half + 1) * sizes.quarter, :
            ]
    for d, out in enumerate(outs):
        out[...] = table[c ^ d]


def second_kernel(sizes, z_offsets, *refs):
    cols, quarter = sizes.cols, sizes.quarter
    zp, z_tile = refs[0], refs[1]
    n_slots = len(z_offsets) * (cols - 1)
    slots = refs[2 : 2 + n_slots]
    messages = refs[2 + n_slots : 2 + n_slots + cols]
    out, xm = refs[2 + n_slots + cols :]
    r, c, l = lax.axis_index("row"), lax.axis_index("col"), lax.axis_index("layer")
    per_tile = sizes.cols_here // BS
    for d in range(cols):
        xm[c ^ d] = messages[d][...]
    for n, dl in enumerate(z_offsets):
        ll = l ^ dl
        total = None
        for s in range(cols):
            cc = mod(c - s, cols)
            strips = []
            for half in range(sizes.per):
                if s == 0:
                    strip = z_tile[pl.ds(strip_rows(r, ll, half, sizes), quarter), :]
                else:
                    strip = slots[n * (cols - 1) + s - 1][half * quarter : (half + 1) * quarter, :]
                strips.append(mask_row(zp, strip_block(r, ll, half, sizes), cc * per_tile, strip))
            part = lax.dot_general(
                jnp.concatenate(strips, axis=0),
                xm[cc],
                (((1,), (1,)), ((), ())),
                preferred_element_type=jnp.float32,
            )
            total = part if total is None else total + part
        for half in range(sizes.per):
            out[pl.ds(strip_rows(r, ll, half, sizes), quarter), :] = total[
                half * quarter : (half + 1) * quarter, :
            ].astype(out.dtype)


def local(sizes, hamiltonian, inv_root, h_pattern, z_pattern):
    rows, cols, layers = sizes.rows, sizes.cols, sizes.layers
    quarter, cols_here = sizes.quarter, sizes.cols_here
    order = rows * sizes.rows_here
    strip_height = sizes.per * quarter
    l = lax.axis_index("layer")
    smem = pl.BlockSpec(memory_space=pltpu.SMEM)
    vmem = pl.BlockSpec(memory_space=pltpu.VMEM)
    params = pltpu.CompilerParams(vmem_limit_bytes=VMEM_LIMIT)

    striped = inv_root.reshape(sizes.per, layers, quarter, cols_here)
    own = lax.dynamic_index_in_dim(striped, l, 1, keepdims=False).reshape(strip_height, cols_here)
    ring = [(i, (i + 1) % cols) for i in range(cols)]
    z_slots = [own]
    for _ in range(1, cols):
        z_slots.append(lax.ppermute(z_slots[-1], "col", ring))

    h_pieces = {(0, 0): hamiltonian}
    row_bits, layer_bits = bits_of(rows), bits_of(layers)
    steps = [("layer", layers, layer_bits[0])]
    steps += [("row", rows, b) for b in row_bits]
    steps += [("layer", layers, b) for b in layer_bits[1:]]
    for axis, size, bit in steps:
        for (dr, dl), piece in list(h_pieces.items()):
            there = (dr ^ bit, dl) if axis == "row" else (dr, dl ^ bit)
            h_pieces[there] = lax.ppermute(piece, axis, flip(size, bit))
    h_offsets = list(h_pieces)

    shared = {0: z_slots[1:]}
    for bit in layer_bits:
        for dl, pieces in list(shared.items()):
            shared[dl ^ bit] = [lax.ppermute(p, "layer", flip(layers, bit)) for p in pieces]
    z_offsets = list(shared)

    product = pl.pallas_call(
        functools.partial(first_kernel, sizes, h_offsets),
        out_shape=jax.ShapeDtypeStruct((strip_height, cols_here), jnp.bfloat16),
        in_specs=[smem, smem] + [vmem] * (cols + len(h_offsets)),
        out_specs=vmem,
        scratch_shapes=[
            pltpu.VMEM((strip_height, order), jnp.bfloat16),
            pltpu.VMEM((order, cols_here), jnp.bfloat16),
        ],
        compiler_params=params,
        name="first_product",
    )(h_pattern, z_pattern, *z_slots, *[h_pieces[o] for o in h_offsets])

    gathered = {0: product}
    for bit in row_bits:
        for dr, piece in list(gathered.items()):
            gathered[dr ^ bit] = lax.ppermute(piece, "row", flip(rows, bit))
    row_offsets = list(gathered)
    strip = jax.ShapeDtypeStruct((quarter, cols_here), jnp.bfloat16)
    outgoing = pl.pallas_call(
        functools.partial(route_kernel, sizes, row_offsets),
        out_shape=[strip] * cols,
        in_specs=[vmem] * rows,
        out_specs=[vmem] * cols,
        scratch_shapes=[pltpu.VMEM((cols, quarter, cols_here), jnp.bfloat16)],
        compiler_params=params,
        name="route",
    )(*[gathered[o] for o in row_offsets])
    messages = [outgoing[0]] + [
        lax.ppermute(outgoing[d], "col", flip(cols, d)) for d in range(1, cols)
    ]

    flat = [p for o in z_offsets for p in shared[o]]
    return pl.pallas_call(
        functools.partial(second_kernel, sizes, z_offsets),
        out_shape=jax.ShapeDtypeStruct(hamiltonian.shape, jnp.bfloat16),
        in_specs=[smem] + [vmem] * (1 + len(flat) + cols),
        out_specs=vmem,
        scratch_shapes=[pltpu.VMEM((cols, quarter, cols_here), jnp.bfloat16)],
        compiler_params=params,
        name="second_product",
    )(z_pattern, inv_root, *flat, *messages)


def solution(mesh):
    rows, cols, layers = (mesh.shape[a] for a in ("row", "col", "layer"))

    def whole(hamiltonian, inv_root, h_pattern, z_pattern):
        order = hamiltonian.shape[0]
        cols_here = order // cols
        sizes = Sizes(
            rows, cols, layers, order // rows, cols_here, cols_here // layers, cols // rows
        )
        return jax.shard_map(
            functools.partial(local, sizes),
            mesh=mesh,
            in_specs=(P("row", ("col", "layer")), P("row", "col"), P(), P()),
            out_specs=P("row", ("col", "layer")),
            check_vma=False,
        )(hamiltonian, inv_root, h_pattern, z_pattern)

    return whole
```

```python
import functools
from typing import NamedTuple

import jax
import jax.numpy as jnp
from jax import lax
from jax.experimental import pallas as pl
from jax.experimental.pallas import tpu as pltpu
from jax.sharding import PartitionSpec as P

BS = 256
VMEM_LIMIT = 48 * 1024 * 1024


class Sizes(NamedTuple):
    rows: int
    cols: int
    layers: int
    rows_here: int
    cols_here: int
    quarter: int
    per: int
    sub: int


def bits_of(size):
    return [1 << b for b in reversed(range(size.bit_length() - 1))]


def flip(size, bit):
    return [(i, i ^ bit) for i in range(size)]


def mod(a, n):
    return lax.rem(a + n, n)


def keep_block(pattern, i, j, block):
    return jnp.where(pattern[i, j] > 0, block, jnp.zeros_like(block))


def strip_rows(l, half, part, sizes):
    start = half * sizes.cols_here + l * sizes.quarter + part * sizes.sub
    return pl.multiple_of(start, sizes.sub)


def strip_block(r, l, half, sizes):
    return (r * sizes.rows_here + half * sizes.cols_here + l * sizes.quarter) // BS


def mask_row(zp, block_row, first_block, piece):
    parts = [
        keep_block(zp, block_row, first_block + t, piece[:, t * BS : (t + 1) * BS])
        for t in range(piece.shape[1] // BS)
    ]
    return jnp.concatenate(parts, axis=1)


def mask_part(zp, r, l, cc, piece, sizes):
    first_block = cc * (sizes.cols_here // BS)
    return jnp.concatenate(
        [
            mask_row(
                zp,
                strip_block(r, l, half, sizes),
                first_block,
                piece[half * sizes.sub : (half + 1) * sizes.sub, :],
            )
            for half in range(sizes.per)
        ],
        axis=0,
    )


def columns_of(cc, sizes):
    return pl.ds(pl.multiple_of(cc * sizes.cols_here, sizes.cols_here), sizes.cols_here)


def cut_kernel(sizes, z_ref, h_ref, *refs):
    outs, sems = refs[:3], refs[3]
    l = lax.axis_index("layer")
    copies = [pltpu.make_async_copy(h_ref, outs[2], sems.at[2 * sizes.per])]
    copies[0].start()
    for part in range(2):
        for half in range(sizes.per):
            copy = pltpu.make_async_copy(
                z_ref.at[pl.ds(strip_rows(l, half, part, sizes), sizes.sub), :],
                outs[part].at[pl.ds(half * sizes.sub, sizes.sub), :],
                sems.at[part * sizes.per + half],
            )
            copy.start()
            copies.append(copy)
    for copy in copies:
        copy.wait()


def pack_kernel(n, *refs):
    out, row = refs[-1], 0
    for ref in refs[:n]:
        out[row : row + ref.shape[0], :] = ref[...]
        row += ref.shape[0]


def pack(pieces, after=()):
    height = sum(p.shape[0] for p in pieces)
    return pl.pallas_call(
        functools.partial(pack_kernel, len(pieces)),
        out_shape=jax.ShapeDtypeStruct((height, pieces[0].shape[1]), pieces[0].dtype),
        in_specs=[pl.BlockSpec(memory_space=pltpu.VMEM)] * len(pieces)
        + [pl.BlockSpec(memory_space=pl.ANY)] * len(after),
        out_specs=pl.BlockSpec(memory_space=pltpu.VMEM),
        compiler_params=pltpu.CompilerParams(vmem_limit_bytes=VMEM_LIMIT),
        name="pack",
    )(*pieces, *after)


def first_kernel(sizes, h_table, n_early, *refs):
    cols, quarter, height = sizes.cols, sizes.quarter, sizes.per * sizes.sub
    hp, zp = refs[0], refs[1]
    parts = (refs[2 : 2 + n_early], refs[2 + n_early : 2 + 2 * n_early])
    h_refs = refs[2 + 2 * n_early : -3]
    hm, total, zm = refs[-3:]
    r, c, l = lax.axis_index("row"), lax.axis_index("col"), lax.axis_index("layer")
    per_rows = sizes.rows_here // BS
    for part, sign in ((0, -1), (1, 1)):
        rows = slice(part * height, (part + 1) * height)
        for s in range(n_early):
            cc = mod(c + sign * s, cols)
            zm[rows, columns_of(cc, sizes)] = mask_part(zp, r, l, cc, parts[part][s][...], sizes)
        for s in range(n_early, cols):
            cc = mod(c + sign * s, cols)
            zm[rows, columns_of(cc, sizes)] = jnp.zeros((height, sizes.cols_here), zm.dtype)
    for index, row, dr, dl in h_table:
        piece = h_refs[index]
        rr, ll = r ^ dr, l ^ dl
        block_col = (c * sizes.cols_here + ll * quarter) // BS
        for q in range(per_rows):
            j = rr * per_rows + q
            hm[
                pl.ds(pl.multiple_of(j * BS, BS), BS),
                pl.ds(pl.multiple_of(ll * quarter, quarter), quarter),
            ] = keep_block(hp, j, block_col, piece[row + q * BS : row + (q + 1) * BS, :])
    order = zm.shape[1]
    chunk = min(order, 2048)
    acc = None
    for k in range(0, order, chunk):
        part = jnp.dot(
            zm[:, k : k + chunk], hm[k : k + chunk, :], preferred_element_type=jnp.float32
        )
        acc = part if acc is None else acc + part
    total[...] = acc


def finish_kernel(sizes, zp, hm, total, right, left, out):
    cols, height = sizes.cols, sizes.per * sizes.sub
    r, c, l = lax.axis_index("row"), lax.axis_index("col"), lax.axis_index("layer")
    for part, sign, piece in ((0, -1, right), (1, 1, left)):
        cc = mod(c + sign * (cols - 1), cols)
        rows = slice(part * height, (part + 1) * height)
        added = jnp.dot(
            mask_part(zp, r, l, cc, piece[...], sizes),
            hm[columns_of(cc, sizes), :],
            preferred_element_type=jnp.float32,
        )
        out[rows, :] = (total[rows, :] + added).astype(out.dtype)


def route_kernel(sizes, row_offsets, *refs):
    n = len(row_offsets)
    pieces, table = refs[:n], refs[n]
    r = lax.axis_index("row")
    sub, height = sizes.sub, sizes.per * sizes.sub
    for dr, piece in zip(row_offsets, pieces):
        for half in range(sizes.per):
            for part in range(2):
                first = part * height + half * sub
                table[(r ^ dr) * sizes.per + half, part * sub : (part + 1) * sub, :] = piece[
                    first : first + sub, :
                ]


def place_rows(out, ll, rows, first, sizes):
    for part in range(2):
        for half in range(sizes.per):
            out[pl.ds(strip_rows(ll, half, part, sizes), sizes.sub), :] = rows[
                first : first + sizes.sub, :
            ].astype(out.dtype)
            first += sizes.sub


def second_kernel(sizes, z_table, offsets, ready, *refs):
    cols, sub, height = sizes.cols, sizes.sub, sizes.per * sizes.sub
    zp, z_tile, xm = refs[:3]
    out = refs[-1]
    held = refs[4:-1] if ready else refs[3:-1]
    r, c, l = lax.axis_index("row"), lax.axis_index("col"), lax.axis_index("layer")
    for n, dl in enumerate(ready):
        place_rows(out, l ^ dl, refs[3], n * 2 * height, sizes)
    for n, dl in enumerate(offsets):
        ll = l ^ dl
        total = None
        for s in range(cols):
            cc = mod(c - s, cols)
            parts = []
            for part in range(2):
                if s == 0:
                    piece = jnp.concatenate(
                        [
                            z_tile[pl.ds(strip_rows(ll, half, part, sizes), sub), :]
                            for half in range(sizes.per)
                        ],
                        axis=0,
                    )
                else:
                    index, row = z_table[dl, s if part == 0 else cols - s, part]
                    piece = held[index][row : row + height, :]
                parts.append(mask_part(zp, r, ll, cc, piece, sizes))
            part = lax.dot_general(
                jnp.concatenate(parts, axis=0),
                xm[cc],
                (((1,), (1,)), ((), ())),
                preferred_element_type=jnp.float32,
            )
            total = part if total is None else total + part
        if ready:
            place_rows(out, ll, total, 0, sizes)
        else:
            out[n * 2 * height : (n + 1) * 2 * height, :] = total.astype(out.dtype)


def local(sizes, hamiltonian, inv_root, h_pattern, z_pattern):
    rows, cols, layers = sizes.rows, sizes.cols, sizes.layers
    quarter, cols_here = sizes.quarter, sizes.cols_here
    order = rows * sizes.rows_here
    height = sizes.per * sizes.sub
    smem = pl.BlockSpec(memory_space=pltpu.SMEM)
    vmem = pl.BlockSpec(memory_space=pltpu.VMEM)
    params = pltpu.CompilerParams(vmem_limit_bytes=VMEM_LIMIT)
    row_bits, layer_bits = bits_of(rows), bits_of(layers)

    own = pl.pallas_call(
        functools.partial(cut_kernel, sizes),
        out_shape=[jax.ShapeDtypeStruct((height, cols_here), jnp.bfloat16)] * 2
        + [jax.ShapeDtypeStruct(hamiltonian.shape, jnp.bfloat16)],
        in_specs=[pl.BlockSpec(memory_space=pl.ANY)] * 2,
        out_specs=[vmem] * 3,
        scratch_shapes=[pltpu.SemaphoreType.DMA((2 * sizes.per + 1,))],
        compiler_params=params,
        name="cut",
    )(inv_root, hamiltonian)
    rings = [[(i, (i + step) % cols) for i in range(cols)] for step in (1, -1)]
    slots = [[own[0]], [own[1]]]
    for _ in range(1, cols):
        for part in range(2):
            slots[part].append(lax.ppermute(slots[part][-1], "col", rings[part]))

    top, rest = layer_bits[0], layer_bits[1:]
    h_arrays, h_table = [own[2]], [(0, 0, 0, 0)]
    steps = [("row", b) for b in row_bits] + [("layer", top)]
    for axis, bit in steps:
        for index, _, dr, dl in list(h_table):
            there = (dr ^ bit, dl) if axis == "row" else (dr, dl ^ bit)
            size = rows if axis == "row" else layers
            h_table.append((len(h_arrays), 0) + there)
            source = h_arrays[index]
            if index:
                source = pack([source], [slots[0][1], slots[1][1]])
            h_arrays.append(lax.ppermute(source, axis, flip(size, bit)))
    for bit in rest:
        packed = pack(h_arrays, [slots[0][-2], slots[1][-2]])
        place, starts = 0, []
        for array in h_arrays:
            starts.append(place)
            place += array.shape[0]
        h_table += [
            (len(h_arrays), starts[index] + row, dr, dl ^ bit) for index, row, dr, dl in h_table
        ]
        h_arrays = h_arrays + [lax.ppermute(packed, "layer", flip(layers, bit))]

    n_early = cols - 1
    hm, total = pl.pallas_call(
        functools.partial(first_kernel, sizes, h_table, n_early),
        out_shape=[
            jax.ShapeDtypeStruct((order, cols_here), jnp.bfloat16),
            jax.ShapeDtypeStruct((2 * height, cols_here), jnp.float32),
        ],
        in_specs=[smem, smem] + [vmem] * (2 * n_early + len(h_arrays)),
        out_specs=[vmem, vmem],
        scratch_shapes=[pltpu.VMEM((2 * height, order), jnp.bfloat16)],
        compiler_params=params,
        cost_estimate=pl.CostEstimate(
            flops=0, bytes_accessed=order * cols_here, transcendentals=0
        ),
        name="first_product",
    )(h_pattern, z_pattern, *slots[0][:n_early], *slots[1][:n_early], *h_arrays)
    product = pl.pallas_call(
        functools.partial(finish_kernel, sizes),
        out_shape=jax.ShapeDtypeStruct((2 * height, cols_here), jnp.bfloat16),
        in_specs=[smem] + [vmem] * 4,
        out_specs=vmem,
        compiler_params=params,
        name="finish_product",
    )(z_pattern, hm, total, slots[0][-1], slots[1][-1])

    gathered = {0: product}
    for bit in row_bits:
        for dr, piece in list(gathered.items()):
            gathered[dr ^ bit] = lax.ppermute(piece, "row", flip(rows, bit))
    row_offsets = list(gathered)
    outgoing = pl.pallas_call(
        functools.partial(route_kernel, sizes, row_offsets),
        out_shape=jax.ShapeDtypeStruct((cols, quarter, cols_here), jnp.bfloat16),
        in_specs=[vmem] * rows,
        out_specs=vmem,
        compiler_params=params,
        name="route",
    )(*[gathered[o] for o in row_offsets])
    messages = lax.all_to_all(outgoing, "col", 0, 0, tiled=True)

    held, z_table = [], {}
    for group, gates in (
        (range(1, cols - 1), [[h_arrays[-1]], [outgoing]]),
        (range(cols - 1, cols), [[product], [messages]]),
    ):
        mine = pack([slots[part][s] for s in group for part in range(2)], gates[0])
        arrays, table = [mine], []
        for n, s in enumerate(group):
            for part in range(2):
                table.append((0, (2 * n + part) * height, 0, s, part))
        for step, bit in enumerate(layer_bits):
            packed = pack(arrays, gates[1]) if step else mine
            place, starts = 0, []
            for array in arrays:
                starts.append(place)
                place += array.shape[0]
            table += [
                (len(arrays), starts[index] + row, dl ^ bit, s, part)
                for index, row, dl, s, part in table
            ]
            arrays = arrays + [lax.ppermute(packed, "layer", flip(layers, bit))]
        for index, row, dl, s, part in table:
            z_table[dl, s, part] = (len(held) + index, row)
        held += arrays

    early = [dl for dl in range(layers) if not dl & layer_bits[-1]]
    late = [dl for dl in range(layers) if dl & layer_bits[-1]]
    result = None
    for offsets in (early, late):
        chosen = sorted({z_table[key][0] for key in z_table if key[0] in offsets})
        table = {
            key: (chosen.index(index), row)
            for key, (index, row) in z_table.items()
            if key[0] in offsets
        }
        shape = (len(early) * 2 * height, quarter) if result is None else hamiltonian.shape
        before = [] if result is None else [result]
        result = pl.pallas_call(
            functools.partial(
                second_kernel, sizes, table, offsets, [] if result is None else early
            ),
            out_shape=jax.ShapeDtypeStruct(shape, jnp.bfloat16),
            in_specs=[smem] + [vmem] * (2 + len(before) + len(chosen)),
            out_specs=vmem,
            compiler_params=params,
            name="second_product",
        )(z_pattern, inv_root, messages, *before, *[held[n] for n in chosen])
    return result


def solution(mesh):
    rows, cols, layers = (mesh.shape[a] for a in ("row", "col", "layer"))

    def whole(hamiltonian, inv_root, h_pattern, z_pattern):
        order = hamiltonian.shape[0]
        cols_here = order // cols
        quarter = cols_here // layers
        sizes = Sizes(
            rows, cols, layers, order // rows, cols_here, quarter, cols // rows, quarter // 2
        )
        return jax.shard_map(
            functools.partial(local, sizes),
            mesh=mesh,
            in_specs=(P("row", ("col", "layer")), P("row", "col"), P(), P()),
            out_specs=P("row", ("col", "layer")),
            check_vma=False,
        )(hamiltonian, inv_root, h_pattern, z_pattern)

    return whole
```

```python
import functools
from typing import NamedTuple

import jax
import jax.numpy as jnp
from jax import lax
from jax.experimental import pallas as pl
from jax.experimental.pallas import tpu as pltpu
from jax.sharding import PartitionSpec as P

BS = 256
MARGIN = 4 * 1024 * 1024


class Sizes(NamedTuple):
    rows: int
    cols: int
    layers: int
    rows_here: int
    cols_here: int
    quarter: int
    per: int


def bits_of(size):
    return [1 << b for b in reversed(range(size.bit_length() - 1))]


def flip(size, bit):
    return [(i, i ^ bit) for i in range(size)]


def mod(a, n):
    return lax.rem(a + n, n)


def place():
    return lax.axis_index("row"), lax.axis_index("col"), lax.axis_index("layer")


def run(kernel, name, outs, arrays, smem=(), after=(), scratch=(), flops=0):
    size = sum(a.size * a.dtype.itemsize for a in arrays)
    size += sum(o.size * o.dtype.itemsize for o in outs)
    for kept in scratch:
        size += kept.shape[0] * kept.shape[1] * jnp.dtype(kept.dtype).itemsize
    skip = len(smem) + len(arrays)

    def body(*refs):
        kernel(*refs[:skip], *refs[skip + len(after) :])

    return pl.pallas_call(
        body,
        out_shape=list(outs),
        in_specs=[pl.BlockSpec(memory_space=pltpu.SMEM)] * len(smem)
        + [pl.BlockSpec(memory_space=pltpu.VMEM)] * len(arrays)
        + [pl.BlockSpec(memory_space=pl.ANY)] * len(after),
        out_specs=[pl.BlockSpec(memory_space=pltpu.VMEM)] * len(outs),
        scratch_shapes=list(scratch),
        compiler_params=pltpu.CompilerParams(vmem_limit_bytes=size + MARGIN),
        cost_estimate=pl.CostEstimate(flops=flops, bytes_accessed=size, transcendentals=0),
        name=name,
    )(*smem, *arrays, *after)


def shape(rows, columns, dtype=jnp.bfloat16):
    return jax.ShapeDtypeStruct((rows, columns), dtype)


def keep_block(pattern, i, j, block):
    return jnp.where(pattern[i, j] > 0, block, jnp.zeros_like(block))


def strip_start(l, half, sizes):
    return pl.multiple_of(half * sizes.cols_here + l * sizes.quarter, sizes.quarter)


def columns_of(cc, sizes):
    return pl.ds(pl.multiple_of(cc * sizes.cols_here, sizes.cols_here), sizes.cols_here)


def mask_strip(zp, r, l, half, cc, strip, sizes):
    block_row = (r * sizes.rows_here + half * sizes.cols_here + l * sizes.quarter) // BS
    first = cc * (sizes.cols_here // BS)
    return jnp.concatenate(
        [
            keep_block(zp, block_row, first + t, strip[:, t * BS : (t + 1) * BS])
            for t in range(sizes.cols_here // BS)
        ],
        axis=1,
    )


def mask_piece(zp, r, l, cc, piece, sizes):
    q = sizes.quarter
    return jnp.concatenate(
        [
            mask_strip(zp, r, l, half, cc, piece[half * q : (half + 1) * q, :], sizes)
            for half in range(sizes.per)
        ],
        axis=0,
    )


def pack_kernel(*refs):
    out, row = refs[-1], 0
    for ref in refs[:-1]:
        out[row : row + ref.shape[0], :] = ref[...]
        row += ref.shape[0]


def pack(pieces, after=()):
    height = sum(p.shape[0] for p in pieces)
    out = shape(height, pieces[0].shape[1])
    return run(pack_kernel, "pack", [out], pieces, after=after)[0]


def pick_kernel(choose, *refs):
    for condition, ref in zip(choose(lax.axis_index("col")), refs[:-1]):

        @pl.when(condition)
        def _(ref=ref):
            refs[-1][...] = ref[...]


def pick(choose, pieces, after=()):
    return run(
        functools.partial(pick_kernel, choose), "pick", [shape(*pieces[0].shape)], pieces,
        after=after,
    )[0]


def first_kernel(sizes, h_table, n_h, hp, zp, own, *refs):
    cols, q = sizes.cols, sizes.quarter
    n = cols - 2
    rights, lefts, h_refs = refs[:n], refs[n : 2 * n], refs[2 * n : 2 * n + n_h]
    hm, total, *strips, zm = refs[2 * n + n_h :]
    r, c, l = place()
    zm[...] = jnp.zeros_like(zm)
    zm[:, columns_of(c, sizes)] = mask_piece(zp, r, l, c, own[...], sizes)
    for s in range(1, n + 1):

        @pl.when(c >= s)
        def _(s=s):
            zm[:, columns_of(c - s, sizes)] = mask_piece(
                zp, r, l, c - s, rights[s - 1][...], sizes
            )

        @pl.when(c + s < cols)
        def _(s=s):
            zm[:, columns_of(c + s, sizes)] = mask_piece(
                zp, r, l, c + s, lefts[s - 1][...], sizes
            )

    per_rows = sizes.rows_here // BS
    for index, row, dr, dl in h_table:
        rr, ll = r ^ dr, l ^ dl
        block_col = (c * sizes.cols_here + ll * q) // BS
        for t in range(per_rows):
            j = rr * per_rows + t
            hm[pl.ds(pl.multiple_of(j * BS, BS), BS), pl.ds(pl.multiple_of(ll * q, q), q)] = (
                keep_block(hp, j, block_col, h_refs[index][row + t * BS : row + (t + 1) * BS, :])
            )
    order = zm.shape[1]
    chunk = min(order, 2048)
    acc = None
    for k in range(0, order, chunk):
        part = jnp.dot(
            zm[:, k : k + chunk], hm[k : k + chunk, :], preferred_element_type=jnp.float32
        )
        acc = part if acc is None else acc + part
    total[...] = acc
    for half, strip in enumerate(strips):
        strip[...] = acc[half * q : (half + 1) * q, :].astype(strip.dtype)


def finish_kernel(sizes, zp, hm, total, last, *strips):
    q = sizes.quarter
    r, c, l = place()
    cc = jnp.where(c == 0, sizes.cols - 1, 0)
    acc = total[...] + jnp.dot(
        mask_piece(zp, r, l, cc, last[...], sizes),
        hm[columns_of(cc, sizes), :],
        preferred_element_type=jnp.float32,
    )
    for half, strip in enumerate(strips):
        strip[...] = acc[half * q : (half + 1) * q, :].astype(strip.dtype)


def layers_kernel(sizes, z_table, zp, z_tile, *refs):
    cols, q = sizes.cols, sizes.quarter
    held, out = refs[:-1], refs[-1]
    r, c, l = place()
    sign = jnp.where(c < cols // 2, 1, -1)
    for dl in range(sizes.layers):
        ll = l ^ dl
        for half in range(sizes.per):
            rows = pl.ds(strip_start(ll, half, sizes), q)
            for s in range(cols - 1):
                cc = mod(c + sign * s, cols)
                if s == 0:
                    strip = z_tile[rows, :]
                else:
                    index, row = z_table[dl, s]
                    strip = held[index][row + half * q : row + (half + 1) * q, :]
                out[rows, columns_of(cc, sizes)] = mask_strip(zp, r, ll, half, cc, strip, sizes)
            cc = mod(c + sign * (cols - 1), cols)
            out[rows, columns_of(cc, sizes)] = jnp.zeros((q, sizes.cols_here), out.dtype)


def second_kernel(sizes, *refs):
    per, width = sizes.per, sizes.cols_here
    outside, inside, z_full, xm, total = refs
    r, c, l = place()
    first, second = (
        pl.ds(pl.multiple_of(mod(group - lax.rem(r, per), per) * width, width), width)
        for group in range(2)
    )
    xm[:, first] = outside[...]
    xm[:, second] = inside[...]
    total[...] = jnp.dot(xm[...], z_full[...], preferred_element_type=jnp.float32)


def rest_kernel(sizes, z_table, zp, xm, total, *refs):
    cols, q, wide = sizes.cols, sizes.quarter, sizes.rows_here
    *held, keep = refs[: -1 - sizes.rows]
    *sends, z_last, rest = refs[-1 - sizes.rows :]
    r, c, l = place()
    cc = mod(c + jnp.where(c < cols // 2, 1, -1) * (cols - 1), cols)
    for dl in range(sizes.layers):
        index, row = z_table[dl, cols - 1]
        for half in range(sizes.per):
            strip = held[index][row + half * q : row + (half + 1) * q, :]
            z_last[pl.ds(strip_start(l ^ dl, half, sizes), q), :] = mask_strip(
                zp, r, l ^ dl, half, cc, strip, sizes
            )
    rest[...] = total[...]
    rest[:, columns_of(cc, sizes)] = jnp.dot(
        xm[...], z_last[...], preferred_element_type=jnp.float32
    )
    for dr, out in enumerate([keep, *sends]):
        start = pl.multiple_of((r ^ dr) * wide, wide)
        out[...] = rest[:, pl.ds(start, wide)].astype(out.dtype)


def sum_kernel(*refs):
    keep, received, out = refs[0], refs[1:-1], refs[-1]
    total = keep[...]
    for part in received:
        total = total + part[...].astype(jnp.float32)
    out[...] = total.T.astype(out.dtype)


def local(sizes, hamiltonian, inv_root, h_pattern, z_pattern):
    rows, cols, layers, per = sizes.rows, sizes.cols, sizes.layers, sizes.per
    q, cols_here, rows_here = sizes.quarter, sizes.cols_here, sizes.rows_here
    order = rows * rows_here
    height = per * q
    row_bits, layer_bits = bits_of(rows), bits_of(layers)
    f32 = jnp.float32

    striped = inv_root.reshape(per, layers, q, cols_here)
    l = lax.axis_index("layer")
    own = lax.dynamic_index_in_dim(striped, l, 1, keepdims=False).reshape(height, cols_here)
    rights, lefts = [own], [own]
    for s in range(1, cols - 1):
        to_right = [(i, i + 1) for i in range(s - 1, cols - 1)]
        to_left = [(i, i - 1) for i in range(1, cols - s + 1)]
        rights.append(lax.ppermute(rights[-1], "col", to_right))
        lefts.append(lax.ppermute(lefts[-1], "col", to_left))
    inner = pick(
        lambda c: [c >= cols // 2, c < cols // 2], [rights[-1], lefts[-1]]
    )
    last = lax.ppermute(inner, "col", [(cols - 2, cols - 1), (1, 0)])

    def slot(s, after):
        if s <= cols // 2:
            pieces = [lefts[s], rights[s]]
            return pick(lambda c: [c < cols // 2, c >= cols // 2], pieces, after)
        left = lefts[s] if s < cols - 1 else last
        right = rights[s] if s < cols - 1 else last
        return pick(
            lambda c: [
                (c < cols // 2) & (c + s < cols),
                (c < cols // 2) & (c + s >= cols),
                (c >= cols // 2) & (c >= s),
                (c >= cols // 2) & (c < s),
            ],
            [left, rights[cols - s], right, lefts[cols - s]],
            after,
        )

    def cross(s, after=()):
        mine = slot(s, after)
        return [mine, lax.ppermute(mine, "layer", flip(layers, layer_bits[0]))]

    def share(slots, crossed, gate):
        arrays, table = [], []
        for s, pair in zip(slots, crossed):
            table += [(len(arrays), 0, 0, s), (len(arrays) + 1, 0, layer_bits[0], s)]
            arrays += pair
        for bit in layer_bits[1:]:
            packed = pack(arrays, gate)
            starts = [0]
            for array in arrays:
                starts.append(starts[-1] + array.shape[0])
            table += [
                (len(arrays), starts[index] + row, dl ^ bit, s) for index, row, dl, s in table
            ]
            arrays = arrays + [lax.ppermute(packed, "layer", flip(layers, bit))]
        return arrays, {(dl, s): (index, row) for index, row, dl, s in table}

    crossed = [cross(s) for s in range(1, cols - 1)]

    h_arrays, h_table = [hamiltonian], [(0, 0, 0, 0)]
    for axis, bit in [("layer", layer_bits[0])] + [("row", b) for b in row_bits]:
        for index, _, dr, dl in list(h_table):
            there = (dr ^ bit, dl) if axis == "row" else (dr, dl ^ bit)
            source = h_arrays[index]
            if index:
                source = pack([source], [rights[1], lefts[1]])
            h_table.append((len(h_arrays), 0) + there)
            h_arrays.append(
                lax.ppermute(source, axis, flip(rows if axis == "row" else layers, bit))
            )
    for bit in layer_bits[1:]:
        packed = pack(h_arrays, [rights[-1], lefts[-1], crossed[0][1]])
        starts = [0]
        for array in h_arrays:
            starts.append(starts[-1] + array.shape[0])
        h_table += [
            (len(h_arrays), starts[index] + row, dr, dl ^ bit) for index, row, dr, dl in h_table
        ]
        h_arrays = h_arrays + [lax.ppermute(packed, "layer", flip(layers, bit))]

    strip = shape(q, cols_here)
    hm, total, *early = run(
        functools.partial(first_kernel, sizes, h_table, len(h_arrays)),
        "first_product",
        [shape(order, cols_here), shape(height, cols_here, f32)] + [strip] * per,
        [own, *rights[1:], *lefts[1:], *h_arrays],
        smem=[h_pattern, z_pattern],
        scratch=[pltpu.VMEM((height, order), jnp.bfloat16)],
    )
    late = run(
        functools.partial(finish_kernel, sizes),
        "finish_product",
        [strip] * per,
        [hm, total, last],
        smem=[z_pattern],
        after=[crossed[-1][1]],
    )

    messages = []
    for group, strips in ((1, early), (0, late)):
        part = []
        for half in range(per):
            perm = []
            for r in range(rows):
                for c in range(cols):
                    if (c // per + c) % per != group:
                        continue
                    for k in range(layers):
                        perm.append(
                            (
                                (r * cols + c) * layers + k,
                                ((c // per) * cols + r * per + half) * layers + k,
                            )
                        )
            part.append(lax.ppermute(strips[half], ("row", "col", "layer"), perm))
        messages = part + messages

    from_inside = pick(lambda c: [c % per == half for half in range(per)], messages[per:], late[:1])
    held, z_table = share(range(1, cols - 1), crossed, [from_inside])
    z_full = run(
        functools.partial(layers_kernel, sizes, z_table),
        "layers",
        [shape(rows_here, order)],
        [inv_root, *held],
        smem=[z_pattern],
    )[0]
    from_outside = pick(
        lambda c: [c % per == half for half in range(per)], messages[:per], [z_full]
    )
    xm, total = run(
        functools.partial(second_kernel, sizes),
        "second_product",
        [shape(q, rows_here), shape(q, order, f32)],
        [from_outside, from_inside, z_full],
    )
    held, z_table = share([cols - 1], [cross(cols - 1, late[:1])], [xm])
    keep, *sends = run(
        functools.partial(rest_kernel, sizes, z_table),
        "rest_product",
        [shape(q, rows_here, f32)] + [shape(q, rows_here)] * (rows - 1),
        [xm, total, *held],
        smem=[z_pattern],
        scratch=[pltpu.VMEM((rows_here, cols_here), jnp.bfloat16), pltpu.VMEM((q, order), f32)],
    )
    received = [lax.ppermute(sends[d - 1], "row", flip(rows, d)) for d in range(1, rows)]
    return run(sum_kernel, "sum", [shape(*hamiltonian.shape)], [keep, *received])[0]


def solution(mesh):
    rows, cols, layers = (mesh.shape[a] for a in ("row", "col", "layer"))

    def whole(hamiltonian, inv_root, h_pattern, z_pattern):
        order = hamiltonian.shape[0]
        cols_here = order // cols
        sizes = Sizes(
            rows, cols, layers, order // rows, cols_here, cols_here // layers, cols // rows
        )
        return jax.shard_map(
            functools.partial(local, sizes),
            mesh=mesh,
            in_specs=(P("row", ("col", "layer")), P("row", "col"), P(), P()),
            out_specs=P("row", ("col", "layer")),
            check_vma=False,
        )(hamiltonian, inv_root, h_pattern, z_pattern)

    return whole
```

```python
import functools
from typing import NamedTuple

import jax
import jax.numpy as jnp
from jax import lax
from jax.experimental import pallas as pl
from jax.experimental.pallas import tpu as pltpu
from jax.sharding import PartitionSpec as P

BS = 256
MARGIN = 4 * 1024 * 1024


class Sizes(NamedTuple):
    rows: int
    cols: int
    layers: int
    rows_here: int
    cols_here: int
    quarter: int
    per: int


def bits_of(size):
    return [1 << b for b in reversed(range(size.bit_length() - 1))]


def flip(size, bit):
    return [(i, i ^ bit) for i in range(size)]


def mod(a, n):
    return lax.rem(a + n, n)


def place():
    return lax.axis_index("row"), lax.axis_index("col"), lax.axis_index("layer")


def run(kernel, name, outs, arrays, smem=(), after=(), scratch=(), flops=0):
    size = sum(a.size * a.dtype.itemsize for a in arrays)
    size += sum(o.size * o.dtype.itemsize for o in outs)
    for kept in scratch:
        size += kept.shape[0] * kept.shape[1] * jnp.dtype(kept.dtype).itemsize
    skip = len(smem) + len(arrays)

    def body(*refs):
        kernel(*refs[:skip], *refs[skip + len(after) :])

    return pl.pallas_call(
        body,
        out_shape=list(outs),
        in_specs=[pl.BlockSpec(memory_space=pltpu.SMEM)] * len(smem)
        + [pl.BlockSpec(memory_space=pltpu.VMEM)] * len(arrays)
        + [pl.BlockSpec(memory_space=pl.ANY)] * len(after),
        out_specs=[pl.BlockSpec(memory_space=pltpu.VMEM)] * len(outs),
        scratch_shapes=list(scratch),
        compiler_params=pltpu.CompilerParams(vmem_limit_bytes=size + MARGIN),
        cost_estimate=pl.CostEstimate(flops=flops, bytes_accessed=size, transcendentals=0),
        name=name,
    )(*smem, *arrays, *after)


def shape(rows, columns, dtype=jnp.bfloat16):
    return jax.ShapeDtypeStruct((rows, columns), dtype)


def keep_block(pattern, i, j, block):
    return jnp.where(pattern[i, j] > 0, block, jnp.zeros_like(block))


def strip_start(l, half, sizes):
    return pl.multiple_of(half * sizes.cols_here + l * sizes.quarter, sizes.quarter)


def columns_of(cc, sizes):
    return pl.ds(pl.multiple_of(cc * sizes.cols_here, sizes.cols_here), sizes.cols_here)


def mask_strip(zp, r, l, half, cc, strip, sizes):
    block_row = (r * sizes.rows_here + half * sizes.cols_here + l * sizes.quarter) // BS
    first = cc * (sizes.cols_here // BS)
    return jnp.concatenate(
        [
            keep_block(zp, block_row, first + t, strip[:, t * BS : (t + 1) * BS])
            for t in range(sizes.cols_here // BS)
        ],
        axis=1,
    )


def mask_piece(zp, r, l, cc, piece, sizes):
    q = sizes.quarter
    return jnp.concatenate(
        [
            mask_strip(zp, r, l, half, cc, piece[half * q : (half + 1) * q, :], sizes)
            for half in range(sizes.per)
        ],
        axis=0,
    )


def pack_kernel(*refs):
    out, row = refs[-1], 0
    for ref in refs[:-1]:
        out[row : row + ref.shape[0], :] = ref[...]
        row += ref.shape[0]


def pack(pieces, after=()):
    height = sum(p.shape[0] for p in pieces)
    out = shape(height, pieces[0].shape[1])
    return run(pack_kernel, "pack", [out], pieces, after=after)[0]


def ring_place(c, cols):
    return jnp.where(c % 2 == 0, c // 2, cols - 1 - c // 2)


def ring_column(p, cols):
    return jnp.where(p < cols // 2, 2 * p, 2 * (cols - 1 - p) + 1)


def slot_column(c, s, cols):
    return ring_column(mod(ring_place(c, cols) - s, cols), cols)


def first_kernel(sizes, h_table, n_h, hp, zp, *refs):
    cols, q = sizes.cols, sizes.quarter
    slots, h_refs = refs[: cols - 1], refs[cols - 1 : cols - 1 + n_h]
    hm, total, zm = refs[cols - 1 + n_h :]
    r, c, l = place()
    for s in range(cols - 1):
        cc = slot_column(c, s, cols)
        zm[:, columns_of(cc, sizes)] = mask_piece(zp, r, l, cc, slots[s][...], sizes)
    zm[:, columns_of(slot_column(c, cols - 1, cols), sizes)] = jnp.zeros(
        (zm.shape[0], sizes.cols_here), zm.dtype
    )
    per_rows = sizes.rows_here // BS
    for index, row, dr, dl in h_table:
        rr, ll = r ^ dr, l ^ dl
        block_col = (c * sizes.cols_here + ll * q) // BS
        for t in range(per_rows):
            j = rr * per_rows + t
            hm[pl.ds(pl.multiple_of(j * BS, BS), BS), pl.ds(pl.multiple_of(ll * q, q), q)] = (
                keep_block(hp, j, block_col, h_refs[index][row + t * BS : row + (t + 1) * BS, :])
            )
    order = zm.shape[1]
    chunk = min(order, 2048)
    acc = None
    for k in range(0, order, chunk):
        part = jnp.dot(
            zm[:, k : k + chunk], hm[k : k + chunk, :], preferred_element_type=jnp.float32
        )
        acc = part if acc is None else acc + part
    total[...] = acc


def finish_kernel(sizes, zp, hm, total, last, out):
    r, c, l = place()
    cc = slot_column(c, sizes.cols - 1, sizes.cols)
    out[...] = (
        total[...]
        + jnp.dot(
            mask_piece(zp, r, l, cc, last[...], sizes),
            hm[columns_of(cc, sizes), :],
            preferred_element_type=jnp.float32,
        )
    ).astype(out.dtype)


def route_kernel(sizes, row_offsets, *refs):
    n = len(row_offsets)
    pieces, outs, table = refs[:n], refs[n:-1], refs[-1]
    r, c, _ = place()
    q = sizes.quarter
    for dr, piece in zip(row_offsets, pieces):
        for half in range(sizes.per):
            start = pl.multiple_of(((r ^ dr) * sizes.per + half) * q, q)
            table[pl.ds(start, q), :] = piece[half * q : (half + 1) * q, :]
    for d, out in enumerate(outs):
        out[...] = table[pl.ds(pl.multiple_of((c ^ d) * q, q), q), :]


def layers_kernel(sizes, z_table, slots, zp, *refs):
    cols, q = sizes.cols, sizes.quarter
    out, held = refs[-1], refs[:-1]
    r, c, l = place()
    for dl in range(sizes.layers):
        ll = l ^ dl
        for half in range(sizes.per):
            rows = pl.ds(strip_start(ll, half, sizes), q)
            for s in slots:
                cc = slot_column(c, s, cols)
                if s == 0:
                    strip = held[0][rows, :]
                else:
                    index, row = z_table[dl, s]
                    strip = held[index][row + half * q : row + (half + 1) * q, :]
                columns = columns_of(cc, sizes) if len(slots) > 1 else slice(None)
                out[rows, columns] = mask_strip(zp, r, ll, half, cc, strip, sizes)


def second_kernel(sizes, z_early, z_late, *refs):
    cols, width = sizes.cols, sizes.cols_here
    messages, out, xm = refs[:cols], refs[cols], refs[cols + 1]
    r, c, l = place()
    for d in range(cols):
        xm[:, columns_of(c ^ d, sizes)] = messages[d][...]
    cc = slot_column(c, cols - 1, cols)
    turned = (((1,), (1,)), ((), ()))
    total = lax.dot_general(
        z_late[...], xm[:, columns_of(cc, sizes)], turned, preferred_element_type=jnp.float32
    )
    for s in range(cols - 1):
        columns = columns_of(slot_column(c, s, cols), sizes)
        total += lax.dot_general(
            z_early[:, columns], xm[:, columns], turned, preferred_element_type=jnp.float32
        )
    out[...] = total.astype(out.dtype)


def local(sizes, hamiltonian, inv_root, h_pattern, z_pattern):
    rows, cols, layers, per = sizes.rows, sizes.cols, sizes.layers, sizes.per
    q, cols_here, rows_here = sizes.quarter, sizes.cols_here, sizes.rows_here
    order = rows * rows_here
    height = per * q
    row_bits, layer_bits = bits_of(rows), bits_of(layers)
    f32 = jnp.float32

    striped = inv_root.reshape(per, layers, q, cols_here)
    l = lax.axis_index("layer")
    own = lax.dynamic_index_in_dim(striped, l, 1, keepdims=False).reshape(height, cols_here)
    trip = list(range(0, cols, 2)) + list(range(cols - 1, 0, -2))
    ring = [(trip[i], trip[(i + 1) % cols]) for i in range(cols)]
    slots = [own]
    for _ in range(1, cols):
        slots.append(lax.ppermute(slots[-1], "col", ring))

    def offsets(arrays):
        starts = [0]
        for array in arrays:
            starts.append(starts[-1] + array.shape[0])
        return starts

    crossed = [lax.ppermute(slots[s], "layer", flip(layers, layer_bits[0])) for s in range(1, cols)]

    h_arrays, h_table = [hamiltonian], [(0, 0, 0, 0)]
    for axis, bit in [("layer", layer_bits[0])] + [("row", b) for b in row_bits]:
        for index, _, dr, dl in list(h_table):
            there = (dr ^ bit, dl) if axis == "row" else (dr, dl ^ bit)
            source = h_arrays[index]
            if index:
                source = pack([source], [slots[1]])
            h_table.append((len(h_arrays), 0) + there)
            h_arrays.append(
                lax.ppermute(source, axis, flip(rows if axis == "row" else layers, bit))
            )
    for bit in layer_bits[1:]:
        packed, starts = pack(h_arrays, [slots[-2], crossed[0]]), offsets(h_arrays)
        h_table += [
            (len(h_arrays), starts[index] + row, dr, dl ^ bit) for index, row, dr, dl in h_table
        ]
        h_arrays = h_arrays + [lax.ppermute(packed, "layer", flip(layers, bit))]

    hm, total = run(
        functools.partial(first_kernel, sizes, h_table, len(h_arrays)),
        "first_product",
        [shape(order, cols_here), shape(height, cols_here, f32)],
        [*slots[:-1], *h_arrays],
        smem=[h_pattern, z_pattern],
        scratch=[pltpu.VMEM((height, order), jnp.bfloat16)],
    )
    product = run(
        functools.partial(finish_kernel, sizes),
        "finish_product",
        [shape(height, cols_here)],
        [hm, total, slots[-1]],
        smem=[z_pattern],
    )[0]

    gathered = {0: product}
    for bit in row_bits:
        for dr, piece in list(gathered.items()):
            gathered[dr ^ bit] = lax.ppermute(piece, "row", flip(rows, bit))
    row_offsets = list(gathered)
    outgoing = run(
        functools.partial(route_kernel, sizes, row_offsets),
        "route",
        [shape(q, cols_here)] * cols,
        [gathered[o] for o in row_offsets],
        after=[crossed[-1]],
        scratch=[pltpu.VMEM((cols * q, cols_here), jnp.bfloat16)],
    )
    messages = [outgoing[0]] + [
        lax.ppermute(outgoing[d], "col", flip(cols, d)) for d in range(1, cols)
    ]

    def share(group, gate):
        arrays, table = [], []
        for s in group:
            table += [(len(arrays), 0, 0, s), (len(arrays) + 1, 0, layer_bits[0], s)]
            arrays += [slots[s], crossed[s - 1]]
        for bit in layer_bits[1:]:
            packed, starts = pack(arrays, gate), offsets(arrays)
            table += [
                (len(arrays), starts[index] + row, dl ^ bit, s) for index, row, dl, s in table
            ]
            arrays = arrays + [lax.ppermute(packed, "layer", flip(layers, bit))]
        return arrays, table

    def lay_out(group, tile, gate):
        arrays, table = share([s for s in group if s], gate)
        place_of = {(dl, s): (index + len(tile), row) for index, row, dl, s in table}
        return run(
            functools.partial(layers_kernel, sizes, place_of, group),
            "layers",
            [shape(rows_here, order if len(group) > 1 else cols_here)],
            [*tile, *arrays],
            smem=[z_pattern],
        )[0]

    z_early = lay_out(list(range(cols - 1)), [inv_root], [product])
    z_late = lay_out([cols - 1], [], [outgoing[0]])
    return run(
        functools.partial(second_kernel, sizes),
        "second_product",
        [shape(*hamiltonian.shape)],
        [z_early, z_late, *messages],
        scratch=[pltpu.VMEM((q, order), jnp.bfloat16)],
    )[0]


def solution(mesh):
    rows, cols, layers = (mesh.shape[a] for a in ("row", "col", "layer"))

    def whole(hamiltonian, inv_root, h_pattern, z_pattern):
        order = hamiltonian.shape[0]
        cols_here = order // cols
        sizes = Sizes(
            rows, cols, layers, order // rows, cols_here, cols_here // layers, cols // rows
        )
        return jax.shard_map(
            functools.partial(local, sizes),
            mesh=mesh,
            in_specs=(P("row", ("col", "layer")), P("row", "col"), P(), P()),
            out_specs=P("row", ("col", "layer")),
            check_vma=False,
        )(hamiltonian, inv_root, h_pattern, z_pattern)

    return whole
```

```python
import functools
from typing import NamedTuple

import jax
import jax.numpy as jnp
from jax import lax
from jax.experimental import pallas as pl
from jax.experimental.pallas import tpu as pltpu
from jax.sharding import PartitionSpec as P

BS = 256
MARGIN = 4 * 1024 * 1024


class Sizes(NamedTuple):
    rows: int
    cols: int
    layers: int
    rows_here: int
    cols_here: int
    quarter: int
    per: int


def bits_of(size):
    return [1 << b for b in reversed(range(size.bit_length() - 1))]


def flip(size, bit):
    return [(i, i ^ bit) for i in range(size)]


def mod(a, n):
    return lax.rem(a + n, n)


def place():
    return lax.axis_index("row"), lax.axis_index("col"), lax.axis_index("layer")


def run(kernel, name, outs, arrays, smem=(), after=(), scratch=(), flops=0):
    size = sum(a.size * a.dtype.itemsize for a in arrays)
    size += sum(o.size * o.dtype.itemsize for o in outs)
    for kept in scratch:
        size += kept.shape[0] * kept.shape[1] * jnp.dtype(kept.dtype).itemsize
    skip = len(smem) + len(arrays)

    def body(*refs):
        kernel(*refs[:skip], *refs[skip + len(after) :])

    return pl.pallas_call(
        body,
        out_shape=list(outs),
        in_specs=[pl.BlockSpec(memory_space=pltpu.SMEM)] * len(smem)
        + [pl.BlockSpec(memory_space=pltpu.VMEM)] * len(arrays)
        + [pl.BlockSpec(memory_space=pl.ANY)] * len(after),
        out_specs=[pl.BlockSpec(memory_space=pltpu.VMEM)] * len(outs),
        scratch_shapes=list(scratch),
        compiler_params=pltpu.CompilerParams(vmem_limit_bytes=size + MARGIN),
        cost_estimate=pl.CostEstimate(flops=flops, bytes_accessed=size, transcendentals=0),
        name=name,
    )(*smem, *arrays, *after)


def shape(rows, columns, dtype=jnp.bfloat16):
    return jax.ShapeDtypeStruct((rows, columns), dtype)


def keep_block(pattern, i, j, block):
    return jnp.where(pattern[i, j] > 0, block, jnp.zeros_like(block))


def strip_start(l, half, sizes):
    return pl.multiple_of(half * sizes.cols_here + l * sizes.quarter, sizes.quarter)


def columns_of(cc, sizes):
    return pl.ds(pl.multiple_of(cc * sizes.cols_here, sizes.cols_here), sizes.cols_here)


def mask_strip(zp, r, l, half, cc, strip, sizes):
    block_row = (r * sizes.rows_here + half * sizes.cols_here + l * sizes.quarter) // BS
    first = cc * (sizes.cols_here // BS)
    return jnp.concatenate(
        [
            keep_block(zp, block_row, first + t, strip[:, t * BS : (t + 1) * BS])
            for t in range(sizes.cols_here // BS)
        ],
        axis=1,
    )


def mask_piece(zp, r, l, cc, piece, sizes):
    q = sizes.quarter
    return jnp.concatenate(
        [
            mask_strip(zp, r, l, half, cc, piece[half * q : (half + 1) * q, :], sizes)
            for half in range(sizes.per)
        ],
        axis=0,
    )


def pack_kernel(*refs):
    out, row = refs[-1], 0
    for ref in refs[:-1]:
        out[row : row + ref.shape[0], :] = ref[...]
        row += ref.shape[0]


def pack(pieces, after=()):
    height = sum(p.shape[0] for p in pieces)
    out = shape(height, pieces[0].shape[1])
    return run(pack_kernel, "pack", [out], pieces, after=after)[0]


def ring_place(c, cols):
    return jnp.where(c % 2 == 0, c // 2, cols - 1 - c // 2)


def ring_column(p, cols):
    return jnp.where(p < cols // 2, 2 * p, 2 * (cols - 1 - p) + 1)


def slot_column(c, s, cols):
    return ring_column(mod(ring_place(c, cols) - s, cols), cols)


def mask_kernel(sizes, numbers, zp, *refs):
    slots, before, out = refs[: len(numbers)], refs[len(numbers) : -1], refs[-1]
    r, c, l = place()
    if before:
        out[...] = before[0][...]
    for s, slot in zip(numbers, slots):
        cc = slot_column(c, s, sizes.cols)
        out[:, columns_of(cc, sizes)] = mask_piece(zp, r, l, cc, slot[...], sizes)


def first_kernel(sizes, top, zm, h_own, h_other, out):
    q, (_, _, l) = sizes.quarter, place()
    for side, h in ((l, h_own), (l ^ 1, h_other)):
        part = jnp.dot(zm[...], h[...], preferred_element_type=jnp.float32).astype(out.dtype)
        for n, ll in enumerate((side, side ^ top)):
            out[:, pl.ds(pl.multiple_of(ll * q, q), q)] = part[:, n * q : (n + 1) * q]


def bring_kernel(sizes, h_table, hp, *refs):
    *pieces, piece, hm, piece_out = refs
    r, c, l = place()
    q, per_rows = sizes.quarter, sizes.rows_here // BS
    for h, (dr, dl) in zip(pieces, h_table):
        n = 1 if dl else 0
        block_col = (c * sizes.cols_here + (l ^ dl) * q) // BS
        for t in range(per_rows):
            j = (r ^ dr) * per_rows + t
            hm[pl.ds(pl.multiple_of(j * BS, BS), BS), n * q : (n + 1) * q] = keep_block(
                hp, j, block_col, h[t * BS : (t + 1) * BS, :]
            )
    piece_out[...] = piece[...]


def route_kernel(sizes, row_offsets, *refs):
    table, (r, _, _), q = refs[-1], place(), sizes.quarter
    for dr, piece in zip(row_offsets, refs[:-1]):
        for half in range(sizes.per):
            start = pl.multiple_of(((r ^ dr) * sizes.per + half) * q, q)
            table[pl.ds(start, q), :] = piece[half * q : (half + 1) * q, :]


def cut_kernel(sizes, table, *outs):
    c, q = lax.axis_index("col"), sizes.quarter
    for d, out in enumerate(outs):
        out[...] = table[pl.ds(pl.multiple_of((c ^ d) * q, q), q), :]


def layers_kernel(sizes, z_table, zp, *refs):
    cols, q = sizes.cols, sizes.quarter
    out, held = refs[-1], refs[:-1]
    r, c, l = place()
    for dl in range(sizes.layers):
        ll = l ^ dl
        for half in range(sizes.per):
            rows = pl.ds(strip_start(ll, half, sizes), q)
            for s in range(cols):
                cc = slot_column(c, s, cols)
                if s == 0:
                    strip = held[0][rows, :]
                else:
                    index, row = z_table[dl, s]
                    strip = held[index][row + half * q : row + (half + 1) * q, :]
                out[rows, columns_of(cc, sizes)] = mask_strip(zp, r, ll, half, cc, strip, sizes)


def second_kernel(sizes, part, z_full, *refs):
    messages, before, out = refs[: len(part)], refs[len(part) : -1], refs[-1]
    c = lax.axis_index("col")
    total = before[0][...] if before else None
    for d, message in zip(part, messages):
        added = lax.dot_general(
            z_full[:, columns_of(c ^ d, sizes)],
            message[...],
            (((1,), (1,)), ((), ())),
            preferred_element_type=jnp.float32,
        )
        total = added if total is None else total + added
    out[...] = total.astype(out.dtype)


def local(sizes, hamiltonian, inv_root, h_pattern, z_pattern):
    rows, cols, layers, per = sizes.rows, sizes.cols, sizes.layers, sizes.per
    q, cols_here, rows_here = sizes.quarter, sizes.cols_here, sizes.rows_here
    order = rows * rows_here
    height = per * q
    row_bits, layer_bits = bits_of(rows), bits_of(layers)
    f32 = jnp.float32

    striped = inv_root.reshape(per, layers, q, cols_here)
    l = lax.axis_index("layer")
    own = lax.dynamic_index_in_dim(striped, l, 1, keepdims=False).reshape(height, cols_here)
    trip = list(range(0, cols, 2)) + list(range(cols - 1, 0, -2))
    ring = [(trip[i], trip[(i + 1) % cols]) for i in range(cols)]
    slots = [own]
    for _ in range(1, cols):
        slots.append(lax.ppermute(slots[-1], "col", ring))

    def offsets(arrays):
        starts = [0]
        for array in arrays:
            starts.append(starts[-1] + array.shape[0])
        return starts

    top, low = layer_bits
    h_pieces, h_table = [hamiltonian], [(0, 0)]
    for dr in range(rows):
        for dl in (0, top):
            if dr or dl:
                perm = [
                    (r * layers + k, (r ^ dr) * layers + (k ^ dl))
                    for r in range(rows)
                    for k in range(layers)
                ]
                h_pieces.append(lax.ppermute(hamiltonian, ("row", "layer"), perm))
                h_table.append((dr, dl))
    h_own, first_slot = run(
        functools.partial(bring_kernel, sizes, h_table),
        "bring",
        [shape(order, 2 * q), shape(height, cols_here)],
        [*h_pieces, slots[1]],
        smem=[h_pattern],
    )

    def cross(piece):
        return lax.ppermute(piece, "layer", flip(layers, top))

    crossed = [cross(first_slot)] + [cross(slots[s]) for s in range(2, cols - 1)]
    h_sent = pack([h_own], [slots[-2]])
    h_other = lax.ppermute(h_sent, "layer", flip(layers, low))

    zm = []
    for numbers, after in ((range(cols - 1), [crossed[0]]), ([cols - 1], [])):
        zm = run(
            functools.partial(mask_kernel, sizes, numbers),
            "mask",
            [shape(height, order)],
            [*(slots[s] for s in numbers), *zm],
            smem=[z_pattern],
            after=after,
            flops=0 if after else 0,
        )
    product = run(
        functools.partial(first_kernel, sizes, top),
        "first_product",
        [shape(height, cols_here)],
        [*zm, h_sent, h_other],
    )[0]

    gathered = {0: product}
    for bit in row_bits:
        for dr, piece in list(gathered.items()):
            gathered[dr ^ bit] = lax.ppermute(piece, "row", flip(rows, bit))
    row_offsets = list(gathered)
    crossed.append(cross(pack([slots[-1]], [product])))
    table = run(
        functools.partial(route_kernel, sizes, row_offsets),
        "route",
        [shape(cols * q, cols_here)],
        [gathered[o] for o in row_offsets],
    )[0]
    outgoing = run(
        functools.partial(cut_kernel, sizes),
        "cut",
        [shape(q, cols_here)] * cols,
        [table],
        after=[crossed[-1]],
    )
    messages = [outgoing[0]] + [
        lax.ppermute(outgoing[d], "col", flip(cols, d)) for d in range(1, cols)
    ]

    def share(group, gate):
        arrays, table = [], []
        for s in group:
            table += [(len(arrays), 0, 0, s), (len(arrays) + 1, 0, layer_bits[0], s)]
            arrays += [slots[s], crossed[s - 1]]
        for bit in layer_bits[1:]:
            packed, starts = pack(arrays, gate), offsets(arrays)
            table += [
                (len(arrays), starts[index] + row, dl ^ bit, s) for index, row, dl, s in table
            ]
            arrays = arrays + [lax.ppermute(packed, "layer", flip(layers, bit))]
        return arrays, table

    held, z_table = [inv_root], {}
    for group, gate in ((range(1, cols - 1), [product]), ([cols - 1], [outgoing[0]])):
        arrays, entries = share(group, gate)
        for index, row, dl, s in entries:
            z_table[dl, s] = (index + len(held), row)
        held += arrays
    z_full = run(
        functools.partial(layers_kernel, sizes, z_table),
        "layers",
        [shape(rows_here, order)],
        held,
        smem=[z_pattern],
    )[0]
    total = []
    for part in (range(cols // 2), range(cols // 2, cols)):
        last_part = part[-1] == cols - 1
        total = run(
            functools.partial(second_kernel, sizes, part),
            "second_product",
            [shape(*hamiltonian.shape, jnp.bfloat16 if last_part else f32)],
            [z_full, *[messages[d] for d in part], *total],
        )
    return total[0]


def solution(mesh):
    rows, cols, layers = (mesh.shape[a] for a in ("row", "col", "layer"))

    def whole(hamiltonian, inv_root, h_pattern, z_pattern):
        order = hamiltonian.shape[0]
        cols_here = order // cols
        sizes = Sizes(
            rows, cols, layers, order // rows, cols_here, cols_here // layers, cols // rows
        )
        return jax.shard_map(
            functools.partial(local, sizes),
            mesh=mesh,
            in_specs=(P("row", ("col", "layer")), P("row", "col"), P(), P()),
            out_specs=P("row", ("col", "layer")),
            check_vma=False,
        )(hamiltonian, inv_root, h_pattern, z_pattern)

    return whole
```

```python
import functools
from typing import NamedTuple

import jax
import jax.numpy as jnp
from jax import lax
from jax.experimental import pallas as pl
from jax.experimental.pallas import tpu as pltpu
from jax.sharding import PartitionSpec as P

BS = 256
MARGIN = 4 * 1024 * 1024


class Sizes(NamedTuple):
    rows: int
    cols: int
    layers: int
    rows_here: int
    cols_here: int
    quarter: int
    per: int


def bits_of(size):
    return [1 << b for b in reversed(range(size.bit_length() - 1))]


def flip(size, bit):
    return [(i, i ^ bit) for i in range(size)]


def mod(a, n):
    return lax.rem(a + n, n)


def place():
    return lax.axis_index("row"), lax.axis_index("col"), lax.axis_index("layer")


def run(kernel, name, outs, arrays, smem=(), after=(), scratch=(), flops=0):
    size = sum(a.size * a.dtype.itemsize for a in arrays)
    size += sum(o.size * o.dtype.itemsize for o in outs)
    for kept in scratch:
        size += kept.shape[0] * kept.shape[1] * jnp.dtype(kept.dtype).itemsize
    skip = len(smem) + len(arrays)

    def body(*refs):
        kernel(*refs[:skip], *refs[skip + len(after) :])

    return pl.pallas_call(
        body,
        out_shape=list(outs),
        in_specs=[pl.BlockSpec(memory_space=pltpu.SMEM)] * len(smem)
        + [pl.BlockSpec(memory_space=pltpu.VMEM)] * len(arrays)
        + [pl.BlockSpec(memory_space=pl.ANY)] * len(after),
        out_specs=[pl.BlockSpec(memory_space=pltpu.VMEM)] * len(outs),
        scratch_shapes=list(scratch),
        compiler_params=pltpu.CompilerParams(vmem_limit_bytes=size + MARGIN),
        cost_estimate=pl.CostEstimate(flops=flops, bytes_accessed=size, transcendentals=0),
        name=name,
    )(*smem, *arrays, *after)


def shape(rows, columns, dtype=jnp.bfloat16):
    return jax.ShapeDtypeStruct((rows, columns), dtype)


def keep_block(pattern, i, j, block):
    return jnp.where(pattern[i, j] > 0, block, jnp.zeros_like(block))


def strip_start(l, half, sizes):
    return pl.multiple_of(half * sizes.cols_here + l * sizes.quarter, sizes.quarter)


def columns_of(cc, sizes):
    return pl.ds(pl.multiple_of(cc * sizes.cols_here, sizes.cols_here), sizes.cols_here)


def mask_strip(zp, r, l, half, cc, strip, sizes):
    block_row = (r * sizes.rows_here + half * sizes.cols_here + l * sizes.quarter) // BS
    first = cc * (sizes.cols_here // BS)
    return jnp.concatenate(
        [
            keep_block(zp, block_row, first + t, strip[:, t * BS : (t + 1) * BS])
            for t in range(sizes.cols_here // BS)
        ],
        axis=1,
    )


def mask_piece(zp, r, l, cc, piece, sizes):
    q = sizes.quarter
    return jnp.concatenate(
        [
            mask_strip(zp, r, l, half, cc, piece[half * q : (half + 1) * q, :], sizes)
            for half in range(sizes.per)
        ],
        axis=0,
    )


def pack_kernel(*refs):
    out, row = refs[-1], 0
    for ref in refs[:-1]:
        out[row : row + ref.shape[0], :] = ref[...]
        row += ref.shape[0]


def pack(pieces, after=()):
    height = sum(p.shape[0] for p in pieces)
    out = shape(height, pieces[0].shape[1])
    return run(pack_kernel, "pack", [out], pieces, after=after)[0]


def ring_place(c, cols):
    return jnp.where(c % 2 == 0, c // 2, cols - 1 - c // 2)


def ring_column(p, cols):
    return jnp.where(p < cols // 2, 2 * p, 2 * (cols - 1 - p) + 1)


def inner(c):
    return (c == 1) | (c == 2)


def slot_column(c, s, cols):
    if cols == 4:
        near, far = jnp.where(inner(c), c ^ 3, c ^ 2), jnp.where(inner(c), c ^ 2, c ^ 3)
        return (c, c ^ 1, near, far)[s]
    return ring_column(mod(ring_place(c, cols) - s, cols), cols)


def pick_kernel(inside, outside, out):
    c = lax.axis_index("col")

    @pl.when(inner(c))
    def _():
        out[...] = inside[...]

    @pl.when(jnp.logical_not(inner(c)))
    def _():
        out[...] = outside[...]


def pick(inside, outside):
    return run(pick_kernel, "pick", [shape(*inside.shape)], [inside, outside])[0]


def send(piece, *pairs):
    return lax.ppermute(piece, "col", pairs)


def gather_columns(own, cols):
    if cols == 4:
        first = send(own, (0, 1), (1, 0), (2, 3), (3, 2))
        middle = send(own, (1, 2), (2, 1))
        across = send(first, (1, 2), (2, 1))
        outer = send(middle, (1, 0), (2, 3))
        last = send(across, (1, 0), (2, 3))
        return [own, first, pick(middle, outer), pick(across, last)], [middle], [across, outer]
    trip = list(range(0, cols, 2)) + list(range(cols - 1, 0, -2))
    ring = [(trip[i], trip[(i + 1) % cols]) for i in range(cols)]
    slots = [own]
    for _ in range(1, cols):
        slots.append(lax.ppermute(slots[-1], "col", ring))
    return slots, [slots[1]], [slots[-2]]


def first_kernel(sizes, h_table, n_h, hp, zp, *refs):
    cols, q = sizes.cols, sizes.quarter
    slots, h_refs = refs[: cols - 1], refs[cols - 1 : cols - 1 + n_h]
    hm, total, zm = refs[cols - 1 + n_h :]
    r, c, l = place()
    for s in range(cols - 1):
        cc = slot_column(c, s, cols)
        zm[:, columns_of(cc, sizes)] = mask_piece(zp, r, l, cc, slots[s][...], sizes)
    zm[:, columns_of(slot_column(c, cols - 1, cols), sizes)] = jnp.zeros(
        (zm.shape[0], sizes.cols_here), zm.dtype
    )
    per_rows = sizes.rows_here // BS
    for index, row, dr, dl in h_table:
        rr, ll = r ^ dr, l ^ dl
        block_col = (c * sizes.cols_here + ll * q) // BS
        for t in range(per_rows):
            j = rr * per_rows + t
            hm[pl.ds(pl.multiple_of(j * BS, BS), BS), pl.ds(pl.multiple_of(ll * q, q), q)] = (
                keep_block(hp, j, block_col, h_refs[index][row + t * BS : row + (t + 1) * BS, :])
            )
    order = zm.shape[1]
    chunk = min(order, 2048)
    acc = None
    for k in range(0, order, chunk):
        part = jnp.dot(
            zm[:, k : k + chunk], hm[k : k + chunk, :], preferred_element_type=jnp.float32
        )
        acc = part if acc is None else acc + part
    total[...] = acc


def finish_kernel(sizes, zp, hm, total, last, out):
    r, c, l = place()
    cc = slot_column(c, sizes.cols - 1, sizes.cols)
    out[...] = (
        total[...]
        + jnp.dot(
            mask_piece(zp, r, l, cc, last[...], sizes),
            hm[columns_of(cc, sizes), :],
            preferred_element_type=jnp.float32,
        )
    ).astype(out.dtype)


def route_kernel(sizes, row_offsets, *refs):
    n = len(row_offsets)
    pieces, outs, table = refs[:n], refs[n:-1], refs[-1]
    r, c, _ = place()
    q = sizes.quarter
    for dr, piece in zip(row_offsets, pieces):
        for half in range(sizes.per):
            start = pl.multiple_of(((r ^ dr) * sizes.per + half) * q, q)
            table[pl.ds(start, q), :] = piece[half * q : (half + 1) * q, :]
    for d, out in enumerate(outs):
        out[...] = table[pl.ds(pl.multiple_of((c ^ d) * q, q), q), :]


def bring_kernel(hp, zp, h, piece, h_out, piece_out):
    h_out[...] = h[...]
    piece_out[...] = piece[...]


def layers_kernel(sizes, z_table, zp, *refs):
    cols, q = sizes.cols, sizes.quarter
    out, held = refs[-1], refs[:-1]
    r, c, l = place()
    for dl in range(sizes.layers):
        ll = l ^ dl
        for half in range(sizes.per):
            rows = pl.ds(strip_start(ll, half, sizes), q)
            for s in range(cols):
                cc = slot_column(c, s, cols)
                if s == 0:
                    strip = held[0][rows, :]
                else:
                    index, row = z_table[dl, s]
                    strip = held[index][row + half * q : row + (half + 1) * q, :]
                out[rows, columns_of(cc, sizes)] = mask_strip(zp, r, ll, half, cc, strip, sizes)


def second_kernel(sizes, part, z_full, *refs):
    messages, before, out = refs[: len(part)], refs[len(part) : -1], refs[-1]
    c = lax.axis_index("col")
    total = before[0][...] if before else None
    for d, message in zip(part, messages):
        added = lax.dot_general(
            z_full[:, columns_of(c ^ d, sizes)],
            message[...],
            (((1,), (1,)), ((), ())),
            preferred_element_type=jnp.float32,
        )
        total = added if total is None else total + added
    out[...] = total.astype(out.dtype)


def local(sizes, hamiltonian, inv_root, h_pattern, z_pattern):
    rows, cols, layers, per = sizes.rows, sizes.cols, sizes.layers, sizes.per
    q, cols_here, rows_here = sizes.quarter, sizes.cols_here, sizes.rows_here
    order = rows * rows_here
    height = per * q
    row_bits, layer_bits = bits_of(rows), bits_of(layers)
    f32 = jnp.float32

    striped = inv_root.reshape(per, layers, q, cols_here)
    l = lax.axis_index("layer")
    own = lax.dynamic_index_in_dim(striped, l, 1, keepdims=False).reshape(height, cols_here)
    slots, step_one, step_two = gather_columns(own, cols)

    def offsets(arrays):
        starts = [0]
        for array in arrays:
            starts.append(starts[-1] + array.shape[0])
        return starts

    top, low = layer_bits
    crossed = [lax.ppermute(slots[s], "layer", flip(layers, top)) for s in range(1, cols)]

    h_arrays, h_table = [hamiltonian], [(0, 0, 0, 0)]
    for axis, bit in [("layer", top)] + [("row", b) for b in row_bits]:
        for index, _, dr, dl in list(h_table):
            there = (dr ^ bit, dl) if axis == "row" else (dr, dl ^ bit)
            source = h_arrays[index]
            if index == 1:
                h_arrays[0], source = run(
                    bring_kernel,
                    "bring",
                    [shape(*hamiltonian.shape)] * 2,
                    [hamiltonian, source],
                    smem=[h_pattern, z_pattern],
                    after=[slots[1], *step_one],
                )
            h_table.append((len(h_arrays), 0) + there)
            h_arrays.append(
                lax.ppermute(source, axis, flip(rows if axis == "row" else layers, bit))
            )
    packed, starts = pack(h_arrays, [*step_two, crossed[0]]), offsets(h_arrays)
    h_table += [
        (len(h_arrays), starts[index] + row, dr, dl ^ low) for index, row, dr, dl in h_table
    ]
    h_arrays = h_arrays + [lax.ppermute(packed, "layer", flip(layers, low))]

    hm, total = run(
        functools.partial(first_kernel, sizes, h_table, len(h_arrays)),
        "first_product",
        [shape(order, cols_here), shape(height, cols_here, f32)],
        [*slots[:-1], *h_arrays],
        smem=[h_pattern, z_pattern],
        scratch=[pltpu.VMEM((height, order), jnp.bfloat16)],
    )
    product = run(
        functools.partial(finish_kernel, sizes),
        "finish_product",
        [shape(height, cols_here)],
        [hm, total, slots[-1]],
        smem=[z_pattern],
    )[0]

    gathered = {0: product}
    for bit in row_bits:
        for dr, piece in list(gathered.items()):
            gathered[dr ^ bit] = lax.ppermute(piece, "row", flip(rows, bit))
    row_offsets = list(gathered)
    outgoing = run(
        functools.partial(route_kernel, sizes, row_offsets),
        "route",
        [shape(q, cols_here)] * cols,
        [gathered[o] for o in row_offsets],
        after=[crossed[-1]],
        scratch=[pltpu.VMEM((cols * q, cols_here), jnp.bfloat16)],
    )
    messages = [outgoing[0]] + [
        lax.ppermute(outgoing[d], "col", flip(cols, d)) for d in range(1, cols)
    ]

    held, z_table = [inv_root], {}

    def share(group, gate):
        arrays, table = [], []
        for s in group:
            table += [(len(arrays), 0, 0, s), (len(arrays) + 1, 0, top, s)]
            arrays += [slots[s], crossed[s - 1]]
        starts = offsets(arrays)
        table += [(len(arrays), starts[index] + row, dl ^ low, s) for index, row, dl, s in table]
        for index, row, dl, s in table:
            z_table[dl, s] = (index + len(held), row)
        return arrays + [lax.ppermute(pack(arrays, gate), "layer", flip(layers, low))]

    held += share(range(1, cols - 1), [product])
    held += share([cols - 1], [outgoing[0]])
    z_full = run(
        functools.partial(layers_kernel, sizes, z_table),
        "layers",
        [shape(rows_here, order)],
        held,
        smem=[z_pattern],
    )[0]
    total = []
    for part in (range(cols // 2), range(cols // 2, cols)):
        last_part = part[-1] == cols - 1
        total = run(
            functools.partial(second_kernel, sizes, part),
            "second_product",
            [shape(*hamiltonian.shape, jnp.bfloat16 if last_part else f32)],
            [z_full, *[messages[d] for d in part], *total],
        )
    return total[0]


def solution(mesh):
    rows, cols, layers = (mesh.shape[a] for a in ("row", "col", "layer"))

    def whole(hamiltonian, inv_root, h_pattern, z_pattern):
        order = hamiltonian.shape[0]
        cols_here = order // cols
        sizes = Sizes(
            rows, cols, layers, order // rows, cols_here, cols_here // layers, cols // rows
        )
        return jax.shard_map(
            functools.partial(local, sizes),
            mesh=mesh,
            in_specs=(P("row", ("col", "layer")), P("row", "col"), P(), P()),
            out_specs=P("row", ("col", "layer")),
            check_vma=False,
        )(hamiltonian, inv_root, h_pattern, z_pattern)

    return whole
```

```python
import functools
from typing import NamedTuple

import jax
import jax.numpy as jnp
from jax import lax
from jax.experimental import pallas as pl
from jax.experimental.pallas import tpu as pltpu
from jax.sharding import PartitionSpec as P

BS = 256
MARGIN = 4 * 1024 * 1024


class Sizes(NamedTuple):
    rows: int
    cols: int
    layers: int
    rows_here: int
    cols_here: int
    quarter: int
    per: int


def bits_of(size):
    return [1 << b for b in reversed(range(size.bit_length() - 1))]


def flip(size, bit):
    return [(i, i ^ bit) for i in range(size)]


def mod(a, n):
    return lax.rem(a + n, n)


def place():
    return lax.axis_index("row"), lax.axis_index("col"), lax.axis_index("layer")


def run(kernel, name, outs, arrays, smem=(), after=(), scratch=(), flops=0):
    size = sum(a.size * a.dtype.itemsize for a in arrays)
    size += sum(o.size * o.dtype.itemsize for o in outs)
    for kept in scratch:
        size += kept.shape[0] * kept.shape[1] * jnp.dtype(kept.dtype).itemsize
    skip = len(smem) + len(arrays)

    def body(*refs):
        kernel(*refs[:skip], *refs[skip + len(after) :])

    return pl.pallas_call(
        body,
        out_shape=list(outs),
        in_specs=[pl.BlockSpec(memory_space=pltpu.SMEM)] * len(smem)
        + [pl.BlockSpec(memory_space=pltpu.VMEM)] * len(arrays)
        + [pl.BlockSpec(memory_space=pl.ANY)] * len(after),
        out_specs=[pl.BlockSpec(memory_space=pltpu.VMEM)] * len(outs),
        scratch_shapes=list(scratch),
        compiler_params=pltpu.CompilerParams(vmem_limit_bytes=size + MARGIN),
        cost_estimate=pl.CostEstimate(flops=flops, bytes_accessed=size, transcendentals=0),
        name=name,
    )(*smem, *arrays, *after)


def shape(rows, columns, dtype=jnp.bfloat16):
    return jax.ShapeDtypeStruct((rows, columns), dtype)


def keep_block(pattern, i, j, block):
    return jnp.where(pattern[i, j] > 0, block, jnp.zeros_like(block))


def strip_start(l, half, sizes):
    return pl.multiple_of(half * sizes.cols_here + l * sizes.quarter, sizes.quarter)


def columns_of(cc, sizes):
    return pl.ds(pl.multiple_of(cc * sizes.cols_here, sizes.cols_here), sizes.cols_here)


def mask_strip(zp, r, l, half, cc, strip, sizes):
    block_row = (r * sizes.rows_here + half * sizes.cols_here + l * sizes.quarter) // BS
    first = cc * (sizes.cols_here // BS)
    return jnp.concatenate(
        [
            keep_block(zp, block_row, first + t, strip[:, t * BS : (t + 1) * BS])
            for t in range(sizes.cols_here // BS)
        ],
        axis=1,
    )


def mask_piece(zp, r, l, cc, piece, sizes):
    q = sizes.quarter
    return jnp.concatenate(
        [
            mask_strip(zp, r, l, half, cc, piece[half * q : (half + 1) * q, :], sizes)
            for half in range(sizes.per)
        ],
        axis=0,
    )


def pack_kernel(*refs):
    out, row = refs[-1], 0
    for ref in refs[:-1]:
        out[row : row + ref.shape[0], :] = ref[...]
        row += ref.shape[0]


def pack(pieces, after=()):
    height = sum(p.shape[0] for p in pieces)
    out = shape(height, pieces[0].shape[1])
    return run(pack_kernel, "pack", [out], pieces, after=after)[0]


def slot_column(c, s, cols):
    return mod(c - s, cols)


def first_kernel(sizes, h_table, n_h, hp, zp, *refs):
    cols, q = sizes.cols, sizes.quarter
    slots, h_refs = refs[: cols - 1], refs[cols - 1 : cols - 1 + n_h]
    hm, total, zm = refs[cols - 1 + n_h :]
    r, c, l = place()
    for s in range(cols - 1):
        cc = slot_column(c, s, cols)
        zm[:, columns_of(cc, sizes)] = mask_piece(zp, r, l, cc, slots[s][...], sizes)
    zm[:, columns_of(slot_column(c, cols - 1, cols), sizes)] = jnp.zeros(
        (zm.shape[0], sizes.cols_here), zm.dtype
    )
    per_rows = sizes.rows_here // BS
    for index, row, dr, dl in h_table:
        rr, ll = r ^ dr, l ^ dl
        block_col = (c * sizes.cols_here + ll * q) // BS
        for t in range(per_rows):
            j = rr * per_rows + t
            hm[pl.ds(pl.multiple_of(j * BS, BS), BS), pl.ds(pl.multiple_of(ll * q, q), q)] = (
                keep_block(hp, j, block_col, h_refs[index][row + t * BS : row + (t + 1) * BS, :])
            )
    order = zm.shape[1]
    chunk = min(order, 2048)
    acc = None
    for k in range(0, order, chunk):
        part = jnp.dot(
            zm[:, k : k + chunk], hm[k : k + chunk, :], preferred_element_type=jnp.float32
        )
        acc = part if acc is None else acc + part
    total[...] = acc


def finish_kernel(sizes, zp, hm, total, last, out):
    r, c, l = place()
    cc = slot_column(c, sizes.cols - 1, sizes.cols)
    out[...] = (
        total[...]
        + jnp.dot(
            mask_piece(zp, r, l, cc, last[...], sizes),
            hm[columns_of(cc, sizes), :],
            preferred_element_type=jnp.float32,
        )
    ).astype(out.dtype)


def route_kernel(sizes, row_offsets, *refs):
    table, (r, _, _), q = refs[-1], place(), sizes.quarter
    for dr, piece in zip(row_offsets, refs[:-1]):
        for half in range(sizes.per):
            start = pl.multiple_of(((r ^ dr) * sizes.per + half) * q, q)
            table[pl.ds(start, q), :] = piece[half * q : (half + 1) * q, :]


def cut_kernel(sizes, table, *outs):
    c, q = lax.axis_index("col"), sizes.quarter
    for d, out in enumerate(outs):
        out[...] = table[pl.ds(pl.multiple_of((c ^ d) * q, q), q), :]


def layers_kernel(sizes, z_table, zp, *refs):
    cols, q = sizes.cols, sizes.quarter
    out, held = refs[-1], refs[:-1]
    r, c, l = place()
    for dl in range(sizes.layers):
        ll = l ^ dl
        for half in range(sizes.per):
            rows = pl.ds(strip_start(ll, half, sizes), q)
            for s in range(cols):
                cc = slot_column(c, s, cols)
                if s == 0:
                    strip = held[0][rows, :]
                else:
                    index, row = z_table[dl, s]
                    strip = held[index][row + half * q : row + (half + 1) * q, :]
                out[rows, columns_of(cc, sizes)] = mask_strip(zp, r, ll, half, cc, strip, sizes)


def second_kernel(sizes, part, z_full, *refs):
    messages, before, out = refs[: len(part)], refs[len(part) : -1], refs[-1]
    c = lax.axis_index("col")
    total = before[0][...] if before else None
    for d, message in zip(part, messages):
        added = lax.dot_general(
            z_full[:, columns_of(c ^ d, sizes)],
            message[...],
            (((1,), (1,)), ((), ())),
            preferred_element_type=jnp.float32,
        )
        total = added if total is None else total + added
    out[...] = total.astype(out.dtype)


def local(sizes, hamiltonian, inv_root, h_pattern, z_pattern):
    rows, cols, layers, per = sizes.rows, sizes.cols, sizes.layers, sizes.per
    q, cols_here, rows_here = sizes.quarter, sizes.cols_here, sizes.rows_here
    order = rows * rows_here
    height = per * q
    row_bits, layer_bits = bits_of(rows), bits_of(layers)
    f32 = jnp.float32

    striped = inv_root.reshape(per, layers, q, cols_here)
    l = lax.axis_index("layer")
    own = lax.dynamic_index_in_dim(striped, l, 1, keepdims=False).reshape(height, cols_here)
    ring = [(i, (i + 1) % cols) for i in range(cols)]
    slots = [own]
    for _ in range(1, cols):
        slots.append(lax.ppermute(slots[-1], "col", ring))

    def offsets(arrays):
        starts = [0]
        for array in arrays:
            starts.append(starts[-1] + array.shape[0])
        return starts

    def cross(piece):
        return lax.ppermute(piece, "layer", flip(layers, layer_bits[0]))

    top, low = layer_bits
    h_arrays, h_table = [hamiltonian], [(0, 0, 0, 0)]
    for axis, bit in [("layer", top)] + [("row", b) for b in row_bits]:
        perm = flip(rows if axis == "row" else layers, bit)
        for index, _, dr, dl in list(h_table):
            there = (dr ^ bit, dl) if axis == "row" else (dr, dl ^ bit)
            source = h_arrays[index]
            if index and False:
                source = pack([source], [slots[1]])
            h_table.append((len(h_arrays), 0) + there)
            h_arrays.append(lax.ppermute(source, axis, perm))
    across = lax.ppermute(hamiltonian, "layer", flip(layers, low))
    crossed = [cross(slots[1])] + [cross(slots[s]) for s in range(2, cols - 1)]
    packed, starts = pack(h_arrays[1:], [slots[-2], crossed[0]]), offsets(h_arrays[1:])
    n = len(h_arrays)
    h_table += [(n, 0, 0, low)] + [
        (n + 1, starts[index - 1], dr, dl ^ low) for index, _, dr, dl in h_table[1:]
    ]
    h_arrays = h_arrays + [across, lax.ppermute(packed, "layer", flip(layers, low))]

    hm, total = run(
        functools.partial(first_kernel, sizes, h_table, len(h_arrays)),
        "first_product",
        [shape(order, cols_here), shape(height, cols_here, f32)],
        [*slots[:-1], *h_arrays],
        smem=[h_pattern, z_pattern],
        scratch=[pltpu.VMEM((height, order), jnp.bfloat16)],
    )
    product = run(
        functools.partial(finish_kernel, sizes),
        "finish_product",
        [shape(height, cols_here)],
        [hm, total, slots[-1]],
        smem=[z_pattern],
    )[0]

    gathered = {0: product}
    for bit in row_bits:
        for dr, piece in list(gathered.items()):
            gathered[dr ^ bit] = lax.ppermute(piece, "row", flip(rows, bit))
    row_offsets = list(gathered)
    held, z_table = [inv_root], {}

    crossed.append(cross(pack([slots[-1]], [product])))
    table = run(
        functools.partial(route_kernel, sizes, row_offsets),
        "route",
        [shape(cols * q, cols_here)],
        [gathered[o] for o in row_offsets],
    )[0]
    outgoing = run(
        functools.partial(cut_kernel, sizes),
        "cut",
        [shape(q, cols_here)] * cols,
        [table],
        after=[crossed[-1]],
    )
    messages = [outgoing[0]] + [
        lax.ppermute(outgoing[d], "col", flip(cols, d)) for d in range(1, cols)
    ]

    for group, gate in ((range(1, cols - 1), [product]), ([cols - 1], [outgoing[0]])):
        arrays = [a for s in group for a in (slots[s], crossed[s - 1])]
        base = len(held)
        held += arrays + [lax.ppermute(pack(arrays, gate), "layer", flip(layers, low))]
        for n, s in enumerate(group):
            z_table[0, s], z_table[top, s] = (base + 2 * n, 0), (base + 2 * n + 1, 0)
            z_table[low, s] = (base + len(arrays), 2 * n * height)
            z_table[low ^ top, s] = (base + len(arrays), (2 * n + 1) * height)
    z_full = run(
        functools.partial(layers_kernel, sizes, z_table),
        "layers",
        [shape(rows_here, order)],
        held,
        smem=[z_pattern],
    )[0]
    total = []
    for part in (range(cols // 2), range(cols // 2, cols)):
        last_part = part[-1] == cols - 1
        total = run(
            functools.partial(second_kernel, sizes, part),
            "second_product",
            [shape(*hamiltonian.shape, jnp.bfloat16 if last_part else f32)],
            [z_full, *[messages[d] for d in part], *total],
        )
    return total[0]


def solution(mesh):
    rows, cols, layers = (mesh.shape[a] for a in ("row", "col", "layer"))

    def whole(hamiltonian, inv_root, h_pattern, z_pattern):
        order = hamiltonian.shape[0]
        cols_here = order // cols
        sizes = Sizes(
            rows, cols, layers, order // rows, cols_here, cols_here // layers, cols // rows
        )
        return jax.shard_map(
            functools.partial(local, sizes),
            mesh=mesh,
            in_specs=(P("row", ("col", "layer")), P("row", "col"), P(), P()),
            out_specs=P("row", ("col", "layer")),
            check_vma=False,
        )(hamiltonian, inv_root, h_pattern, z_pattern)

    return whole
```

```python
import functools
from typing import NamedTuple

import jax
import jax.numpy as jnp
from jax import lax
from jax.experimental import pallas as pl
from jax.experimental.pallas import tpu as pltpu
from jax.sharding import PartitionSpec as P

BS = 256
MARGIN = 4 * 1024 * 1024


class Sizes(NamedTuple):
    rows: int
    cols: int
    layers: int
    rows_here: int
    cols_here: int
    quarter: int
    per: int


def bits_of(size):
    return [1 << b for b in reversed(range(size.bit_length() - 1))]


def flip(size, bit):
    return [(i, i ^ bit) for i in range(size)]


def mod(a, n):
    return lax.rem(a + n, n)


def place():
    return lax.axis_index("row"), lax.axis_index("col"), lax.axis_index("layer")


def run(kernel, name, outs, arrays, smem=(), after=(), scratch=(), flops=0):
    size = sum(a.size * a.dtype.itemsize for a in arrays)
    size += sum(o.size * o.dtype.itemsize for o in outs)
    for kept in scratch:
        size += kept.shape[0] * kept.shape[1] * jnp.dtype(kept.dtype).itemsize
    skip = len(smem) + len(arrays)

    def body(*refs):
        kernel(*refs[:skip], *refs[skip + len(after) :])

    return pl.pallas_call(
        body,
        out_shape=list(outs),
        in_specs=[pl.BlockSpec(memory_space=pltpu.SMEM)] * len(smem)
        + [pl.BlockSpec(memory_space=pltpu.VMEM)] * len(arrays)
        + [pl.BlockSpec(memory_space=pl.ANY)] * len(after),
        out_specs=[pl.BlockSpec(memory_space=pltpu.VMEM)] * len(outs),
        scratch_shapes=list(scratch),
        compiler_params=pltpu.CompilerParams(vmem_limit_bytes=size + MARGIN),
        cost_estimate=pl.CostEstimate(flops=flops, bytes_accessed=size, transcendentals=0),
        name=name,
    )(*smem, *arrays, *after)


def shape(rows, columns, dtype=jnp.bfloat16):
    return jax.ShapeDtypeStruct((rows, columns), dtype)


def keep_block(pattern, i, j, block):
    return jnp.where(pattern[i, j] > 0, block, jnp.zeros_like(block))


def strip_start(l, half, sizes):
    return pl.multiple_of(half * sizes.cols_here + l * sizes.quarter, sizes.quarter)


def columns_of(cc, sizes):
    return pl.ds(pl.multiple_of(cc * sizes.cols_here, sizes.cols_here), sizes.cols_here)


def mask_strip(zp, r, l, half, cc, strip, sizes):
    block_row = (r * sizes.rows_here + half * sizes.cols_here + l * sizes.quarter) // BS
    first = cc * (sizes.cols_here // BS)
    return jnp.concatenate(
        [
            keep_block(zp, block_row, first + t, strip[:, t * BS : (t + 1) * BS])
            for t in range(sizes.cols_here // BS)
        ],
        axis=1,
    )


def mask_piece(zp, r, l, cc, piece, sizes):
    q = sizes.quarter
    return jnp.concatenate(
        [
            mask_strip(zp, r, l, half, cc, piece[half * q : (half + 1) * q, :], sizes)
            for half in range(sizes.per)
        ],
        axis=0,
    )


def pack_kernel(*refs):
    out, row = refs[-1], 0
    for ref in refs[:-1]:
        out[row : row + ref.shape[0], :] = ref[...]
        row += ref.shape[0]


def pack(pieces, after=()):
    height = sum(p.shape[0] for p in pieces)
    out = shape(height, pieces[0].shape[1])
    return run(pack_kernel, "pack", [out], pieces, after=after)[0]


def slot_column(c, s, cols):
    return mod(c - s, cols)


def first_kernel(sizes, h_table, n_h, hp, zp, *refs):
    cols, q = sizes.cols, sizes.quarter
    slots, h_refs = refs[: cols - 1], refs[cols - 1 : cols - 1 + n_h]
    hm, total, zm = refs[cols - 1 + n_h :]
    r, c, l = place()
    for s in range(cols - 1):
        cc = slot_column(c, s, cols)
        zm[:, columns_of(cc, sizes)] = mask_piece(zp, r, l, cc, slots[s][...], sizes)
    zm[:, columns_of(slot_column(c, cols - 1, cols), sizes)] = jnp.zeros(
        (zm.shape[0], sizes.cols_here), zm.dtype
    )
    per_rows = sizes.rows_here // BS
    for index, row, dr, dl in h_table:
        rr, ll = r ^ dr, l ^ dl
        block_col = (c * sizes.cols_here + ll * q) // BS
        for t in range(per_rows):
            j = rr * per_rows + t
            hm[pl.ds(pl.multiple_of(j * BS, BS), BS), pl.ds(pl.multiple_of(ll * q, q), q)] = (
                keep_block(hp, j, block_col, h_refs[index][row + t * BS : row + (t + 1) * BS, :])
            )
    order = zm.shape[1]
    chunk = min(order, 2048)
    acc = None
    for k in range(0, order, chunk):
        part = jnp.dot(
            zm[:, k : k + chunk], hm[k : k + chunk, :], preferred_element_type=jnp.float32
        )
        acc = part if acc is None else acc + part
    total[...] = acc


def finish_kernel(sizes, zp, hm, total, last, out):
    r, c, l = place()
    cc = slot_column(c, sizes.cols - 1, sizes.cols)
    out[...] = (
        total[...]
        + jnp.dot(
            mask_piece(zp, r, l, cc, last[...], sizes),
            hm[columns_of(cc, sizes), :],
            preferred_element_type=jnp.float32,
        )
    ).astype(out.dtype)


def route_kernel(sizes, row_offsets, *refs):
    table, (r, _, _), q = refs[-1], place(), sizes.quarter
    for dr, piece in zip(row_offsets, refs[:-1]):
        for half in range(sizes.per):
            start = pl.multiple_of(((r ^ dr) * sizes.per + half) * q, q)
            table[pl.ds(start, q), :] = piece[half * q : (half + 1) * q, :]


def cut_kernel(sizes, table, *outs):
    c, q = lax.axis_index("col"), sizes.quarter
    for d, out in enumerate(outs):
        out[...] = table[pl.ds(pl.multiple_of((c ^ d) * q, q), q), :]


def layers_kernel(sizes, z_table, zp, *refs):
    cols, q = sizes.cols, sizes.quarter
    out, held = refs[-1], refs[:-1]
    r, c, l = place()
    for dl in range(sizes.layers):
        ll = l ^ dl
        for half in range(sizes.per):
            rows = pl.ds(strip_start(ll, half, sizes), q)
            for s in range(cols):
                cc = slot_column(c, s, cols)
                if s == 0:
                    strip = held[0][rows, :]
                else:
                    index, row = z_table[dl, s]
                    strip = held[index][row + half * q : row + (half + 1) * q, :]
                out[rows, columns_of(cc, sizes)] = mask_strip(zp, r, ll, half, cc, strip, sizes)


def second_kernel(sizes, part, z_full, *refs):
    messages, before, out = refs[: len(part)], refs[len(part) : -1], refs[-1]
    c = lax.axis_index("col")
    total = before[0][...] if before else None
    for d, message in zip(part, messages):
        added = lax.dot_general(
            z_full[:, columns_of(c ^ d, sizes)],
            message[...],
            (((1,), (1,)), ((), ())),
            preferred_element_type=jnp.float32,
        )
        total = added if total is None else total + added
    out[...] = total.astype(out.dtype)


def local(sizes, hamiltonian, inv_root, h_pattern, z_pattern):
    rows, cols, layers, per = sizes.rows, sizes.cols, sizes.layers, sizes.per
    q, cols_here, rows_here = sizes.quarter, sizes.cols_here, sizes.rows_here
    order = rows * rows_here
    height = per * q
    row_bits, layer_bits = bits_of(rows), bits_of(layers)
    f32 = jnp.float32

    striped = inv_root.reshape(per, layers, q, cols_here)
    l = lax.axis_index("layer")
    own = lax.dynamic_index_in_dim(striped, l, 1, keepdims=False).reshape(height, cols_here)
    ring = [(i, (i + 1) % cols) for i in range(cols)]
    slots = [own]
    for _ in range(1, cols):
        slots.append(lax.ppermute(slots[-1], "col", ring))

    def offsets(arrays):
        starts = [0]
        for array in arrays:
            starts.append(starts[-1] + array.shape[0])
        return starts

    def cross(piece):
        return lax.ppermute(piece, "layer", flip(layers, layer_bits[0]))

    top, low = layer_bits
    h_arrays, h_table = [hamiltonian], [(0, 0, 0, 0)]
    for axis, bit in [("layer", top)] + [("row", b) for b in row_bits]:
        perm = flip(rows if axis == "row" else layers, bit)
        for index, _, dr, dl in list(h_table):
            there = (dr ^ bit, dl) if axis == "row" else (dr, dl ^ bit)
            source = h_arrays[index]
            if index and False:
                source = pack([source], [slots[1]])
            h_table.append((len(h_arrays), 0) + there)
            h_arrays.append(lax.ppermute(source, axis, perm))
    across = lax.ppermute(hamiltonian, "layer", flip(layers, low))
    crossed = [cross(slots[1])] + [cross(slots[s]) for s in range(2, cols - 1)]
    packed, starts = pack(h_arrays[1:], [slots[-2], crossed[0]]), offsets(h_arrays[1:])
    n = len(h_arrays)
    h_table += [(n, 0, 0, low)] + [
        (n + 1, starts[index - 1], dr, dl ^ low) for index, _, dr, dl in h_table[1:]
    ]
    h_arrays = h_arrays + [across, lax.ppermute(packed, "layer", flip(layers, low))]

    hm, total = run(
        functools.partial(first_kernel, sizes, h_table, len(h_arrays)),
        "first_product",
        [shape(order, cols_here), shape(height, cols_here, f32)],
        [*slots[:-1], *h_arrays],
        smem=[h_pattern, z_pattern],
        scratch=[pltpu.VMEM((height, order), jnp.bfloat16)],
    )
    product = run(
        functools.partial(finish_kernel, sizes),
        "finish_product",
        [shape(height, cols_here)],
        [hm, total, slots[-1]],
        smem=[z_pattern],
    )[0]

    gathered = {0: product}
    for bit in row_bits:
        for dr, piece in list(gathered.items()):
            gathered[dr ^ bit] = lax.ppermute(piece, "row", flip(rows, bit))
    row_offsets = list(gathered)
    held, z_table = [inv_root], {}

    crossed.append(cross(pack([slots[-1]], [product])))
    table = run(
        functools.partial(route_kernel, sizes, row_offsets),
        "route",
        [shape(cols * q, cols_here)],
        [gathered[o] for o in row_offsets],
    )[0]
    outgoing = run(
        functools.partial(cut_kernel, sizes),
        "cut",
        [shape(q, cols_here)] * cols,
        [table],
        after=[crossed[-1]],
    )
    messages = [
        lax.ppermute(outgoing[d], "col", flip(cols, d)) for d in range(cols - 1, 0, -1)
    ]
    messages = [outgoing[0]] + messages[::-1]

    for group, gate in ((range(1, cols - 1), [product]), ([cols - 1], [outgoing[0]])):
        arrays = [a for s in group for a in (slots[s], crossed[s - 1])]
        base = len(held)
        held += arrays + [lax.ppermute(pack(arrays, gate), "layer", flip(layers, low))]
        for n, s in enumerate(group):
            z_table[0, s], z_table[top, s] = (base + 2 * n, 0), (base + 2 * n + 1, 0)
            z_table[low, s] = (base + len(arrays), 2 * n * height)
            z_table[low ^ top, s] = (base + len(arrays), (2 * n + 1) * height)
    z_full = run(
        functools.partial(layers_kernel, sizes, z_table),
        "layers",
        [shape(rows_here, order)],
        held,
        smem=[z_pattern],
    )[0]
    total = []
    far = list(range(cols - 1, cols // 2, -1))
    for part in ([0, *far], [d for d in range(cols - 1, 0, -1) if d not in far]):
        last_part = 0 not in part
        total = run(
            functools.partial(second_kernel, sizes, part),
            "second_product",
            [shape(*hamiltonian.shape, jnp.bfloat16 if last_part else f32)],
            [z_full, *[messages[d] for d in part], *total],
        )
    return total[0]


def solution(mesh):
    rows, cols, layers = (mesh.shape[a] for a in ("row", "col", "layer"))

    def whole(hamiltonian, inv_root, h_pattern, z_pattern):
        order = hamiltonian.shape[0]
        cols_here = order // cols
        sizes = Sizes(
            rows, cols, layers, order // rows, cols_here, cols_here // layers, cols // rows
        )
        return jax.shard_map(
            functools.partial(local, sizes),
            mesh=mesh,
            in_specs=(P("row", ("col", "layer")), P("row", "col"), P(), P()),
            out_specs=P("row", ("col", "layer")),
            check_vma=False,
        )(hamiltonian, inv_root, h_pattern, z_pattern)

    return whole
```

```python
import functools
from typing import NamedTuple

import jax
import jax.numpy as jnp
from jax import lax
from jax.experimental import pallas as pl
from jax.experimental.pallas import tpu as pltpu
from jax.sharding import PartitionSpec as P

BS = 256
MARGIN = 4 * 1024 * 1024


class Sizes(NamedTuple):
    rows: int
    cols: int
    layers: int
    rows_here: int
    cols_here: int
    quarter: int
    per: int


def bits_of(size):
    return [1 << b for b in reversed(range(size.bit_length() - 1))]


def flip(size, bit):
    return [(i, i ^ bit) for i in range(size)]


def mod(a, n):
    return lax.rem(a + n, n)


def place():
    return lax.axis_index("row"), lax.axis_index("col"), lax.axis_index("layer")


def run(kernel, name, outs, arrays, smem=(), after=(), scratch=(), flops=0):
    size = sum(a.size * a.dtype.itemsize for a in arrays)
    size += sum(o.size * o.dtype.itemsize for o in outs)
    for kept in scratch:
        size += kept.shape[0] * kept.shape[1] * jnp.dtype(kept.dtype).itemsize
    skip = len(smem) + len(arrays)

    def body(*refs):
        kernel(*refs[:skip], *refs[skip + len(after) :])

    return pl.pallas_call(
        body,
        out_shape=list(outs),
        in_specs=[pl.BlockSpec(memory_space=pltpu.SMEM)] * len(smem)
        + [pl.BlockSpec(memory_space=pltpu.VMEM)] * len(arrays)
        + [pl.BlockSpec(memory_space=pl.ANY)] * len(after),
        out_specs=[pl.BlockSpec(memory_space=pltpu.VMEM)] * len(outs),
        scratch_shapes=list(scratch),
        compiler_params=pltpu.CompilerParams(vmem_limit_bytes=size + MARGIN),
        cost_estimate=pl.CostEstimate(flops=flops, bytes_accessed=size, transcendentals=0),
        name=name,
    )(*smem, *arrays, *after)


def shape(rows, columns, dtype=jnp.bfloat16):
    return jax.ShapeDtypeStruct((rows, columns), dtype)


def keep_block(pattern, i, j, block):
    return jnp.where(pattern[i, j] > 0, block, jnp.zeros_like(block))


def strip_start(l, half, sizes):
    return pl.multiple_of(half * sizes.cols_here + l * sizes.quarter, sizes.quarter)


def columns_of(cc, sizes):
    return pl.ds(pl.multiple_of(cc * sizes.cols_here, sizes.cols_here), sizes.cols_here)


def mask_strip(zp, r, l, half, cc, strip, sizes):
    block_row = (r * sizes.rows_here + half * sizes.cols_here + l * sizes.quarter) // BS
    first = cc * (sizes.cols_here // BS)
    return jnp.concatenate(
        [
            keep_block(zp, block_row, first + t, strip[:, t * BS : (t + 1) * BS])
            for t in range(sizes.cols_here // BS)
        ],
        axis=1,
    )


def mask_piece(zp, r, l, cc, piece, sizes):
    q = sizes.quarter
    return jnp.concatenate(
        [
            mask_strip(zp, r, l, half, cc, piece[half * q : (half + 1) * q, :], sizes)
            for half in range(sizes.per)
        ],
        axis=0,
    )


def pack_kernel(*refs):
    out, row = refs[-1], 0
    for ref in refs[:-1]:
        out[row : row + ref.shape[0], :] = ref[...]
        row += ref.shape[0]


def pack(pieces, after=()):
    height = sum(p.shape[0] for p in pieces)
    out = shape(height, pieces[0].shape[1])
    return run(pack_kernel, "pack", [out], pieces, after=after)[0]


def slot_column(c, s, cols):
    return mod(c - (s + 1) // 2 if s % 2 else c + s // 2, cols)


def mask_kernel(sizes, zp, *refs):
    slots, out = refs[:-1], refs[-1]
    r, c, l = place()
    out[...] = jnp.zeros_like(out)
    for s, slot in enumerate(slots):
        cc = slot_column(c, s, sizes.cols)
        out[:, columns_of(cc, sizes)] = mask_piece(zp, r, l, cc, slot[...], sizes)


def bring_kernel(sizes, dr, with_z, hp, zp, near, far, *refs):
    slots, blocks = (refs[: sizes.cols - 1], refs[sizes.cols :]) if with_z else ((), refs)
    r, c, l = place()
    q, wide = sizes.quarter, sizes.cols_here
    for n, (h, dl) in enumerate(((near, 0), (far, sizes.layers // 2))):
        block_col = (c * wide + (l ^ dl) * q) // BS
        for part in range(sizes.per):
            for first in range(0, wide, BS):
                row = part * wide + first
                j = ((r ^ dr) * sizes.rows_here + row) // BS
                blocks[part][first : first + BS, n * q : (n + 1) * q] = keep_block(
                    hp, j, block_col, h[row : row + BS, :]
                )
    if with_z:
        mask_kernel(sizes, zp, *slots, refs[sizes.cols - 1])


def first_kernel(sizes, zp, zm, last, *refs):
    cols, q, width, per = sizes.cols, sizes.quarter, sizes.cols_here, sizes.per
    sides, (out, zs) = (refs[:cols], refs[cols : 2 * cols]), refs[-2:]
    r, c, l = place()
    cc = slot_column(c, cols - 1, cols)
    zs[...] = zm[...]
    zs[:, columns_of(cc, sizes)] = mask_piece(zp, r, l, cc, last[...], sizes)
    for side, blocks in zip((l, l ^ 1), sides):
        acc = None
        for n, block in enumerate(blocks):
            at = (r ^ (n // per)) * per + n % per
            part = jnp.dot(
                zs[:, columns_of(at, sizes)], block[...], preferred_element_type=jnp.float32
            )
            acc = part if acc is None else acc + part
        for n, ll in enumerate((side, side ^ (sizes.layers // 2))):
            out[:, pl.ds(pl.multiple_of(ll * q, q), q)] = acc[:, n * q : (n + 1) * q].astype(
                out.dtype
            )


def route_kernel(sizes, row_offsets, *refs):
    n = len(row_offsets)
    pieces, outs, table = refs[:n], refs[n:-1], refs[-1]
    r, c, _ = place()
    q = sizes.quarter
    for dr, piece in zip(row_offsets, pieces):
        for half in range(sizes.per):
            start = pl.multiple_of(((r ^ dr) * sizes.per + half) * q, q)
            table[pl.ds(start, q), :] = piece[half * q : (half + 1) * q, :]
    for d, out in enumerate(outs):
        out[...] = table[pl.ds(pl.multiple_of((c ^ d) * q, q), q), :]


def split_kernel(*refs):
    pieces, outs = [], []
    for ref in refs:
        (pieces if ref.shape[0] > refs[-1].shape[0] else outs).append(ref)
    per, height = len(outs) // len(pieces), outs[0].shape[0]
    for n, out in enumerate(outs):
        first = n % per * height
        out[...] = pieces[n // per][first : first + height, :]


def layers_kernel(sizes, z_table, zp, *refs):
    cols, q = sizes.cols, sizes.quarter
    out, held = refs[-1], refs[:-1]
    r, c, l = place()
    for dl in range(sizes.layers):
        ll = l ^ dl
        for half in range(sizes.per):
            rows = pl.ds(strip_start(ll, half, sizes), q)
            for s in range(cols):
                cc = slot_column(c, s, cols)
                columns = columns_of(cc, sizes)
                if s and (dl, s) not in z_table:
                    out[rows, columns] = jnp.zeros((q, sizes.cols_here), out.dtype)
                    continue
                if s == 0:
                    strip = held[0][rows, :]
                else:
                    index, row = z_table[dl, s]
                    strip = held[index][row + half * q : row + (half + 1) * q, :]
                out[rows, columns] = mask_strip(zp, r, ll, half, cc, strip, sizes)


def turned_dot(left, right):
    return lax.dot_general(
        left, right, (((1,), (1,)), ((), ())), preferred_element_type=jnp.float32
    )


def second_kernel(sizes, part, z_full, *refs):
    messages, before, out = refs[: len(part)], refs[len(part) : -1], refs[-1]
    c = lax.axis_index("col")
    total = before[0][...] if before else None
    for d, message in zip(part, messages):
        added = turned_dot(z_full[:, columns_of(c ^ d, sizes)], message[...])
        total = added if total is None else total + added
    out[...] = total


def last_kernel(sizes, offsets, zp, total, *refs):
    cols, q, per = sizes.cols, sizes.quarter, sizes.per
    messages, strips, out, xm, acc = refs[:cols], refs[cols:-3], refs[-3], refs[-2], refs[-1]
    r, c, l = place()
    for d, message in enumerate(messages):
        xm[:, columns_of(c ^ d, sizes)] = message[...]
    acc[...] = total[...]
    cc = slot_column(c, cols - 1, cols)
    for n, dl in enumerate(offsets):
        for half in range(per):
            rows = pl.ds(strip_start(l ^ dl, half, sizes), q)
            strip = strips[n * per + half][...]
            acc[rows, :] += turned_dot(
                mask_strip(zp, r, l ^ dl, half, cc, strip, sizes), xm[:, columns_of(cc, sizes)]
            )
    out[...] = acc[...].astype(out.dtype)


def local(sizes, hamiltonian, inv_root, h_pattern, z_pattern):
    rows, cols, layers, per = sizes.rows, sizes.cols, sizes.layers, sizes.per
    q, cols_here, rows_here = sizes.quarter, sizes.cols_here, sizes.rows_here
    order = rows * rows_here
    height = per * q
    row_bits, layer_bits = bits_of(rows), bits_of(layers)
    f32 = jnp.float32
    strip_shape = shape(q, cols_here)

    striped = inv_root.reshape(per, layers, q, cols_here)
    l = lax.axis_index("layer")
    own = lax.dynamic_index_in_dim(striped, l, 1, keepdims=False).reshape(height, cols_here)
    slots = [own]
    right = left = own
    for s in range(1, cols):
        if s % 2:
            right = lax.ppermute(right, "col", [(i, (i + 1) % cols) for i in range(cols)])
        else:
            left = lax.ppermute(left, "col", [(i, (i - 1) % cols) for i in range(cols)])
        slots.append(right if s % 2 else left)

    def cross(piece):
        return lax.ppermute(piece, "layer", flip(layers, layer_bits[0]))

    top, low = layer_bits
    h_pieces, h_table = [hamiltonian], [(0, 0)]
    for axis, bit in [("layer", top)] + [("row", b) for b in row_bits]:
        perm = flip(rows if axis == "row" else layers, bit)
        for piece, (dr, dl) in list(zip(h_pieces, h_table)):
            h_table.append((dr ^ bit, dl) if axis == "row" else (dr, dl ^ bit))
            if dl and axis == 'row':
                piece = pack([piece], [slots[1]])
            h_pieces.append(lax.ppermute(piece, axis, perm))
    h_own, h_other, zm = [], [], []
    for dr in range(rows):
        with_z = dr == rows - 1
        blocks = run(
            functools.partial(bring_kernel, sizes, dr, with_z),
            "bring",
            ([shape(height, order)] if with_z else []) + [shape(cols_here, 2 * q)] * per,
            [h_pieces[h_table.index((dr, 0))], h_pieces[h_table.index((dr, top))]]
            + (slots[:-1] if with_z else []),
            smem=[h_pattern, z_pattern],
            after=h_other[-per:] or slots[2:3],
        )
        zm, h_own = blocks[:-per], [*h_own, *blocks[-per:]]
        h_other += [lax.ppermute(block, "layer", flip(layers, low)) for block in blocks[-per:]]
    product = run(
        functools.partial(first_kernel, sizes),
        "first_product",
        [shape(height, cols_here)],
        [*zm, slots[-1], *h_own, *h_other],
        smem=[z_pattern],
        scratch=[pltpu.VMEM((height, order), jnp.bfloat16)],
    )[0]

    gathered = {0: product}
    for bit in row_bits:
        for dr, piece in list(gathered.items()):
            gathered[dr ^ bit] = lax.ppermute(piece, "row", flip(rows, bit))
    row_offsets = list(gathered)
    held, z_table = [inv_root], {}

    last = pack([slots[-1]], [product])
    last_top = cross(last)
    outgoing = run(
        functools.partial(route_kernel, sizes, row_offsets),
        "route",
        [shape(q, cols_here)] * cols,
        [gathered[o] for o in row_offsets],
        scratch=[pltpu.VMEM((cols * q, cols_here), jnp.bfloat16)],
    )
    messages = [outgoing[0]] + [
        lax.ppermute(outgoing[d], "col", flip(cols, d)) for d in range(1, cols)
    ]
    group = range(1, cols - 1)
    mine = pack([slots[s] for s in group])
    other = cross(mine)
    both = lax.ppermute(pack([mine, other], [outgoing[0]]), "layer", flip(layers, low))
    held, z_table = [inv_root, mine, other, both, last, last_top], {}
    for n, s in enumerate(group):
        row = n * height
        z_table[0, s], z_table[top, s], z_table[low, s] = (1, row), (2, row), (3, row)
        z_table[low ^ top, s] = (3, len(group) * height + row)
    z_table[0, cols - 1], z_table[top, cols - 1] = (4, 0), (5, 0)
    parts = run(split_kernel, "split", [strip_shape] * (2 * per), [last, last_top])
    parts = [lax.ppermute(part, "layer", flip(layers, low)) for part in parts]
    z_full = run(
        functools.partial(layers_kernel, sizes, z_table),
        "layers",
        [shape(rows_here, order)],
        held,
        smem=[z_pattern],
    )[0]
    total = []
    for part in (range(cols // 2), range(cols // 2, cols)):
        total = run(
            functools.partial(second_kernel, sizes, part),
            "second_product",
            [shape(*hamiltonian.shape, f32)],
            [z_full, *[messages[d] for d in part], *total],
        )
    return run(
        functools.partial(last_kernel, sizes, (low, low ^ top)),
        "last_product",
        [shape(*hamiltonian.shape)],
        [*total, *messages, *parts],
        smem=[z_pattern],
        scratch=[pltpu.VMEM((q, order), jnp.bfloat16), pltpu.VMEM(hamiltonian.shape, f32)],
    )[0]


def solution(mesh):
    rows, cols, layers = (mesh.shape[a] for a in ("row", "col", "layer"))

    def whole(hamiltonian, inv_root, h_pattern, z_pattern):
        order = hamiltonian.shape[0]
        cols_here = order // cols
        sizes = Sizes(
            rows, cols, layers, order // rows, cols_here, cols_here // layers, cols // rows
        )
        return jax.shard_map(
            functools.partial(local, sizes),
            mesh=mesh,
            in_specs=(P("row", ("col", "layer")), P("row", "col"), P(), P()),
            out_specs=P("row", ("col", "layer")),
            check_vma=False,
        )(hamiltonian, inv_root, h_pattern, z_pattern)

    return whole
```

```python
import functools
from typing import NamedTuple

import jax
import jax.numpy as jnp
from jax import lax
from jax.experimental import pallas as pl
from jax.experimental.pallas import tpu as pltpu
from jax.sharding import PartitionSpec as P

BS = 256
MARGIN = 4 * 1024 * 1024


class Sizes(NamedTuple):
    rows: int
    cols: int
    layers: int
    rows_here: int
    cols_here: int
    quarter: int
    per: int


def bits_of(size):
    return [1 << b for b in reversed(range(size.bit_length() - 1))]


def flip(size, bit):
    return [(i, i ^ bit) for i in range(size)]


def mod(a, n):
    return lax.rem(a + n, n)


def place():
    return lax.axis_index("row"), lax.axis_index("col"), lax.axis_index("layer")


def run(kernel, name, outs, arrays, smem=(), after=(), scratch=(), flops=0):
    size = sum(a.size * a.dtype.itemsize for a in arrays)
    size += sum(o.size * o.dtype.itemsize for o in outs)
    for kept in scratch:
        size += kept.shape[0] * kept.shape[1] * jnp.dtype(kept.dtype).itemsize
    skip = len(smem) + len(arrays)

    def body(*refs):
        kernel(*refs[:skip], *refs[skip + len(after) :])

    return pl.pallas_call(
        body,
        out_shape=list(outs),
        in_specs=[pl.BlockSpec(memory_space=pltpu.SMEM)] * len(smem)
        + [pl.BlockSpec(memory_space=pltpu.VMEM)] * len(arrays)
        + [pl.BlockSpec(memory_space=pl.ANY)] * len(after),
        out_specs=[
            pl.BlockSpec(memory_space=pltpu.SMEM if o.dtype == jnp.int32 else pltpu.VMEM)
            for o in outs
        ],
        scratch_shapes=list(scratch),
        compiler_params=pltpu.CompilerParams(vmem_limit_bytes=size + MARGIN),
        cost_estimate=pl.CostEstimate(flops=flops, bytes_accessed=size, transcendentals=0),
        name=name,
    )(*smem, *arrays, *after)


def shape(rows, columns, dtype=jnp.bfloat16):
    return jax.ShapeDtypeStruct((rows, columns), dtype)


def keep_block(pattern, i, j, block):
    return jnp.where(pattern[i, j] > 0, block, jnp.zeros_like(block))


def strip_start(l, half, sizes):
    return pl.multiple_of(half * sizes.cols_here + l * sizes.quarter, sizes.quarter)


def columns_of(cc, sizes):
    return pl.ds(pl.multiple_of(cc * sizes.cols_here, sizes.cols_here), sizes.cols_here)


def mask_strip(zp, r, l, half, cc, strip, sizes):
    block_row = (r * sizes.rows_here + half * sizes.cols_here + l * sizes.quarter) // BS
    first = cc * (sizes.cols_here // BS)
    return jnp.concatenate(
        [
            keep_block(zp, block_row, first + t, strip[:, t * BS : (t + 1) * BS])
            for t in range(sizes.cols_here // BS)
        ],
        axis=1,
    )


def mask_piece(zp, r, l, cc, piece, sizes):
    q = sizes.quarter
    return jnp.concatenate(
        [
            mask_strip(zp, r, l, half, cc, piece[half * q : (half + 1) * q, :], sizes)
            for half in range(sizes.per)
        ],
        axis=0,
    )


def pack_kernel(*refs):
    out, row = refs[-1], 0
    for ref in refs[:-1]:
        out[row : row + ref.shape[0], :] = ref[...]
        row += ref.shape[0]


def pack(pieces, after=()):
    height = sum(p.shape[0] for p in pieces)
    out = shape(height, pieces[0].shape[1])
    return run(pack_kernel, "pack", [out], pieces, after=after)[0]


def slot_column(c, s, cols):
    return mod(c - (s + 1) // 2 if s % 2 else c + s // 2, cols)


def mask_kernel(sizes, zp, *refs):
    slots, out = refs[:-1], refs[-1]
    r, c, l = place()
    out[...] = jnp.zeros_like(out)
    for s, slot in enumerate(slots):
        cc = slot_column(c, s, sizes.cols)
        out[:, columns_of(cc, sizes)] = mask_piece(zp, r, l, cc, slot[...], sizes)


def fetch_kernel(hp, zp, h, hp_out, zp_out, h_out):
    h_out[...] = h[...]
    for i in range(hp.shape[0]):
        for j in range(hp.shape[1]):
            hp_out[i, j] = hp[i, j]
            zp_out[i, j] = zp[i, j]


def bring_kernel(sizes, h_table, hp, zp, *refs):
    n = len(h_table)
    pieces, slots = refs[:n], refs[n : n + sizes.cols - 1]
    zm, blocks = refs[n + sizes.cols - 1], refs[n + sizes.cols :]
    r, c, l = place()
    q, wide = sizes.quarter, blocks[0].shape[0]
    for h, (dr, dl) in zip(pieces, h_table):
        columns = slice(q, 2 * q) if dl else slice(0, q)
        block_col = (c * sizes.cols_here + (l ^ dl) * q) // BS
        for rr in range(sizes.rows):

            @pl.when((r ^ dr) == rr)
            def _(h=h, rr=rr, columns=columns, block_col=block_col):
                for first in range(0, sizes.rows_here, BS):
                    row = rr * sizes.rows_here + first
                    at = row % wide
                    blocks[row // wide][at : at + BS, columns] = keep_block(
                        hp, row // BS, block_col, h[first : first + BS, :]
                    )

    mask_kernel(sizes, zp, *slots, zm)


def first_kernel(sizes, top, zp, zm, last, *refs):
    cols, q = sizes.cols, sizes.quarter
    n, (out, zs) = len(refs) // 2 - 1, refs[-2:]
    sides, width = (refs[:n], refs[n : 2 * n]), refs[0].shape[0]
    r, c, l = place()
    cc = slot_column(c, cols - 1, cols)
    zs[...] = zm[...]
    zs[:, columns_of(cc, sizes)] = mask_piece(zp, r, l, cc, last[...], sizes)
    for side, blocks in zip((l, l ^ 1), sides):
        acc = None
        for n, block in enumerate(blocks):
            part = jnp.dot(
                zs[:, n * width : (n + 1) * width], block[...], preferred_element_type=jnp.float32
            )
            acc = part if acc is None else acc + part
        for n, ll in enumerate((side, side ^ top)):
            out[:, pl.ds(pl.multiple_of(ll * q, q), q)] = acc[:, n * q : (n + 1) * q].astype(
                out.dtype
            )


def route_kernel(sizes, row_offsets, *refs):
    n = len(row_offsets)
    pieces, outs, table = refs[:n], refs[n:-1], refs[-1]
    r, c, _ = place()
    q = sizes.quarter
    for dr, piece in zip(row_offsets, pieces):
        for half in range(sizes.per):
            start = pl.multiple_of(((r ^ dr) * sizes.per + half) * q, q)
            table[pl.ds(start, q), :] = piece[half * q : (half + 1) * q, :]
    for d, out in enumerate(outs):
        out[...] = table[pl.ds(pl.multiple_of((c ^ d) * q, q), q), :]


def split_kernel(*refs):
    pieces, outs = [], []
    for ref in refs:
        (pieces if ref.shape[0] > refs[-1].shape[0] else outs).append(ref)
    per, height = len(outs) // len(pieces), outs[0].shape[0]
    for n, out in enumerate(outs):
        first = n % per * height
        out[...] = pieces[n // per][first : first + height, :]


def layers_kernel(sizes, z_table, zp, *refs):
    cols, q = sizes.cols, sizes.quarter
    out, held = refs[-1], refs[:-1]
    r, c, l = place()
    for dl in range(sizes.layers):
        ll = l ^ dl
        for half in range(sizes.per):
            rows = pl.ds(strip_start(ll, half, sizes), q)
            for s in range(cols):
                cc = slot_column(c, s, cols)
                columns = columns_of(cc, sizes)
                if s and (dl, s) not in z_table:
                    out[rows, columns] = jnp.zeros((q, sizes.cols_here), out.dtype)
                    continue
                if s == 0:
                    strip = held[0][rows, :]
                else:
                    index, row = z_table[dl, s]
                    strip = held[index][row + half * q : row + (half + 1) * q, :]
                out[rows, columns] = mask_strip(zp, r, ll, half, cc, strip, sizes)


def turned_dot(left, right):
    return lax.dot_general(
        left, right, (((1,), (1,)), ((), ())), preferred_element_type=jnp.float32
    )


def second_kernel(sizes, part, z_full, *refs):
    messages, before, out = refs[: len(part)], refs[len(part) : -1], refs[-1]
    c = lax.axis_index("col")
    total = before[0][...] if before else None
    for d, message in zip(part, messages):
        added = turned_dot(z_full[:, columns_of(c ^ d, sizes)], message[...])
        total = added if total is None else total + added
    out[...] = total


def last_kernel(sizes, part, offsets, zp, z_full, before, *refs):
    cols, q, per = sizes.cols, sizes.quarter, sizes.per
    messages, piece, strips = refs[:cols], refs[cols], refs[cols + 1 : -3]
    out, acc, xm = refs[-3:]
    r, c, l = place()
    total = before[...]
    for d in part:
        total += turned_dot(z_full[:, columns_of(c ^ d, sizes)], messages[d][...])
    acc[...] = total
    cc = slot_column(c, cols - 1, cols)
    for d in range(cols):

        @pl.when((c ^ d) == cc)
        def _(d=d):
            xm[...] = messages[d][...]

    for n, dl in enumerate(offsets):
        for half in range(per):
            rows = pl.ds(strip_start(l ^ dl, half, sizes), q)
            strip = strips[half][...] if n else piece[half * q : (half + 1) * q, :]
            acc[rows, :] += turned_dot(mask_strip(zp, r, l ^ dl, half, cc, strip, sizes), xm[...])
    out[...] = acc[...].astype(out.dtype)


def local(sizes, hamiltonian, inv_root, h_pattern, z_pattern):
    rows, cols, layers, per = sizes.rows, sizes.cols, sizes.layers, sizes.per
    q, cols_here, rows_here = sizes.quarter, sizes.cols_here, sizes.rows_here
    order = rows * rows_here
    height = per * q
    row_bits, layer_bits = bits_of(rows), bits_of(layers)
    f32 = jnp.float32
    strip_shape = shape(q, cols_here)

    striped = inv_root.reshape(per, layers, q, cols_here)
    l = lax.axis_index("layer")
    own = lax.dynamic_index_in_dim(striped, l, 1, keepdims=False).reshape(height, cols_here)
    slots = [own]
    right = left = own
    for s in range(1, cols):
        if s % 2:
            right = lax.ppermute(right, "col", [(i, (i + 1) % cols) for i in range(cols)])
        else:
            left = lax.ppermute(left, "col", [(i, (i - 1) % cols) for i in range(cols)])
        slots.append(right if s % 2 else left)

    def cross(piece):
        return lax.ppermute(piece, "layer", flip(layers, layer_bits[0]))

    top, low = layer_bits
    h_pattern, z_pattern, fetched = run(
        fetch_kernel,
        "fetch",
        [shape(*h_pattern.shape, jnp.int32)] * 2 + [shape(*hamiltonian.shape)],
        [hamiltonian],
        smem=[h_pattern, z_pattern],
    )
    h_pieces, h_table = [hamiltonian], [(0, 0)]
    for axis, bit in [("layer", top)] + [("row", b) for b in row_bits]:
        perm = flip(rows if axis == "row" else layers, bit)
        for piece, (dr, dl) in list(zip(h_pieces, h_table)):
            h_table.append((dr ^ bit, dl) if axis == "row" else (dr, dl ^ bit))
            if axis == "row" and not dr and not dl:
                piece = fetched
            if dl and axis == 'row':
                piece = pack([piece], [slots[1]])
            h_pieces.append(lax.ppermute(piece, axis, perm))
    zm, *h_own = run(
        functools.partial(bring_kernel, sizes, h_table),
        "bring",
        [shape(height, order)] + [shape(cols_here, 2 * q)] * cols,
        [fetched, *h_pieces[1:], *slots[:-1]],
        smem=[h_pattern, z_pattern],
    )
    h_other = [lax.ppermute(block, "layer", flip(layers, low)) for block in h_own]
    product = run(
        functools.partial(first_kernel, sizes, top),
        "first_product",
        [shape(height, cols_here)],
        [zm, slots[-1], *h_own, *h_other],
        smem=[z_pattern],
        scratch=[pltpu.VMEM((height, order), jnp.bfloat16)],
    )[0]

    gathered = {0: product}
    for bit in row_bits:
        for dr, piece in list(gathered.items()):
            gathered[dr ^ bit] = lax.ppermute(piece, "row", flip(rows, bit))
    row_offsets = list(gathered)
    held, z_table = [inv_root], {}

    last = pack([slots[-1]], [product])
    last_top = cross(last)
    last_low = lax.ppermute(last, "layer", flip(layers, low))
    outgoing = run(
        functools.partial(route_kernel, sizes, row_offsets),
        "route",
        [shape(q, cols_here)] * cols,
        [gathered[o] for o in row_offsets],
        after=[last_low],
        scratch=[pltpu.VMEM((cols * q, cols_here), jnp.bfloat16)],
    )
    messages = [outgoing[0]] + [
        lax.ppermute(outgoing[d], "col", flip(cols, d)) for d in range(1, cols)
    ]
    group = range(1, cols - 1)
    mine = pack([slots[s] for s in group])
    other = cross(mine)
    both = lax.ppermute(pack([mine, other], [outgoing[0]]), "layer", flip(layers, low))
    held, z_table = [inv_root, mine, other, both, last, last_low], {}
    for n, s in enumerate(group):
        row = n * height
        z_table[0, s], z_table[top, s], z_table[low, s] = (1, row), (2, row), (3, row)
        z_table[low ^ top, s] = (3, len(group) * height + row)
    z_table[0, cols - 1], z_table[low, cols - 1] = (4, 0), (5, 0)
    parts = run(split_kernel, "split", [strip_shape] * per, [last_top])
    parts = [lax.ppermute(part, "layer", flip(layers, low)) for part in parts]
    z_full = run(
        functools.partial(layers_kernel, sizes, z_table),
        "layers",
        [shape(rows_here, order)],
        held,
        smem=[z_pattern],
    )[0]
    early, late = range(cols // 2), range(cols // 2, cols)
    total = run(
        functools.partial(second_kernel, sizes, early),
        "second_product",
        [shape(*hamiltonian.shape, f32)],
        [z_full, *[messages[d] for d in early]],
    )[0]
    return run(
        functools.partial(last_kernel, sizes, late, (top, low ^ top)),
        "last_product",
        [shape(*hamiltonian.shape)],
        [z_full, total, *messages, last_top, *parts],
        smem=[z_pattern],
        scratch=[pltpu.VMEM(hamiltonian.shape, f32), pltpu.VMEM((q, cols_here), jnp.bfloat16)],
    )[0]


def solution(mesh):
    rows, cols, layers = (mesh.shape[a] for a in ("row", "col", "layer"))

    def whole(hamiltonian, inv_root, h_pattern, z_pattern):
        order = hamiltonian.shape[0]
        cols_here = order // cols
        sizes = Sizes(
            rows, cols, layers, order // rows, cols_here, cols_here // layers, cols // rows
        )
        return jax.shard_map(
            functools.partial(local, sizes),
            mesh=mesh,
            in_specs=(P("row", ("col", "layer")), P("row", "col"), P(), P()),
            out_specs=P("row", ("col", "layer")),
            check_vma=False,
        )(hamiltonian, inv_root, h_pattern, z_pattern)

    return whole
```

```python
import functools
from typing import NamedTuple

import jax
import jax.numpy as jnp
from jax import lax
from jax.experimental import pallas as pl
from jax.experimental.pallas import tpu as pltpu
from jax.sharding import PartitionSpec as P

BS = 256
MARGIN = 4 * 1024 * 1024


class Sizes(NamedTuple):
    rows: int
    cols: int
    layers: int
    rows_here: int
    cols_here: int
    quarter: int
    per: int


def bits_of(size):
    return [1 << b for b in reversed(range(size.bit_length() - 1))]


def flip(size, bit):
    return [(i, i ^ bit) for i in range(size)]


def mod(a, n):
    return lax.rem(a + n, n)


def place():
    return lax.axis_index("row"), lax.axis_index("col"), lax.axis_index("layer")


def run(kernel, name, outs, arrays, smem=(), after=(), scratch=(), flops=0):
    size = sum(a.size * a.dtype.itemsize for a in arrays)
    size += sum(o.size * o.dtype.itemsize for o in outs)
    for kept in scratch:
        size += kept.shape[0] * kept.shape[1] * jnp.dtype(kept.dtype).itemsize
    skip = len(smem) + len(arrays)

    def body(*refs):
        kernel(*refs[:skip], *refs[skip + len(after) :])

    return pl.pallas_call(
        body,
        out_shape=list(outs),
        in_specs=[pl.BlockSpec(memory_space=pltpu.SMEM)] * len(smem)
        + [pl.BlockSpec(memory_space=pltpu.VMEM)] * len(arrays)
        + [pl.BlockSpec(memory_space=pl.ANY)] * len(after),
        out_specs=[
            pl.BlockSpec(memory_space=pltpu.SMEM if o.dtype == jnp.int32 else pltpu.VMEM)
            for o in outs
        ],
        scratch_shapes=list(scratch),
        compiler_params=pltpu.CompilerParams(vmem_limit_bytes=size + MARGIN),
        cost_estimate=pl.CostEstimate(flops=flops, bytes_accessed=size, transcendentals=0),
        name=name,
    )(*smem, *arrays, *after)


def shape(rows, columns, dtype=jnp.bfloat16):
    return jax.ShapeDtypeStruct((rows, columns), dtype)


def keep_block(pattern, i, j, block):
    return jnp.where(pattern[i, j] > 0, block, jnp.zeros_like(block))


def strip_start(l, half, sizes):
    return pl.multiple_of(half * sizes.cols_here + l * sizes.quarter, sizes.quarter)


def columns_of(cc, sizes):
    return pl.ds(pl.multiple_of(cc * sizes.cols_here, sizes.cols_here), sizes.cols_here)


def mask_strip(zp, r, l, half, cc, strip, sizes):
    block_row = (r * sizes.rows_here + half * sizes.cols_here + l * sizes.quarter) // BS
    first = cc * (sizes.cols_here // BS)
    return jnp.concatenate(
        [
            keep_block(zp, block_row, first + t, strip[:, t * BS : (t + 1) * BS])
            for t in range(sizes.cols_here // BS)
        ],
        axis=1,
    )


def mask_piece(zp, r, l, cc, piece, sizes):
    q = sizes.quarter
    return jnp.concatenate(
        [
            mask_strip(zp, r, l, half, cc, piece[half * q : (half + 1) * q, :], sizes)
            for half in range(sizes.per)
        ],
        axis=0,
    )


def pack_kernel(*refs):
    out, row = refs[-1], 0
    for ref in refs[:-1]:
        out[row : row + ref.shape[0], :] = ref[...]
        row += ref.shape[0]


def pack(pieces, after=()):
    height = sum(p.shape[0] for p in pieces)
    out = shape(height, pieces[0].shape[1])
    return run(pack_kernel, "pack", [out], pieces, after=after)[0]


def slot_column(c, s, cols):
    return mod(c - (s + 1) // 2 if s % 2 else c + s // 2, cols)


def mask_kernel(sizes, zp, *refs):
    slots, out = refs[:-1], refs[-1]
    r, c, l = place()
    out[...] = jnp.zeros_like(out)
    for s, slot in enumerate(slots):
        cc = slot_column(c, s, sizes.cols)
        out[:, columns_of(cc, sizes)] = mask_piece(zp, r, l, cc, slot[...], sizes)


def fetch_kernel(hp, zp, h, hp_out, zp_out, h_out):
    h_out[...] = h[...]
    for i in range(hp.shape[0]):
        for j in range(hp.shape[1]):
            hp_out[i, j] = hp[i, j]
            zp_out[i, j] = zp[i, j]


def bring_kernel(sizes, h_table, hp, zp, *refs):
    n = len(h_table)
    pieces, slots = refs[:n], refs[n : n + sizes.cols - 1]
    zm, blocks = refs[n + sizes.cols - 1], refs[n + sizes.cols :]
    r, c, l = place()
    q, wide = sizes.quarter, blocks[0].shape[0]
    for h, (dr, dl) in zip(pieces, h_table):
        columns = slice(q, 2 * q) if dl else slice(0, q)
        block_col = (c * sizes.cols_here + (l ^ dl) * q) // BS
        for rr in range(sizes.rows):

            @pl.when((r ^ dr) == rr)
            def _(h=h, rr=rr, columns=columns, block_col=block_col):
                for first in range(0, sizes.rows_here, BS):
                    row = rr * sizes.rows_here + first
                    at = row % wide
                    blocks[row // wide][at : at + BS, columns] = keep_block(
                        hp, row // BS, block_col, h[first : first + BS, :]
                    )

    mask_kernel(sizes, zp, *slots, zm)


def first_kernel(sizes, top, zp, zm, last, *refs):
    cols, q = sizes.cols, sizes.quarter
    n, (out, zs) = len(refs) // 2 - 1, refs[-2:]
    sides, width = (refs[:n], refs[n : 2 * n]), refs[0].shape[0]
    r, c, l = place()
    cc = slot_column(c, cols - 1, cols)
    zs[...] = zm[...]
    zs[:, columns_of(cc, sizes)] = mask_piece(zp, r, l, cc, last[...], sizes)
    for side, blocks in zip((l, l ^ 1), sides):
        acc = None
        for n, block in enumerate(blocks):
            part = jnp.dot(
                zs[:, n * width : (n + 1) * width], block[...], preferred_element_type=jnp.float32
            )
            acc = part if acc is None else acc + part
        for n, ll in enumerate((side, side ^ top)):
            out[:, pl.ds(pl.multiple_of(ll * q, q), q)] = acc[:, n * q : (n + 1) * q].astype(
                out.dtype
            )


def route_kernel(sizes, row_offsets, *refs):
    table, (r, _, _), q = refs[-1], place(), sizes.quarter
    for dr, piece in zip(row_offsets, refs[:-1]):
        for half in range(sizes.per):
            start = pl.multiple_of(((r ^ dr) * sizes.per + half) * q, q)
            table[pl.ds(start, q), :] = piece[half * q : (half + 1) * q, :]


def layers_kernel(sizes, z_table, zp, *refs):
    cols, q = sizes.cols, sizes.quarter
    out, held = refs[-1], refs[:-1]
    r, c, l = place()
    for dl in range(sizes.layers):
        ll = l ^ dl
        for half in range(sizes.per):
            rows = pl.ds(strip_start(ll, half, sizes), q)
            for s in range(cols):
                cc = slot_column(c, s, cols)
                if s == 0:
                    strip = held[0][rows, :]
                else:
                    index, row = z_table[dl, s]
                    strip = held[index][row + half * q : row + (half + 1) * q, :]
                out[rows, columns_of(cc, sizes)] = mask_strip(zp, r, ll, half, cc, strip, sizes)


def second_kernel(sizes, part, z_full, messages, *refs):
    before, out = refs[:-1], refs[-1]
    q, c = sizes.quarter, lax.axis_index("col")
    total = before[0][...] if before else None
    for d in part:
        cc = c ^ d
        added = lax.dot_general(
            z_full[:, columns_of(cc, sizes)],
            messages[pl.ds(pl.multiple_of(cc * q, q), q), :],
            (((1,), (1,)), ((), ())),
            preferred_element_type=jnp.float32,
        )
        total = added if total is None else total + added
    out[...] = total.astype(out.dtype)


def local(sizes, hamiltonian, inv_root, h_pattern, z_pattern):
    rows, cols, layers, per = sizes.rows, sizes.cols, sizes.layers, sizes.per
    q, cols_here, rows_here = sizes.quarter, sizes.cols_here, sizes.rows_here
    order = rows * rows_here
    height = per * q
    row_bits, layer_bits = bits_of(rows), bits_of(layers)
    f32 = jnp.float32
    strip_shape = shape(q, cols_here)

    striped = inv_root.reshape(per, layers, q, cols_here)
    l = lax.axis_index("layer")
    own = lax.dynamic_index_in_dim(striped, l, 1, keepdims=False).reshape(height, cols_here)
    slots = [own]
    right = left = own
    for s in range(1, cols):
        if s % 2:
            right = lax.ppermute(right, "col", [(i, (i + 1) % cols) for i in range(cols)])
        else:
            left = lax.ppermute(left, "col", [(i, (i - 1) % cols) for i in range(cols)])
        slots.append(right if s % 2 else left)

    def cross(piece):
        return lax.ppermute(piece, "layer", flip(layers, layer_bits[0]))

    top, low = layer_bits
    h_pattern, z_pattern, fetched = run(
        fetch_kernel,
        "fetch",
        [shape(*h_pattern.shape, jnp.int32)] * 2 + [shape(*hamiltonian.shape)],
        [hamiltonian],
        smem=[h_pattern, z_pattern],
    )
    h_pieces, h_table = [hamiltonian], [(0, 0)]
    for axis, bit in [("layer", top)] + [("row", b) for b in row_bits]:
        perm = flip(rows if axis == "row" else layers, bit)
        for piece, (dr, dl) in list(zip(h_pieces, h_table)):
            h_table.append((dr ^ bit, dl) if axis == "row" else (dr, dl ^ bit))
            if dl and axis == 'row':
                piece = pack([piece], [slots[1]])
            h_pieces.append(lax.ppermute(piece, axis, perm))
    zm, *h_own = run(
        functools.partial(bring_kernel, sizes, h_table),
        "bring",
        [shape(height, order)] + [shape(cols_here, 2 * q)] * cols,
        [fetched, *h_pieces[1:], *slots[:-1]],
        smem=[h_pattern, z_pattern],
    )
    h_other = [lax.ppermute(block, "layer", flip(layers, low)) for block in h_own]
    product = run(
        functools.partial(first_kernel, sizes, top),
        "first_product",
        [shape(height, cols_here)],
        [zm, slots[-1], *h_own, *h_other],
        smem=[z_pattern],
        scratch=[pltpu.VMEM((height, order), jnp.bfloat16)],
    )[0]

    gathered = {0: product}
    for bit in row_bits:
        for dr, piece in list(gathered.items()):
            gathered[dr ^ bit] = lax.ppermute(piece, "row", flip(rows, bit))
    row_offsets = list(gathered)
    table = run(
        functools.partial(route_kernel, sizes, row_offsets),
        "route",
        [shape(cols * q, cols_here)],
        [gathered[o] for o in row_offsets],
    )[0]
    messages = lax.all_to_all(table, "col", 0, 0, tiled=True)

    held, z_table = [inv_root], {}
    for group, gates in ((range(1, cols - 1), [[], [table]]), ([cols - 1], [[product], []])):
        mine = pack([slots[s] for s in group], gates[0])
        other = cross(mine)
        both = lax.ppermute(pack([mine, other], gates[1]), "layer", flip(layers, low))
        base = len(held)
        held += [mine, other, both]
        for n, s in enumerate(group):
            row = n * height
            z_table[0, s], z_table[top, s] = (base, row), (base + 1, row)
            z_table[low, s] = (base + 2, row)
            z_table[low ^ top, s] = (base + 2, len(group) * height + row)
    z_full = run(
        functools.partial(layers_kernel, sizes, z_table),
        "layers",
        [shape(rows_here, order)],
        held,
        smem=[z_pattern],
    )[0]
    total = run(
        functools.partial(second_kernel, sizes, (0,)),
        "second_product",
        [shape(*hamiltonian.shape, f32)],
        [z_full, table],
    )
    return run(
        functools.partial(second_kernel, sizes, range(1, cols)),
        "second_product",
        [shape(*hamiltonian.shape)],
        [z_full, messages, *total],
    )[0]


def solution(mesh):
    rows, cols, layers = (mesh.shape[a] for a in ("row", "col", "layer"))

    def whole(hamiltonian, inv_root, h_pattern, z_pattern):
        order = hamiltonian.shape[0]
        cols_here = order // cols
        sizes = Sizes(
            rows, cols, layers, order // rows, cols_here, cols_here // layers, cols // rows
        )
        return jax.shard_map(
            functools.partial(local, sizes),
            mesh=mesh,
            in_specs=(P("row", ("col", "layer")), P("row", "col"), P(), P()),
            out_specs=P("row", ("col", "layer")),
            check_vma=False,
        )(hamiltonian, inv_root, h_pattern, z_pattern)

    return whole
```

```python
import functools
from typing import NamedTuple

import jax
import jax.numpy as jnp
from jax import lax
from jax.experimental import pallas as pl
from jax.experimental.pallas import tpu as pltpu
from jax.sharding import PartitionSpec as P

BS = 256
MARGIN = 4 * 1024 * 1024


class Sizes(NamedTuple):
    rows: int
    cols: int
    layers: int
    rows_here: int
    cols_here: int
    quarter: int
    per: int


def bits_of(size):
    return [1 << b for b in reversed(range(size.bit_length() - 1))]


def flip(size, bit):
    return [(i, i ^ bit) for i in range(size)]


def mod(a, n):
    return lax.rem(a + n, n)


def place():
    return lax.axis_index("row"), lax.axis_index("col"), lax.axis_index("layer")


def run(kernel, name, outs, arrays, smem=(), after=(), scratch=(), flops=0):
    size = sum(a.size * a.dtype.itemsize for a in arrays)
    size += sum(o.size * o.dtype.itemsize for o in outs)
    for kept in scratch:
        size += kept.shape[0] * kept.shape[1] * jnp.dtype(kept.dtype).itemsize
    skip = len(smem) + len(arrays)

    def body(*refs):
        kernel(*refs[:skip], *refs[skip + len(after) :])

    return pl.pallas_call(
        body,
        out_shape=list(outs),
        in_specs=[pl.BlockSpec(memory_space=pltpu.SMEM)] * len(smem)
        + [pl.BlockSpec(memory_space=pltpu.VMEM)] * len(arrays)
        + [pl.BlockSpec(memory_space=pl.ANY)] * len(after),
        out_specs=[
            pl.BlockSpec(memory_space=pltpu.SMEM if o.dtype == jnp.int32 else pltpu.VMEM)
            for o in outs
        ],
        scratch_shapes=list(scratch),
        compiler_params=pltpu.CompilerParams(vmem_limit_bytes=size + MARGIN),
        cost_estimate=pl.CostEstimate(flops=flops, bytes_accessed=size, transcendentals=0),
        name=name,
    )(*smem, *arrays, *after)


def shape(rows, columns, dtype=jnp.bfloat16):
    return jax.ShapeDtypeStruct((rows, columns), dtype)


def keep_block(pattern, i, j, block):
    return jnp.where(pattern[i, j] > 0, block, jnp.zeros_like(block))


def strip_start(l, half, sizes):
    return pl.multiple_of(half * sizes.cols_here + l * sizes.quarter, sizes.quarter)


def columns_of(cc, sizes):
    return pl.ds(pl.multiple_of(cc * sizes.cols_here, sizes.cols_here), sizes.cols_here)


def mask_strip(zp, r, l, half, cc, strip, sizes):
    block_row = (r * sizes.rows_here + half * sizes.cols_here + l * sizes.quarter) // BS
    first = cc * (sizes.cols_here // BS)
    return jnp.concatenate(
        [
            keep_block(zp, block_row, first + t, strip[:, t * BS : (t + 1) * BS])
            for t in range(sizes.cols_here // BS)
        ],
        axis=1,
    )


def mask_piece(zp, r, l, cc, piece, sizes):
    q = sizes.quarter
    return jnp.concatenate(
        [
            mask_strip(zp, r, l, half, cc, piece[half * q : (half + 1) * q, :], sizes)
            for half in range(sizes.per)
        ],
        axis=0,
    )


def pack_kernel(*refs):
    out, row = refs[-1], 0
    for ref in refs[:-1]:
        out[row : row + ref.shape[0], :] = ref[...]
        row += ref.shape[0]


def pack(pieces, after=()):
    height = sum(p.shape[0] for p in pieces)
    out = shape(height, pieces[0].shape[1])
    return run(pack_kernel, "pack", [out], pieces, after=after)[0]


def slot_column(c, s, cols):
    return mod(c - (s + 1) // 2 if s % 2 else c + s // 2, cols)


def mask_kernel(sizes, zp, *refs):
    slots, out = refs[:-1], refs[-1]
    r, c, l = place()
    out[...] = jnp.zeros_like(out)
    for s, slot in enumerate(slots):
        cc = slot_column(c, s, sizes.cols)
        out[:, columns_of(cc, sizes)] = mask_piece(zp, r, l, cc, slot[...], sizes)


def fetch_kernel(hp, zp, h, hp_out, zp_out, h_out):
    h_out[...] = h[...]
    for i in range(hp.shape[0]):
        for j in range(hp.shape[1]):
            hp_out[i, j] = hp[i, j]
            zp_out[i, j] = zp[i, j]


def bring_kernel(sizes, h_table, hp, zp, *refs):
    n = len(h_table)
    pieces, slots = refs[:n], refs[n : n + sizes.cols - 1]
    zm, blocks = refs[n + sizes.cols - 1], refs[n + sizes.cols :]
    r, c, l = place()
    q, wide = sizes.quarter, blocks[0].shape[0]
    for h, (dr, dl) in zip(pieces, h_table):
        columns = slice(q, 2 * q) if dl else slice(0, q)
        block_col = (c * sizes.cols_here + (l ^ dl) * q) // BS
        for rr in range(sizes.rows):

            @pl.when((r ^ dr) == rr)
            def _(h=h, rr=rr, columns=columns, block_col=block_col):
                for first in range(0, sizes.rows_here, BS):
                    row = rr * sizes.rows_here + first
                    at = row % wide
                    blocks[row // wide][at : at + BS, columns] = keep_block(
                        hp, row // BS, block_col, h[first : first + BS, :]
                    )

    mask_kernel(sizes, zp, *slots, zm)


def first_kernel(sizes, top, zp, zm, last, *refs):
    cols, q = sizes.cols, sizes.quarter
    n, (out, zs) = len(refs) // 2 - 1, refs[-2:]
    sides, width = (refs[:n], refs[n : 2 * n]), refs[0].shape[0]
    r, c, l = place()
    cc = slot_column(c, cols - 1, cols)
    zs[...] = zm[...]
    zs[:, columns_of(cc, sizes)] = mask_piece(zp, r, l, cc, last[...], sizes)
    for side, blocks in zip((l, l ^ 1), sides):
        acc = None
        for n, block in enumerate(blocks):
            part = jnp.dot(
                zs[:, n * width : (n + 1) * width], block[...], preferred_element_type=jnp.float32
            )
            acc = part if acc is None else acc + part
        for n, ll in enumerate((side, side ^ top)):
            out[:, pl.ds(pl.multiple_of(ll * q, q), q)] = acc[:, n * q : (n + 1) * q].astype(
                out.dtype
            )


def route_kernel(sizes, row_offsets, *refs):
    n = len(row_offsets)
    pieces, outs, table = refs[:n], refs[n:-1], refs[-1]
    r, c, _ = place()
    q = sizes.quarter
    for dr, piece in zip(row_offsets, pieces):
        for half in range(sizes.per):
            start = pl.multiple_of(((r ^ dr) * sizes.per + half) * q, q)
            table[pl.ds(start, q), :] = piece[half * q : (half + 1) * q, :]
    for d, out in enumerate(outs):
        out[...] = table[pl.ds(pl.multiple_of((c ^ d) * q, q), q), :]


def split_kernel(*refs):
    pieces, outs = [], []
    for ref in refs:
        (pieces if ref.shape[0] > refs[-1].shape[0] else outs).append(ref)
    per, height = len(outs) // len(pieces), outs[0].shape[0]
    for n, out in enumerate(outs):
        first = n % per * height
        out[...] = pieces[n // per][first : first + height, :]


def layers_kernel(sizes, z_table, zp, *refs):
    cols, q = sizes.cols, sizes.quarter
    out, held = refs[-1], refs[:-1]
    r, c, l = place()
    for dl in range(sizes.layers):
        ll = l ^ dl
        for half in range(sizes.per):
            rows = pl.ds(strip_start(ll, half, sizes), q)
            for s in range(cols):
                cc = slot_column(c, s, cols)
                columns = columns_of(cc, sizes)
                if s and (dl, s) not in z_table:
                    out[rows, columns] = jnp.zeros((q, sizes.cols_here), out.dtype)
                    continue
                if s == 0:
                    strip = held[0][rows, :]
                else:
                    index, row = z_table[dl, s]
                    strip = held[index][row + half * q : row + (half + 1) * q, :]
                out[rows, columns] = mask_strip(zp, r, ll, half, cc, strip, sizes)


def turned_dot(left, right):
    return lax.dot_general(
        left, right, (((1,), (1,)), ((), ())), preferred_element_type=jnp.float32
    )


def second_kernel(sizes, part, z_full, *refs):
    messages, before, out = refs[: len(part)], refs[len(part) : -1], refs[-1]
    c = lax.axis_index("col")
    total = before[0][...] if before else None
    for d, message in zip(part, messages):
        added = turned_dot(z_full[:, columns_of(c ^ d, sizes)], message[...])
        total = added if total is None else total + added
    out[...] = total


def last_kernel(sizes, part, dl, zp, z_full, before, *refs):
    cols, q = sizes.cols, sizes.quarter
    messages, strips = refs[:cols], refs[cols:-3]
    out, acc, xm = refs[-3:]
    r, c, l = place()
    total = before[...]
    for d in part:
        total += turned_dot(z_full[:, columns_of(c ^ d, sizes)], messages[d][...])
    acc[...] = total
    out[...] = total.astype(out.dtype)
    cc = slot_column(c, cols - 1, cols)
    for d in range(cols):

        @pl.when((c ^ d) == cc)
        def _(d=d):
            xm[...] = messages[d][...]

    masked = [mask_strip(zp, r, l ^ dl, n, cc, strip[...], sizes) for n, strip in enumerate(strips)]
    added = turned_dot(jnp.concatenate(masked, axis=0), xm[...])
    for n in range(len(strips)):
        rows = pl.ds(strip_start(l ^ dl, n, sizes), q)
        out[rows, :] = (acc[rows, :] + added[n * q : (n + 1) * q, :]).astype(out.dtype)


def local(sizes, hamiltonian, inv_root, h_pattern, z_pattern):
    rows, cols, layers, per = sizes.rows, sizes.cols, sizes.layers, sizes.per
    q, cols_here, rows_here = sizes.quarter, sizes.cols_here, sizes.rows_here
    order = rows * rows_here
    height = per * q
    row_bits, layer_bits = bits_of(rows), bits_of(layers)
    f32 = jnp.float32
    strip_shape = shape(q, cols_here)

    striped = inv_root.reshape(per, layers, q, cols_here)
    l = lax.axis_index("layer")
    own = lax.dynamic_index_in_dim(striped, l, 1, keepdims=False).reshape(height, cols_here)
    slots = [own]
    right = left = own
    for s in range(1, cols):
        if s % 2:
            right = lax.ppermute(right, "col", [(i, (i + 1) % cols) for i in range(cols)])
        else:
            left = lax.ppermute(left, "col", [(i, (i - 1) % cols) for i in range(cols)])
        slots.append(right if s % 2 else left)

    def cross(piece):
        return lax.ppermute(piece, "layer", flip(layers, layer_bits[0]))

    top, low = layer_bits
    h_pattern, z_pattern, fetched = run(
        fetch_kernel,
        "fetch",
        [shape(*h_pattern.shape, jnp.int32)] * 2 + [shape(*hamiltonian.shape)],
        [hamiltonian],
        smem=[h_pattern, z_pattern],
    )
    h_pieces, h_table = [hamiltonian], [(0, 0)]
    for axis, bit in [("layer", top)] + [("row", b) for b in row_bits]:
        perm = flip(rows if axis == "row" else layers, bit)
        for piece, (dr, dl) in list(zip(h_pieces, h_table)):
            h_table.append((dr ^ bit, dl) if axis == "row" else (dr, dl ^ bit))
            if dl and axis == 'row':
                piece = pack([piece], [slots[1]])
            h_pieces.append(lax.ppermute(piece, axis, perm))
    zm, *h_own = run(
        functools.partial(bring_kernel, sizes, h_table),
        "bring",
        [shape(height, order)] + [shape(cols_here, 2 * q)] * cols,
        [fetched, *h_pieces[1:], *slots[:-1]],
        smem=[h_pattern, z_pattern],
    )
    h_other = [lax.ppermute(block, "layer", flip(layers, low)) for block in h_own]
    product = run(
        functools.partial(first_kernel, sizes, top),
        "first_product",
        [shape(height, cols_here)],
        [zm, slots[-1], *h_own, *h_other],
        smem=[z_pattern],
        scratch=[pltpu.VMEM((height, order), jnp.bfloat16)],
    )[0]

    gathered = {0: product}
    for bit in row_bits:
        for dr, piece in list(gathered.items()):
            gathered[dr ^ bit] = lax.ppermute(piece, "row", flip(rows, bit))
    row_offsets = list(gathered)
    held, z_table = [inv_root], {}

    last = pack([slots[-1]], [product])
    last_top = cross(last)
    last_low = lax.ppermute(last, "layer", flip(layers, low))
    outgoing = run(
        functools.partial(route_kernel, sizes, row_offsets),
        "route",
        [shape(q, cols_here)] * cols,
        [gathered[o] for o in row_offsets],
        after=[last_low],
        scratch=[pltpu.VMEM((cols * q, cols_here), jnp.bfloat16)],
    )
    messages = [outgoing[0]] + [
        lax.ppermute(outgoing[d], "col", flip(cols, d)) for d in range(1, cols)
    ]
    group = range(1, cols - 1)
    mine = pack([slots[s] for s in group])
    other = cross(mine)
    both = lax.ppermute(pack([mine, other], [outgoing[0]]), "layer", flip(layers, low))
    held, z_table = [inv_root, mine, other, both, last, last_low, last_top], {}
    for n, s in enumerate(group):
        row = n * height
        z_table[0, s], z_table[top, s], z_table[low, s] = (1, row), (2, row), (3, row)
        z_table[low ^ top, s] = (3, len(group) * height + row)
    for n, dl in enumerate((0, low, top)):
        z_table[dl, cols - 1] = (4 + n, 0)
    parts = run(split_kernel, "split", [strip_shape] * per, [last_top])
    parts = [lax.ppermute(part, "layer", flip(layers, low)) for part in parts]
    z_full = run(
        functools.partial(layers_kernel, sizes, z_table),
        "layers",
        [shape(rows_here, order)],
        held,
        smem=[z_pattern],
    )[0]
    early, late = range(cols // 2), range(cols // 2, cols)
    total = run(
        functools.partial(second_kernel, sizes, early),
        "second_product",
        [shape(*hamiltonian.shape, f32)],
        [z_full, *[messages[d] for d in early]],
    )[0]
    return run(
        functools.partial(last_kernel, sizes, late, low ^ top),
        "last_product",
        [shape(*hamiltonian.shape)],
        [z_full, total, *messages, *parts],
        smem=[z_pattern],
        scratch=[pltpu.VMEM(hamiltonian.shape, f32), pltpu.VMEM((q, cols_here), jnp.bfloat16)],
    )[0]


def solution(mesh):
    rows, cols, layers = (mesh.shape[a] for a in ("row", "col", "layer"))

    def whole(hamiltonian, inv_root, h_pattern, z_pattern):
        order = hamiltonian.shape[0]
        cols_here = order // cols
        sizes = Sizes(
            rows, cols, layers, order // rows, cols_here, cols_here // layers, cols // rows
        )
        return jax.shard_map(
            functools.partial(local, sizes),
            mesh=mesh,
            in_specs=(P("row", ("col", "layer")), P("row", "col"), P(), P()),
            out_specs=P("row", ("col", "layer")),
            check_vma=False,
        )(hamiltonian, inv_root, h_pattern, z_pattern)

    return whole
```

```python
import functools
from typing import NamedTuple

import jax
import jax.numpy as jnp
from jax import lax
from jax.experimental import pallas as pl
from jax.experimental.pallas import tpu as pltpu
from jax.sharding import PartitionSpec as P

BS = 256
MARGIN = 4 * 1024 * 1024


class Sizes(NamedTuple):
    rows: int
    cols: int
    layers: int
    rows_here: int
    cols_here: int
    quarter: int
    per: int


def bits_of(size):
    return [1 << b for b in reversed(range(size.bit_length() - 1))]


def flip(size, bit):
    return [(i, i ^ bit) for i in range(size)]


def mod(a, n):
    return lax.rem(a + n, n)


def place():
    return lax.axis_index("row"), lax.axis_index("col"), lax.axis_index("layer")


def run(kernel, name, outs, arrays, smem=(), after=(), scratch=(), flops=0):
    size = sum(a.size * a.dtype.itemsize for a in arrays)
    size += sum(o.size * o.dtype.itemsize for o in outs)
    for kept in scratch:
        size += kept.shape[0] * kept.shape[1] * jnp.dtype(kept.dtype).itemsize
    skip = len(smem) + len(arrays)

    def body(*refs):
        kernel(*refs[:skip], *refs[skip + len(after) :])

    return pl.pallas_call(
        body,
        out_shape=list(outs),
        in_specs=[pl.BlockSpec(memory_space=pltpu.SMEM)] * len(smem)
        + [pl.BlockSpec(memory_space=pltpu.VMEM)] * len(arrays)
        + [pl.BlockSpec(memory_space=pl.ANY)] * len(after),
        out_specs=[
            pl.BlockSpec(memory_space=pltpu.SMEM if o.dtype == jnp.int32 else pltpu.VMEM)
            for o in outs
        ],
        scratch_shapes=list(scratch),
        compiler_params=pltpu.CompilerParams(vmem_limit_bytes=size + MARGIN),
        cost_estimate=pl.CostEstimate(flops=flops, bytes_accessed=size, transcendentals=0),
        name=name,
    )(*smem, *arrays, *after)


def shape(rows, columns, dtype=jnp.bfloat16):
    return jax.ShapeDtypeStruct((rows, columns), dtype)


def keep_block(pattern, i, j, block):
    return jnp.where(pattern[i, j] > 0, block, jnp.zeros_like(block))


def strip_start(l, half, sizes):
    return pl.multiple_of(half * sizes.cols_here + l * sizes.quarter, sizes.quarter)


def columns_of(cc, sizes):
    return pl.ds(pl.multiple_of(cc * sizes.cols_here, sizes.cols_here), sizes.cols_here)


def mask_strip(zp, r, l, half, cc, strip, sizes):
    block_row = (r * sizes.rows_here + half * sizes.cols_here + l * sizes.quarter) // BS
    first = cc * (sizes.cols_here // BS)
    return jnp.concatenate(
        [
            keep_block(zp, block_row, first + t, strip[:, t * BS : (t + 1) * BS])
            for t in range(sizes.cols_here // BS)
        ],
        axis=1,
    )


def mask_piece(zp, r, l, cc, piece, sizes):
    q = sizes.quarter
    return jnp.concatenate(
        [
            mask_strip(zp, r, l, half, cc, piece[half * q : (half + 1) * q, :], sizes)
            for half in range(sizes.per)
        ],
        axis=0,
    )


def pack_kernel(*refs):
    out, row = refs[-1], 0
    for ref in refs[:-1]:
        out[row : row + ref.shape[0], :] = ref[...]
        row += ref.shape[0]


def pack(pieces, after=()):
    height = sum(p.shape[0] for p in pieces)
    out = shape(height, pieces[0].shape[1])
    return run(pack_kernel, "pack", [out], pieces, after=after)[0]


def slot_column(c, s, cols):
    return mod(c - (s + 1) // 2 if s % 2 else c + s // 2, cols)


def mask_kernel(sizes, zp, *refs):
    slots, out = refs[:-1], refs[-1]
    r, c, l = place()
    out[...] = jnp.zeros_like(out)
    for s, slot in enumerate(slots):
        cc = slot_column(c, s, sizes.cols)
        out[:, columns_of(cc, sizes)] = mask_piece(zp, r, l, cc, slot[...], sizes)


def fetch_kernel(hp, zp, h, hp_out, zp_out, h_out):
    h_out[...] = h[...]
    for i in range(hp.shape[0]):
        for j in range(hp.shape[1]):
            hp_out[i, j] = hp[i, j]
            zp_out[i, j] = zp[i, j]


def bring_kernel(sizes, h_table, hp, zp, *refs):
    n = len(h_table)
    pieces, slots = refs[:n], refs[n : n + sizes.cols - 1]
    zm, blocks = refs[n + sizes.cols - 1], refs[n + sizes.cols :]
    r, c, l = place()
    q, wide = sizes.quarter, blocks[0].shape[0]
    for h, (dr, dl) in zip(pieces, h_table):
        columns = slice(q, 2 * q) if dl else slice(0, q)
        block_col = (c * sizes.cols_here + (l ^ dl) * q) // BS
        for rr in range(sizes.rows):

            @pl.when((r ^ dr) == rr)
            def _(h=h, rr=rr, columns=columns, block_col=block_col):
                for first in range(0, sizes.rows_here, BS):
                    row = rr * sizes.rows_here + first
                    at = row % wide
                    blocks[row // wide][at : at + BS, columns] = keep_block(
                        hp, row // BS, block_col, h[first : first + BS, :]
                    )

    mask_kernel(sizes, zp, *slots, zm)


def first_kernel(sizes, top, zp, zm, last, *refs):
    cols, q = sizes.cols, sizes.quarter
    n, (out, zs) = len(refs) // 2 - 1, refs[-2:]
    sides, width = (refs[:n], refs[n : 2 * n]), refs[0].shape[0]
    r, c, l = place()
    cc = slot_column(c, cols - 1, cols)
    zs[...] = zm[...]
    zs[:, columns_of(cc, sizes)] = mask_piece(zp, r, l, cc, last[...], sizes)
    for side, blocks in zip((l, l ^ 1), sides):
        acc = None
        for n, block in enumerate(blocks):
            part = jnp.dot(
                zs[:, n * width : (n + 1) * width], block[...], preferred_element_type=jnp.float32
            )
            acc = part if acc is None else acc + part
        for n, ll in enumerate((side, side ^ top)):
            out[:, pl.ds(pl.multiple_of(ll * q, q), q)] = acc[:, n * q : (n + 1) * q].astype(
                out.dtype
            )


def route_kernel(sizes, row_offsets, *refs):
    n = len(row_offsets)
    pieces, outs, table = refs[:n], refs[n:-1], refs[-1]
    r, c, _ = place()
    q = sizes.quarter
    for dr, piece in zip(row_offsets, pieces):
        for half in range(sizes.per):
            start = pl.multiple_of(((r ^ dr) * sizes.per + half) * q, q)
            table[pl.ds(start, q), :] = piece[half * q : (half + 1) * q, :]
    for d, out in enumerate(outs):
        out[...] = table[pl.ds(pl.multiple_of((c ^ d) * q, q), q), :]


def split_kernel(*refs):
    pieces, outs = [], []
    for ref in refs:
        (pieces if ref.shape[0] > refs[-1].shape[0] else outs).append(ref)
    per, height = len(outs) // len(pieces), outs[0].shape[0]
    for n, out in enumerate(outs):
        first = n % per * height
        out[...] = pieces[n // per][first : first + height, :]


def layers_kernel(sizes, z_table, zp, *refs):
    cols, q = sizes.cols, sizes.quarter
    out, held = refs[-1], refs[:-1]
    r, c, l = place()
    for dl in range(sizes.layers):
        ll = l ^ dl
        for half in range(sizes.per):
            rows = pl.ds(strip_start(ll, half, sizes), q)
            for s in range(cols):
                cc = slot_column(c, s, cols)
                columns = columns_of(cc, sizes)
                if s and (dl, s) not in z_table:
                    out[rows, columns] = jnp.zeros((q, sizes.cols_here), out.dtype)
                    continue
                if s == 0:
                    strip = held[0][rows, :]
                else:
                    index, row = z_table[dl, s]
                    strip = held[index][row + half * q : row + (half + 1) * q, :]
                out[rows, columns] = mask_strip(zp, r, ll, half, cc, strip, sizes)


def turned_dot(left, right):
    return lax.dot_general(
        left, right, (((1,), (1,)), ((), ())), preferred_element_type=jnp.float32
    )


def second_kernel(sizes, part, z_full, *refs):
    messages, before, out = refs[: len(part)], refs[len(part) : -1], refs[-1]
    c = lax.axis_index("col")
    total = before[0][...] if before else None
    for d, message in zip(part, messages):
        added = turned_dot(z_full[:, columns_of(c ^ d, sizes)], message[...])
        total = added if total is None else total + added
    out[...] = total


def last_kernel(sizes, part, dl, zp, z_full, before, *refs):
    cols, q = sizes.cols, sizes.quarter
    messages, strips = refs[: len(part)], refs[len(part) : -2]
    out, zs = refs[-2:]
    r, c, l = place()
    far = c ^ (cols // 2)
    zs[...] = z_full[:, columns_of(far, sizes)]
    for n, strip in enumerate(strips):
        zs[pl.ds(strip_start(l ^ dl, n, sizes), q), :] = mask_strip(
            zp, r, l ^ dl, n, far, strip[...], sizes
        )
    total = before[...]
    for d, message in zip(part, messages):
        piece = zs[...] if d == cols // 2 else z_full[:, columns_of(c ^ d, sizes)]
        total += turned_dot(piece, message[...])
    out[...] = total.astype(out.dtype)


def local(sizes, hamiltonian, inv_root, h_pattern, z_pattern):
    rows, cols, layers, per = sizes.rows, sizes.cols, sizes.layers, sizes.per
    q, cols_here, rows_here = sizes.quarter, sizes.cols_here, sizes.rows_here
    order = rows * rows_here
    height = per * q
    row_bits, layer_bits = bits_of(rows), bits_of(layers)
    f32 = jnp.float32
    strip_shape = shape(q, cols_here)

    striped = inv_root.reshape(per, layers, q, cols_here)
    l = lax.axis_index("layer")
    own = lax.dynamic_index_in_dim(striped, l, 1, keepdims=False).reshape(height, cols_here)
    slots = [own]
    right = left = own
    for s in range(1, cols):
        if s % 2:
            right = lax.ppermute(right, "col", [(i, (i + 1) % cols) for i in range(cols)])
        else:
            left = lax.ppermute(left, "col", [(i, (i - 1) % cols) for i in range(cols)])
        slots.append(right if s % 2 else left)

    def cross(piece):
        return lax.ppermute(piece, "layer", flip(layers, layer_bits[0]))

    top, low = layer_bits
    h_pattern, z_pattern, fetched = run(
        fetch_kernel,
        "fetch",
        [shape(*h_pattern.shape, jnp.int32)] * 2 + [shape(*hamiltonian.shape)],
        [hamiltonian],
        smem=[h_pattern, z_pattern],
    )
    h_pieces, h_table = [hamiltonian], [(0, 0)]
    for axis, bit in [("layer", top)] + [("row", b) for b in row_bits]:
        perm = flip(rows if axis == "row" else layers, bit)
        for piece, (dr, dl) in list(zip(h_pieces, h_table)):
            h_table.append((dr ^ bit, dl) if axis == "row" else (dr, dl ^ bit))
            if dl and axis == 'row':
                piece = pack([piece], [slots[1]])
            h_pieces.append(lax.ppermute(piece, axis, perm))
    zm, *h_own = run(
        functools.partial(bring_kernel, sizes, h_table),
        "bring",
        [shape(height, order)] + [shape(cols_here, 2 * q)] * cols,
        [fetched, *h_pieces[1:], *slots[:-1]],
        smem=[h_pattern, z_pattern],
    )
    h_other = [lax.ppermute(block, "layer", flip(layers, low)) for block in h_own]
    product = run(
        functools.partial(first_kernel, sizes, top),
        "first_product",
        [shape(height, cols_here)],
        [zm, slots[-1], *h_own, *h_other],
        smem=[z_pattern],
        scratch=[pltpu.VMEM((height, order), jnp.bfloat16)],
    )[0]

    gathered = {0: product}
    for bit in row_bits:
        for dr, piece in list(gathered.items()):
            gathered[dr ^ bit] = lax.ppermute(piece, "row", flip(rows, bit))
    row_offsets = list(gathered)
    held, z_table = [inv_root], {}

    last = pack([slots[-1]], [product])
    last_top = cross(last)
    last_low = lax.ppermute(last, "layer", flip(layers, low))
    outgoing = run(
        functools.partial(route_kernel, sizes, row_offsets),
        "route",
        [shape(q, cols_here)] * cols,
        [gathered[o] for o in row_offsets],
        after=[last_low],
        scratch=[pltpu.VMEM((cols * q, cols_here), jnp.bfloat16)],
    )
    messages = [
        lax.ppermute(outgoing[d], "col", flip(cols, d)) for d in range(cols - 1, 0, -1)
    ]
    messages = [outgoing[0]] + messages[::-1]
    group = range(1, cols - 1)
    mine = pack([slots[s] for s in group])
    other = cross(mine)
    both = lax.ppermute(pack([mine, other], [outgoing[0]]), "layer", flip(layers, low))
    held, z_table = [inv_root, mine, other, both, last, last_low, last_top], {}
    for n, s in enumerate(group):
        row = n * height
        z_table[0, s], z_table[top, s], z_table[low, s] = (1, row), (2, row), (3, row)
        z_table[low ^ top, s] = (3, len(group) * height + row)
    for n, dl in enumerate((0, low, top)):
        z_table[dl, cols - 1] = (4 + n, 0)
    parts = run(split_kernel, "split", [strip_shape] * per, [last_top])
    parts = [lax.ppermute(part, "layer", flip(layers, low)) for part in parts]
    z_full = run(
        functools.partial(layers_kernel, sizes, z_table),
        "layers",
        [shape(rows_here, order)],
        held,
        smem=[z_pattern],
    )[0]
    early = [0, *range(cols - 1, cols // 2, -1)]
    late = range(cols // 2, 0, -1)
    total = run(
        functools.partial(second_kernel, sizes, early),
        "second_product",
        [shape(*hamiltonian.shape, f32)],
        [z_full, *[messages[d] for d in early]],
    )[0]
    return run(
        functools.partial(last_kernel, sizes, late, low ^ top),
        "last_product",
        [shape(*hamiltonian.shape)],
        [z_full, total, *[messages[d] for d in late], *parts],
        smem=[z_pattern],
        scratch=[pltpu.VMEM((rows_here, cols_here), jnp.bfloat16)],
    )[0]


def solution(mesh):
    rows, cols, layers = (mesh.shape[a] for a in ("row", "col", "layer"))

    def whole(hamiltonian, inv_root, h_pattern, z_pattern):
        order = hamiltonian.shape[0]
        cols_here = order // cols
        sizes = Sizes(
            rows, cols, layers, order // rows, cols_here, cols_here // layers, cols // rows
        )
        return jax.shard_map(
            functools.partial(local, sizes),
            mesh=mesh,
            in_specs=(P("row", ("col", "layer")), P("row", "col"), P(), P()),
            out_specs=P("row", ("col", "layer")),
            check_vma=False,
        )(hamiltonian, inv_root, h_pattern, z_pattern)

    return whole
```

```python
import functools
from typing import NamedTuple

import jax
import jax.numpy as jnp
from jax import lax
from jax.experimental import pallas as pl
from jax.experimental.pallas import tpu as pltpu
from jax.sharding import PartitionSpec as P

BS = 256
MARGIN = 4 * 1024 * 1024


class Sizes(NamedTuple):
    rows: int
    cols: int
    layers: int
    rows_here: int
    cols_here: int
    quarter: int
    per: int


def bits_of(size):
    return [1 << b for b in reversed(range(size.bit_length() - 1))]


def flip(size, bit):
    return [(i, i ^ bit) for i in range(size)]


def mod(a, n):
    return lax.rem(a + n, n)


def place():
    return lax.axis_index("row"), lax.axis_index("col"), lax.axis_index("layer")


def run(kernel, name, outs, arrays, smem=(), after=(), scratch=(), flops=0):
    size = sum(a.size * a.dtype.itemsize for a in arrays)
    size += sum(o.size * o.dtype.itemsize for o in outs)
    for kept in scratch:
        size += kept.shape[0] * kept.shape[1] * jnp.dtype(kept.dtype).itemsize
    skip = len(smem) + len(arrays)

    def body(*refs):
        kernel(*refs[:skip], *refs[skip + len(after) :])

    return pl.pallas_call(
        body,
        out_shape=list(outs),
        in_specs=[pl.BlockSpec(memory_space=pltpu.SMEM)] * len(smem)
        + [pl.BlockSpec(memory_space=pltpu.VMEM)] * len(arrays)
        + [pl.BlockSpec(memory_space=pl.ANY)] * len(after),
        out_specs=[
            pl.BlockSpec(memory_space=pltpu.SMEM if o.dtype == jnp.int32 else pltpu.VMEM)
            for o in outs
        ],
        scratch_shapes=list(scratch),
        compiler_params=pltpu.CompilerParams(vmem_limit_bytes=size + MARGIN),
        cost_estimate=pl.CostEstimate(flops=flops, bytes_accessed=size, transcendentals=0),
        name=name,
    )(*smem, *arrays, *after)


def shape(rows, columns, dtype=jnp.bfloat16):
    return jax.ShapeDtypeStruct((rows, columns), dtype)


def keep_block(pattern, i, j, block):
    return jnp.where(pattern[i, j] > 0, block, jnp.zeros_like(block))


def strip_start(l, half, sizes):
    return pl.multiple_of(half * sizes.cols_here + l * sizes.quarter, sizes.quarter)


def columns_of(cc, sizes):
    return pl.ds(pl.multiple_of(cc * sizes.cols_here, sizes.cols_here), sizes.cols_here)


def mask_strip(zp, r, l, half, cc, strip, sizes):
    block_row = (r * sizes.rows_here + half * sizes.cols_here + l * sizes.quarter) // BS
    first = cc * (sizes.cols_here // BS)
    return jnp.concatenate(
        [
            keep_block(zp, block_row, first + t, strip[:, t * BS : (t + 1) * BS])
            for t in range(sizes.cols_here // BS)
        ],
        axis=1,
    )


def mask_piece(zp, r, l, cc, piece, sizes):
    q = sizes.quarter
    return jnp.concatenate(
        [
            mask_strip(zp, r, l, half, cc, piece[half * q : (half + 1) * q, :], sizes)
            for half in range(sizes.per)
        ],
        axis=0,
    )


def pack_kernel(*refs):
    out, row = refs[-1], 0
    for ref in refs[:-1]:
        out[row : row + ref.shape[0], :] = ref[...]
        row += ref.shape[0]


def pack(pieces, after=()):
    height = sum(p.shape[0] for p in pieces)
    out = shape(height, pieces[0].shape[1])
    return run(pack_kernel, "pack", [out], pieces, after=after)[0]


def slot_column(c, s, cols):
    return mod(c - (s + 1) // 2 if s % 2 else c + s // 2, cols)


def mask_kernel(sizes, zp, *refs):
    slots, out = refs[:-1], refs[-1]
    r, c, l = place()
    out[...] = jnp.zeros_like(out)
    for s, slot in enumerate(slots):
        cc = slot_column(c, s, sizes.cols)
        out[:, columns_of(cc, sizes)] = mask_piece(zp, r, l, cc, slot[...], sizes)


def fetch_kernel(hp, zp, h, hp_out, zp_out, h_out):
    h_out[...] = h[...]
    for i in range(hp.shape[0]):
        for j in range(hp.shape[1]):
            hp_out[i, j] = hp[i, j]
            zp_out[i, j] = zp[i, j]


def bring_kernel(sizes, h_table, hp, zp, *refs):
    n = len(h_table)
    pieces, slots = refs[:n], refs[n : n + sizes.cols - 1]
    zm, sent, blocks = refs[n + sizes.cols - 1], refs[n + sizes.cols : 2 * n + sizes.cols - 1], refs[
        2 * n + sizes.cols - 1 :
    ]
    r, c, l = place()
    q, wide = sizes.quarter, blocks[0].shape[0]
    for h, (dr, dl) in zip(pieces, h_table):
        columns = slice(q, 2 * q) if dl else slice(0, q)
        block_col = (c * sizes.cols_here + (l ^ dl) * q) // BS
        for rr in range(sizes.rows):

            @pl.when((r ^ dr) == rr)
            def _(h=h, rr=rr, columns=columns, block_col=block_col):
                for first in range(0, sizes.rows_here, BS):
                    row = rr * sizes.rows_here + first
                    at = row % wide
                    blocks[row // wide][at : at + BS, columns] = keep_block(
                        hp, row // BS, block_col, h[first : first + BS, :]
                    )

    for (dr, dl), h, out in zip(h_table[1:], pieces[1:], sent):
        block_col = (c * sizes.cols_here + (l ^ dl) * q) // BS
        for first in range(0, sizes.rows_here, BS):
            j = ((r ^ dr) * sizes.rows_here + first) // BS
            out[first : first + BS, :] = keep_block(hp, j, block_col, h[first : first + BS, :])
    mask_kernel(sizes, zp, *slots, zm)


def first_kernel(sizes, top, h_table, hp, zp, zm, last, raw, *refs):
    cols, q, n = sizes.cols, sizes.quarter, len(h_table) - 1
    others, blocks, (out, zs, hs) = refs[:n], refs[n:-3], refs[-3:]
    r, c, l = place()
    cc = slot_column(c, cols - 1, cols)
    zs[...] = zm[...]
    zs[:, columns_of(cc, sizes)] = mask_piece(zp, r, l, cc, last[...], sizes)
    block_col = (c * sizes.cols_here + (l ^ 1) * q) // BS
    for first in range(0, sizes.rows_here, BS):
        j = (r * sizes.rows_here + first) // BS
        hs[first : first + BS, :] = keep_block(hp, j, block_col, raw[first : first + BS, :])
    width, acc = blocks[0].shape[0], None
    for n, block in enumerate(blocks):
        part = jnp.dot(
            zs[:, n * width : (n + 1) * width], block[...], preferred_element_type=jnp.float32
        )
        acc = part if acc is None else acc + part
    for n, ll in enumerate((l, l ^ top)):
        out[:, pl.ds(pl.multiple_of(ll * q, q), q)] = acc[:, n * q : (n + 1) * q].astype(out.dtype)
    for dl in (0, top):
        acc = None
        for (dr, there), h in zip(h_table, [hs, *others]):
            if there == dl:
                rows = pl.ds(
                    pl.multiple_of((r ^ dr) * sizes.rows_here, sizes.rows_here), sizes.rows_here
                )
                part = jnp.dot(zs[:, rows], h[...], preferred_element_type=jnp.float32)
                acc = part if acc is None else acc + part
        ll = l ^ 1 ^ dl
        out[:, pl.ds(pl.multiple_of(ll * q, q), q)] = acc.astype(out.dtype)


def route_kernel(sizes, row_offsets, *refs):
    n = len(row_offsets)
    pieces, outs, table = refs[:n], refs[n:-1], refs[-1]
    r, c, _ = place()
    q = sizes.quarter
    for dr, piece in zip(row_offsets, pieces):
        for half in range(sizes.per):
            start = pl.multiple_of(((r ^ dr) * sizes.per + half) * q, q)
            table[pl.ds(start, q), :] = piece[half * q : (half + 1) * q, :]
    for d, out in enumerate(outs):
        out[...] = table[pl.ds(pl.multiple_of((c ^ d) * q, q), q), :]


def split_kernel(*refs):
    pieces, outs = [], []
    for ref in refs:
        (pieces if ref.shape[0] > refs[-1].shape[0] else outs).append(ref)
    per, height = len(outs) // len(pieces), outs[0].shape[0]
    for n, out in enumerate(outs):
        first = n % per * height
        out[...] = pieces[n // per][first : first + height, :]


def layers_kernel(sizes, z_table, zp, *refs):
    cols, q = sizes.cols, sizes.quarter
    out, held = refs[-1], refs[:-1]
    r, c, l = place()
    for dl in range(sizes.layers):
        ll = l ^ dl
        for half in range(sizes.per):
            rows = pl.ds(strip_start(ll, half, sizes), q)
            for s in range(cols):
                cc = slot_column(c, s, cols)
                columns = columns_of(cc, sizes)
                if s and (dl, s) not in z_table:
                    out[rows, columns] = jnp.zeros((q, sizes.cols_here), out.dtype)
                    continue
                if s == 0:
                    strip = held[0][rows, :]
                else:
                    index, row = z_table[dl, s]
                    strip = held[index][row + half * q : row + (half + 1) * q, :]
                out[rows, columns] = mask_strip(zp, r, ll, half, cc, strip, sizes)


def turned_dot(left, right):
    return lax.dot_general(
        left, right, (((1,), (1,)), ((), ())), preferred_element_type=jnp.float32
    )


def second_kernel(sizes, part, z_full, *refs):
    messages, before, out = refs[: len(part)], refs[len(part) : -1], refs[-1]
    c = lax.axis_index("col")
    total = before[0][...] if before else None
    for d, message in zip(part, messages):
        added = turned_dot(z_full[:, columns_of(c ^ d, sizes)], message[...])
        total = added if total is None else total + added
    out[...] = total


def last_kernel(sizes, part, dl, zp, z_full, before, *refs):
    cols, q = sizes.cols, sizes.quarter
    messages, strips = refs[: len(part)], refs[len(part) : -2]
    out, zs = refs[-2:]
    r, c, l = place()
    far = c ^ (cols // 2)
    zs[...] = z_full[:, columns_of(far, sizes)]
    for n, strip in enumerate(strips):
        zs[pl.ds(strip_start(l ^ dl, n, sizes), q), :] = mask_strip(
            zp, r, l ^ dl, n, far, strip[...], sizes
        )
    total = before[...]
    for d, message in zip(part, messages):
        piece = zs[...] if d == cols // 2 else z_full[:, columns_of(c ^ d, sizes)]
        total += turned_dot(piece, message[...])
    out[...] = total.astype(out.dtype)


def local(sizes, hamiltonian, inv_root, h_pattern, z_pattern):
    rows, cols, layers, per = sizes.rows, sizes.cols, sizes.layers, sizes.per
    q, cols_here, rows_here = sizes.quarter, sizes.cols_here, sizes.rows_here
    order = rows * rows_here
    height = per * q
    row_bits, layer_bits = bits_of(rows), bits_of(layers)
    f32 = jnp.float32
    strip_shape = shape(q, cols_here)

    striped = inv_root.reshape(per, layers, q, cols_here)
    l = lax.axis_index("layer")
    own = lax.dynamic_index_in_dim(striped, l, 1, keepdims=False).reshape(height, cols_here)
    slots = [own]
    right = left = own
    for s in range(1, cols):
        if s % 2:
            right = lax.ppermute(right, "col", [(i, (i + 1) % cols) for i in range(cols)])
        else:
            left = lax.ppermute(left, "col", [(i, (i - 1) % cols) for i in range(cols)])
        slots.append(right if s % 2 else left)

    def cross(piece):
        return lax.ppermute(piece, "layer", flip(layers, layer_bits[0]))

    top, low = layer_bits
    h_pattern, z_pattern, fetched = run(
        fetch_kernel,
        "fetch",
        [shape(*h_pattern.shape, jnp.int32)] * 2 + [shape(*hamiltonian.shape)],
        [hamiltonian],
        smem=[h_pattern, z_pattern],
    )
    h_pieces, h_table = [hamiltonian], [(0, 0)]
    for axis, bit in [("layer", top)] + [("row", b) for b in row_bits]:
        perm = flip(rows if axis == "row" else layers, bit)
        for piece, (dr, dl) in list(zip(h_pieces, h_table)):
            h_table.append((dr ^ bit, dl) if axis == "row" else (dr, dl ^ bit))
            if dl and axis == 'row':
                piece = pack([piece], [slots[1]])
            h_pieces.append(lax.ppermute(piece, axis, perm))
    raw = lax.ppermute(hamiltonian, "layer", flip(layers, low))
    group = range(1, cols - 1)
    mine = pack([slots[s] for s in group])
    other = cross(mine)
    n_sent = len(h_table) - 1
    zm, *h_own = run(
        functools.partial(bring_kernel, sizes, h_table),
        "bring",
        [shape(height, order)]
        + [shape(*hamiltonian.shape)] * n_sent
        + [shape(cols_here, 2 * q)] * cols,
        [fetched, *h_pieces[1:], *slots[:-1]],
        smem=[h_pattern, z_pattern],
        after=[raw, mine],
    )
    sent, h_own = h_own[:n_sent], h_own[n_sent:]
    h_other = [lax.ppermute(piece, "layer", flip(layers, low)) for piece in sent]
    crossed = []
    product = run(
        functools.partial(first_kernel, sizes, top, h_table),
        "first_product",
        [shape(height, cols_here)],
        [zm, slots[-1], raw, *h_other, *h_own],
        smem=[h_pattern, z_pattern],
        scratch=[
            pltpu.VMEM((height, order), jnp.bfloat16),
            pltpu.VMEM(hamiltonian.shape, jnp.bfloat16),
        ],
    )[0]

    gathered = {0: product}
    for bit in row_bits:
        for dr, piece in list(gathered.items()):
            gathered[dr ^ bit] = lax.ppermute(piece, "row", flip(rows, bit))
    row_offsets = list(gathered)
    held, z_table = [inv_root], {}

    last = pack([slots[-1]], [product])
    last_top = cross(last)
    last_low = lax.ppermute(last, "layer", flip(layers, low))
    outgoing = run(
        functools.partial(route_kernel, sizes, row_offsets),
        "route",
        [shape(q, cols_here)] * cols,
        [gathered[o] for o in row_offsets],
        after=[last_low],
        scratch=[pltpu.VMEM((cols * q, cols_here), jnp.bfloat16)],
    )
    messages = [
        lax.ppermute(outgoing[d], "col", flip(cols, d)) for d in range(cols - 1, 0, -1)
    ]
    messages = [outgoing[0]] + messages[::-1]
    both = lax.ppermute(pack([mine, other], [outgoing[0]]), "layer", flip(layers, low))
    held, z_table = [inv_root, mine, other, both, last, last_low, last_top], {}
    for n, s in enumerate(group):
        row = n * height
        z_table[0, s], z_table[top, s], z_table[low, s] = (1, row), (2, row), (3, row)
        z_table[low ^ top, s] = (3, len(group) * height + row)
    for n, dl in enumerate((0, low, top)):
        z_table[dl, cols - 1] = (4 + n, 0)
    parts = run(split_kernel, "split", [strip_shape] * per, [last_top])
    parts = [lax.ppermute(part, "layer", flip(layers, low)) for part in parts]
    z_full = run(
        functools.partial(layers_kernel, sizes, z_table),
        "layers",
        [shape(rows_here, order)],
        held,
        smem=[z_pattern],
    )[0]
    early = [0, *range(cols - 1, cols // 2, -1)]
    late = range(cols // 2, 0, -1)
    total = run(
        functools.partial(second_kernel, sizes, early),
        "second_product",
        [shape(*hamiltonian.shape, f32)],
        [z_full, *[messages[d] for d in early]],
    )[0]
    return run(
        functools.partial(last_kernel, sizes, late, low ^ top),
        "last_product",
        [shape(*hamiltonian.shape)],
        [z_full, total, *[messages[d] for d in late], *parts],
        smem=[z_pattern],
        scratch=[pltpu.VMEM((rows_here, cols_here), jnp.bfloat16)],
    )[0]


def solution(mesh):
    rows, cols, layers = (mesh.shape[a] for a in ("row", "col", "layer"))

    def whole(hamiltonian, inv_root, h_pattern, z_pattern):
        order = hamiltonian.shape[0]
        cols_here = order // cols
        sizes = Sizes(
            rows, cols, layers, order // rows, cols_here, cols_here // layers, cols // rows
        )
        return jax.shard_map(
            functools.partial(local, sizes),
            mesh=mesh,
            in_specs=(P("row", ("col", "layer")), P("row", "col"), P(), P()),
            out_specs=P("row", ("col", "layer")),
            check_vma=False,
        )(hamiltonian, inv_root, h_pattern, z_pattern)

    return whole
```

```python
import functools
from typing import NamedTuple

import jax
import jax.numpy as jnp
from jax import lax
from jax.experimental import pallas as pl
from jax.experimental.pallas import tpu as pltpu
from jax.sharding import PartitionSpec as P

BS = 256
MARGIN = 4 * 1024 * 1024


class Sizes(NamedTuple):
    rows: int
    cols: int
    layers: int
    rows_here: int
    cols_here: int
    quarter: int
    per: int


def bits_of(size):
    return [1 << b for b in reversed(range(size.bit_length() - 1))]


def flip(size, bit):
    return [(i, i ^ bit) for i in range(size)]


def mod(a, n):
    return lax.rem(a + n, n)


def place():
    return lax.axis_index("row"), lax.axis_index("col"), lax.axis_index("layer")


def run(kernel, name, outs, arrays, smem=(), after=(), scratch=(), flops=0):
    size = sum(a.size * a.dtype.itemsize for a in arrays)
    size += sum(o.size * o.dtype.itemsize for o in outs)
    for kept in scratch:
        size += kept.shape[0] * kept.shape[1] * jnp.dtype(kept.dtype).itemsize
    skip = len(smem) + len(arrays)

    def body(*refs):
        kernel(*refs[:skip], *refs[skip + len(after) :])

    return pl.pallas_call(
        body,
        out_shape=list(outs),
        in_specs=[pl.BlockSpec(memory_space=pltpu.SMEM)] * len(smem)
        + [pl.BlockSpec(memory_space=pltpu.VMEM)] * len(arrays)
        + [pl.BlockSpec(memory_space=pl.ANY)] * len(after),
        out_specs=[
            pl.BlockSpec(memory_space=pltpu.SMEM if o.dtype == jnp.int32 else pltpu.VMEM)
            for o in outs
        ],
        scratch_shapes=list(scratch),
        compiler_params=pltpu.CompilerParams(vmem_limit_bytes=size + MARGIN),
        cost_estimate=pl.CostEstimate(flops=flops, bytes_accessed=size, transcendentals=0),
        name=name,
    )(*smem, *arrays, *after)


def shape(rows, columns, dtype=jnp.bfloat16):
    return jax.ShapeDtypeStruct((rows, columns), dtype)


def keep_block(pattern, i, j, block):
    return jnp.where(pattern[i, j] > 0, block, jnp.zeros_like(block))


def strip_start(l, half, sizes):
    return pl.multiple_of(half * sizes.cols_here + l * sizes.quarter, sizes.quarter)


def columns_of(cc, sizes):
    return pl.ds(pl.multiple_of(cc * sizes.cols_here, sizes.cols_here), sizes.cols_here)


def mask_strip(zp, r, l, half, cc, strip, sizes):
    block_row = (r * sizes.rows_here + half * sizes.cols_here + l * sizes.quarter) // BS
    first = cc * (sizes.cols_here // BS)
    return jnp.concatenate(
        [
            keep_block(zp, block_row, first + t, strip[:, t * BS : (t + 1) * BS])
            for t in range(sizes.cols_here // BS)
        ],
        axis=1,
    )


def mask_piece(zp, r, l, cc, piece, sizes):
    q = sizes.quarter
    return jnp.concatenate(
        [
            mask_strip(zp, r, l, half, cc, piece[half * q : (half + 1) * q, :], sizes)
            for half in range(sizes.per)
        ],
        axis=0,
    )


def pack_kernel(*refs):
    out, row = refs[-1], 0
    for ref in refs[:-1]:
        out[row : row + ref.shape[0], :] = ref[...]
        row += ref.shape[0]


def pack(pieces, after=()):
    height = sum(p.shape[0] for p in pieces)
    out = shape(height, pieces[0].shape[1])
    return run(pack_kernel, "pack", [out], pieces, after=after)[0]


def slot_column(c, s, cols):
    return mod(c - (s + 1) // 2 if s % 2 else c + s // 2, cols)


def mask_kernel(sizes, zp, *refs):
    slots, out = refs[:-1], refs[-1]
    r, c, l = place()
    out[...] = jnp.zeros_like(out)
    for s, slot in enumerate(slots):
        cc = slot_column(c, s, sizes.cols)
        out[:, columns_of(cc, sizes)] = mask_piece(zp, r, l, cc, slot[...], sizes)


def fetch_kernel(hp, zp, h, hp_out, zp_out, h_out):
    h_out[...] = h[...]
    for i in range(hp.shape[0]):
        for j in range(hp.shape[1]):
            hp_out[i, j] = hp[i, j]
            zp_out[i, j] = zp[i, j]


def bring_kernel(sizes, h_table, hp, zp, *refs):
    n = len(h_table)
    pieces, slots = refs[:n], refs[n : n + sizes.cols - 1]
    zm, blocks = refs[n + sizes.cols - 1], refs[n + sizes.cols :]
    r, c, l = place()
    q, wide = sizes.quarter, blocks[0].shape[0]
    for h, (dr, dl) in zip(pieces, h_table):
        columns = slice(q, 2 * q) if dl else slice(0, q)
        block_col = (c * sizes.cols_here + (l ^ dl) * q) // BS
        for rr in range(sizes.rows):

            @pl.when((r ^ dr) == rr)
            def _(h=h, rr=rr, columns=columns, block_col=block_col):
                for first in range(0, sizes.rows_here, BS):
                    row = rr * sizes.rows_here + first
                    at = row % wide
                    blocks[row // wide][at : at + BS, columns] = keep_block(
                        hp, row // BS, block_col, h[first : first + BS, :]
                    )

    mask_kernel(sizes, zp, *slots, zm)


def first_kernel(sizes, top, zp, zm, last, *refs):
    cols, q = sizes.cols, sizes.quarter
    n, (out, zs) = len(refs) // 2 - 1, refs[-2:]
    sides, width = (refs[:n], refs[n : 2 * n]), refs[0].shape[0]
    r, c, l = place()
    cc = slot_column(c, cols - 1, cols)
    zs[...] = zm[...]
    zs[:, columns_of(cc, sizes)] = mask_piece(zp, r, l, cc, last[...], sizes)
    for side, blocks in zip((l, l ^ 1), sides):
        acc = None
        for n, block in enumerate(blocks):
            part = jnp.dot(
                zs[:, n * width : (n + 1) * width], block[...], preferred_element_type=jnp.float32
            )
            acc = part if acc is None else acc + part
        for n, ll in enumerate((side, side ^ top)):
            out[:, pl.ds(pl.multiple_of(ll * q, q), q)] = acc[:, n * q : (n + 1) * q].astype(
                out.dtype
            )


def route_kernel(sizes, row_offsets, *refs):
    n = len(row_offsets)
    pieces, outs, table = refs[:n], refs[n:-1], refs[-1]
    r, c, _ = place()
    q = sizes.quarter
    for dr, piece in zip(row_offsets, pieces):
        for half in range(sizes.per):
            start = pl.multiple_of(((r ^ dr) * sizes.per + half) * q, q)
            table[pl.ds(start, q), :] = piece[half * q : (half + 1) * q, :]
    for d, out in enumerate(outs):
        out[...] = table[pl.ds(pl.multiple_of((c ^ d) * q, q), q), :]


def split_kernel(*refs):
    pieces, outs = [], []
    for ref in refs:
        (pieces if ref.shape[0] > refs[-1].shape[0] else outs).append(ref)
    per, height = len(outs) // len(pieces), outs[0].shape[0]
    for n, out in enumerate(outs):
        first = n % per * height
        out[...] = pieces[n // per][first : first + height, :]


def layers_kernel(sizes, z_table, zp, *refs):
    cols, q = sizes.cols, sizes.quarter
    out, held = refs[-1], refs[:-1]
    r, c, l = place()
    for dl in range(sizes.layers):
        ll = l ^ dl
        for half in range(sizes.per):
            rows = pl.ds(strip_start(ll, half, sizes), q)
            for s in range(cols):
                cc = slot_column(c, s, cols)
                columns = columns_of(cc, sizes)
                if s and (dl, s) not in z_table:
                    out[rows, columns] = jnp.zeros((q, sizes.cols_here), out.dtype)
                    continue
                if s == 0:
                    strip = held[0][rows, :]
                else:
                    index, row = z_table[dl, s]
                    strip = held[index][row + half * q : row + (half + 1) * q, :]
                out[rows, columns] = mask_strip(zp, r, ll, half, cc, strip, sizes)


def turned_dot(left, right):
    return lax.dot_general(
        left, right, (((1,), (1,)), ((), ())), preferred_element_type=jnp.float32
    )


def second_kernel(sizes, part, z_full, *refs):
    messages, before, out = refs[: len(part)], refs[len(part) : -1], refs[-1]
    c = lax.axis_index("col")
    total = before[0][...] if before else None
    for d, message in zip(part, messages):
        added = turned_dot(z_full[:, columns_of(c ^ d, sizes)], message[...])
        total = added if total is None else total + added
    out[...] = total


def last_kernel(sizes, part, dl, zp, z_full, before, *refs):
    cols, q = sizes.cols, sizes.quarter
    messages, strips = refs[: len(part)], refs[len(part) : -2]
    out, zs = refs[-2:]
    r, c, l = place()
    far = c ^ (cols // 2)
    zs[...] = z_full[:, columns_of(far, sizes)]
    for n, strip in enumerate(strips):
        zs[pl.ds(strip_start(l ^ dl, n, sizes), q), :] = mask_strip(
            zp, r, l ^ dl, n, far, strip[...], sizes
        )
    total = before[...]
    for d, message in zip(part, messages):
        piece = zs[...] if d == cols // 2 else z_full[:, columns_of(c ^ d, sizes)]
        total += turned_dot(piece, message[...])
    out[...] = total.astype(out.dtype)


def local(sizes, hamiltonian, inv_root, h_pattern, z_pattern):
    rows, cols, layers, per = sizes.rows, sizes.cols, sizes.layers, sizes.per
    q, cols_here, rows_here = sizes.quarter, sizes.cols_here, sizes.rows_here
    order = rows * rows_here
    height = per * q
    row_bits, layer_bits = bits_of(rows), bits_of(layers)
    f32 = jnp.float32
    strip_shape = shape(q, cols_here)

    striped = inv_root.reshape(per, layers, q, cols_here)
    l = lax.axis_index("layer")
    own = lax.dynamic_index_in_dim(striped, l, 1, keepdims=False).reshape(height, cols_here)
    slots = [own]
    right = left = own
    for s in range(1, cols):
        if s % 2:
            right = lax.ppermute(right, "col", [(i, (i + 1) % cols) for i in range(cols)])
        else:
            left = lax.ppermute(left, "col", [(i, (i - 1) % cols) for i in range(cols)])
        slots.append(right if s % 2 else left)

    def cross(piece):
        return lax.ppermute(piece, "layer", flip(layers, layer_bits[0]))

    top, low = layer_bits
    h_pattern, z_pattern, fetched = run(
        fetch_kernel,
        "fetch",
        [shape(*h_pattern.shape, jnp.int32)] * 2 + [shape(*hamiltonian.shape)],
        [hamiltonian],
        smem=[h_pattern, z_pattern],
    )
    h_pieces, h_table = [hamiltonian], [(0, 0)]
    for axis, bit in [("layer", top)] + [("row", b) for b in row_bits]:
        perm = flip(rows if axis == "row" else layers, bit)
        for piece, (dr, dl) in list(zip(h_pieces, h_table)):
            h_table.append((dr ^ bit, dl) if axis == "row" else (dr, dl ^ bit))
            if False:
                piece = pack([piece], [])
            h_pieces.append(lax.ppermute(piece, axis, perm))
    zm, *h_own = run(
        functools.partial(bring_kernel, sizes, h_table),
        "bring",
        [shape(height, order)] + [shape(cols_here, 2 * q)] * cols,
        [fetched, *h_pieces[1:], *slots[:-1]],
        smem=[h_pattern, z_pattern],
    )
    h_other = [lax.ppermute(block, "layer", flip(layers, low)) for block in h_own]
    product = run(
        functools.partial(first_kernel, sizes, top),
        "first_product",
        [shape(height, cols_here)],
        [zm, slots[-1], *h_own, *h_other],
        smem=[z_pattern],
        scratch=[pltpu.VMEM((height, order), jnp.bfloat16)],
    )[0]

    gathered = {0: product}
    for bit in row_bits:
        for dr, piece in list(gathered.items()):
            gathered[dr ^ bit] = lax.ppermute(piece, "row", flip(rows, bit))
    row_offsets = list(gathered)
    held, z_table = [inv_root], {}

    last = pack([slots[-1]], [product])
    last_top = cross(last)
    last_low = lax.ppermute(last, "layer", flip(layers, low))
    outgoing = run(
        functools.partial(route_kernel, sizes, row_offsets),
        "route",
        [shape(q, cols_here)] * cols,
        [gathered[o] for o in row_offsets],
        after=[last_low],
        scratch=[pltpu.VMEM((cols * q, cols_here), jnp.bfloat16)],
    )
    messages = [
        lax.ppermute(outgoing[d], "col", flip(cols, d)) for d in range(cols - 1, 0, -1)
    ]
    messages = [outgoing[0]] + messages[::-1]
    group = range(1, cols - 1)
    mine = pack([slots[s] for s in group])
    other = cross(mine)
    both = lax.ppermute(pack([mine, other], [outgoing[0]]), "layer", flip(layers, low))
    held, z_table = [inv_root, mine, other, both, last, last_low, last_top], {}
    for n, s in enumerate(group):
        row = n * height
        z_table[0, s], z_table[top, s], z_table[low, s] = (1, row), (2, row), (3, row)
        z_table[low ^ top, s] = (3, len(group) * height + row)
    for n, dl in enumerate((0, low, top)):
        z_table[dl, cols - 1] = (4 + n, 0)
    parts = run(split_kernel, "split", [strip_shape] * per, [last_top])
    parts = [lax.ppermute(part, "layer", flip(layers, low)) for part in parts]
    z_full = run(
        functools.partial(layers_kernel, sizes, z_table),
        "layers",
        [shape(rows_here, order)],
        held,
        smem=[z_pattern],
    )[0]
    early = [0, *range(cols - 1, cols // 2, -1)]
    late = range(cols // 2, 0, -1)
    total = run(
        functools.partial(second_kernel, sizes, early),
        "second_product",
        [shape(*hamiltonian.shape, f32)],
        [z_full, *[messages[d] for d in early]],
    )[0]
    return run(
        functools.partial(last_kernel, sizes, late, low ^ top),
        "last_product",
        [shape(*hamiltonian.shape)],
        [z_full, total, *[messages[d] for d in late], *parts],
        smem=[z_pattern],
        scratch=[pltpu.VMEM((rows_here, cols_here), jnp.bfloat16)],
    )[0]


def solution(mesh):
    rows, cols, layers = (mesh.shape[a] for a in ("row", "col", "layer"))

    def whole(hamiltonian, inv_root, h_pattern, z_pattern):
        order = hamiltonian.shape[0]
        cols_here = order // cols
        sizes = Sizes(
            rows, cols, layers, order // rows, cols_here, cols_here // layers, cols // rows
        )
        return jax.shard_map(
            functools.partial(local, sizes),
            mesh=mesh,
            in_specs=(P("row", ("col", "layer")), P("row", "col"), P(), P()),
            out_specs=P("row", ("col", "layer")),
            check_vma=False,
        )(hamiltonian, inv_root, h_pattern, z_pattern)

    return whole
```

```python
import functools
from typing import NamedTuple

import jax
import jax.numpy as jnp
from jax import lax
from jax.experimental import pallas as pl
from jax.experimental.pallas import tpu as pltpu
from jax.sharding import PartitionSpec as P

BS = 256
MARGIN = 4 * 1024 * 1024


class Sizes(NamedTuple):
    rows: int
    cols: int
    layers: int
    rows_here: int
    cols_here: int
    quarter: int
    per: int


def bits_of(size):
    return [1 << b for b in reversed(range(size.bit_length() - 1))]


def flip(size, bit):
    return [(i, i ^ bit) for i in range(size)]


def mod(a, n):
    return lax.rem(a + n, n)


def place():
    return lax.axis_index("row"), lax.axis_index("col"), lax.axis_index("layer")


def run(kernel, name, outs, arrays, smem=(), after=(), scratch=(), flops=0):
    size = sum(a.size * a.dtype.itemsize for a in arrays)
    size += sum(o.size * o.dtype.itemsize for o in outs)
    for kept in scratch:
        size += kept.shape[0] * kept.shape[1] * jnp.dtype(kept.dtype).itemsize
    skip = len(smem) + len(arrays)

    def body(*refs):
        kernel(*refs[:skip], *refs[skip + len(after) :])

    return pl.pallas_call(
        body,
        out_shape=list(outs),
        in_specs=[pl.BlockSpec(memory_space=pltpu.SMEM)] * len(smem)
        + [pl.BlockSpec(memory_space=pltpu.VMEM)] * len(arrays)
        + [pl.BlockSpec(memory_space=pl.ANY)] * len(after),
        out_specs=[pl.BlockSpec(memory_space=pltpu.VMEM)] * len(outs),
        scratch_shapes=list(scratch),
        compiler_params=pltpu.CompilerParams(vmem_limit_bytes=size + MARGIN),
        cost_estimate=pl.CostEstimate(flops=flops, bytes_accessed=size, transcendentals=0),
        name=name,
    )(*smem, *arrays, *after)


def shape(rows, columns, dtype=jnp.bfloat16):
    return jax.ShapeDtypeStruct((rows, columns), dtype)


def keep_block(pattern, i, j, block):
    return jnp.where(pattern[i, j] > 0, block, jnp.zeros_like(block))


def strip_start(l, half, sizes):
    return pl.multiple_of(half * sizes.cols_here + l * sizes.quarter, sizes.quarter)


def columns_of(cc, sizes):
    return pl.ds(pl.multiple_of(cc * sizes.cols_here, sizes.cols_here), sizes.cols_here)


def mask_strip(zp, r, l, half, cc, strip, sizes):
    block_row = (r * sizes.rows_here + half * sizes.cols_here + l * sizes.quarter) // BS
    first = cc * (sizes.cols_here // BS)
    return jnp.concatenate(
        [
            keep_block(zp, block_row, first + t, strip[:, t * BS : (t + 1) * BS])
            for t in range(sizes.cols_here // BS)
        ],
        axis=1,
    )


def mask_piece(zp, r, l, cc, piece, sizes):
    q = sizes.quarter
    return jnp.concatenate(
        [
            mask_strip(zp, r, l, half, cc, piece[half * q : (half + 1) * q, :], sizes)
            for half in range(sizes.per)
        ],
        axis=0,
    )


def pack_kernel(*refs):
    out, row = refs[-1], 0
    for ref in refs[:-1]:
        out[row : row + ref.shape[0], :] = ref[...]
        row += ref.shape[0]


def pack(pieces, after=()):
    height = sum(p.shape[0] for p in pieces)
    out = shape(height, pieces[0].shape[1])
    return run(pack_kernel, "pack", [out], pieces, after=after)[0]


def slot_column(c, s, cols):
    return mod(c - (s + 1) // 2 if s % 2 else c + s // 2, cols)


def mask_kernel(sizes, zp, *refs):
    slots, out = refs[:-1], refs[-1]
    r, c, l = place()
    out[...] = jnp.zeros_like(out)
    for s, slot in enumerate(slots):
        cc = slot_column(c, s, sizes.cols)
        out[:, columns_of(cc, sizes)] = mask_piece(zp, r, l, cc, slot[...], sizes)


def fetch_kernel(hp, zp, h, hp_out, zp_out, h_out):
    for ref, out in ((hp, hp_out), (zp, zp_out), (h, h_out)):
        out[...] = ref[...]


def bring_kernel(sizes, h_table, hp, zp, *refs):
    n = len(h_table)
    pieces, slots = refs[:n], refs[n : n + sizes.cols - 1]
    zm, blocks = refs[n + sizes.cols - 1], refs[n + sizes.cols :]
    r, c, l = place()
    q, wide = sizes.quarter, blocks[0].shape[0]
    for h, (dr, dl) in zip(pieces, h_table):
        columns = slice(q, 2 * q) if dl else slice(0, q)
        block_col = (c * sizes.cols_here + (l ^ dl) * q) // BS
        for rr in range(sizes.rows):

            @pl.when((r ^ dr) == rr)
            def _(h=h, rr=rr, columns=columns, block_col=block_col):
                for first in range(0, sizes.rows_here, BS):
                    row = rr * sizes.rows_here + first
                    at = row % wide
                    blocks[row // wide][at : at + BS, columns] = keep_block(
                        hp, row // BS, block_col, h[first : first + BS, :]
                    )

    mask_kernel(sizes, zp, *slots, zm)


def first_kernel(sizes, top, zp, zm, last, *refs):
    cols, q = sizes.cols, sizes.quarter
    n, (out, zs) = len(refs) // 2 - 1, refs[-2:]
    sides, width = (refs[:n], refs[n : 2 * n]), refs[0].shape[0]
    r, c, l = place()
    cc = slot_column(c, cols - 1, cols)
    zs[...] = zm[...]
    zs[:, columns_of(cc, sizes)] = mask_piece(zp, r, l, cc, last[...], sizes)
    for side, blocks in zip((l, l ^ 1), sides):
        acc = None
        for n, block in enumerate(blocks):
            part = jnp.dot(
                zs[:, n * width : (n + 1) * width], block[...], preferred_element_type=jnp.float32
            )
            acc = part if acc is None else acc + part
        for n, ll in enumerate((side, side ^ top)):
            out[:, pl.ds(pl.multiple_of(ll * q, q), q)] = acc[:, n * q : (n + 1) * q].astype(
                out.dtype
            )


def route_kernel(sizes, row_offsets, *refs):
    n = len(row_offsets)
    pieces, outs, table = refs[:n], refs[n:-1], refs[-1]
    r, c, _ = place()
    q = sizes.quarter
    for dr, piece in zip(row_offsets, pieces):
        for half in range(sizes.per):
            start = pl.multiple_of(((r ^ dr) * sizes.per + half) * q, q)
            table[pl.ds(start, q), :] = piece[half * q : (half + 1) * q, :]
    for d, out in enumerate(outs):
        out[...] = table[pl.ds(pl.multiple_of((c ^ d) * q, q), q), :]


def split_kernel(*refs):
    pieces, outs = [], []
    for ref in refs:
        (pieces if ref.shape[0] > refs[-1].shape[0] else outs).append(ref)
    per, height = len(outs) // len(pieces), outs[0].shape[0]
    for n, out in enumerate(outs):
        first = n % per * height
        out[...] = pieces[n // per][first : first + height, :]


def layers_kernel(sizes, z_table, zp, *refs):
    cols, q = sizes.cols, sizes.quarter
    out, held = refs[-1], refs[:-1]
    r, c, l = place()
    for dl in range(sizes.layers):
        ll = l ^ dl
        for half in range(sizes.per):
            rows = pl.ds(strip_start(ll, half, sizes), q)
            for s in range(cols):
                cc = slot_column(c, s, cols)
                columns = columns_of(cc, sizes)
                if s and (dl, s) not in z_table:
                    out[rows, columns] = jnp.zeros((q, sizes.cols_here), out.dtype)
                    continue
                if s == 0:
                    strip = held[0][rows, :]
                else:
                    index, row = z_table[dl, s]
                    strip = held[index][row + half * q : row + (half + 1) * q, :]
                out[rows, columns] = mask_strip(zp, r, ll, half, cc, strip, sizes)


def turned_dot(left, right):
    return lax.dot_general(
        left, right, (((1,), (1,)), ((), ())), preferred_element_type=jnp.float32
    )


def second_kernel(sizes, part, z_full, *refs):
    messages, before, out = refs[: len(part)], refs[len(part) : -1], refs[-1]
    c = lax.axis_index("col")
    total = before[0][...] if before else None
    for d, message in zip(part, messages):
        added = turned_dot(z_full[:, columns_of(c ^ d, sizes)], message[...])
        total = added if total is None else total + added
    out[...] = total


def last_kernel(sizes, part, dl, zp, z_full, before, *refs):
    cols, q = sizes.cols, sizes.quarter
    messages, strips = refs[: len(part)], refs[len(part) : -2]
    out, zs = refs[-2:]
    r, c, l = place()
    far = c ^ (cols // 2)
    zs[...] = z_full[:, columns_of(far, sizes)]
    for n, strip in enumerate(strips):
        zs[pl.ds(strip_start(l ^ dl, n, sizes), q), :] = mask_strip(
            zp, r, l ^ dl, n, far, strip[...], sizes
        )
    total = before[...]
    for d, message in zip(part, messages):
        piece = zs[...] if d == cols // 2 else z_full[:, columns_of(c ^ d, sizes)]
        total += turned_dot(piece, message[...])
    out[...] = total.astype(out.dtype)


def local(sizes, hamiltonian, inv_root, h_pattern, z_pattern):
    rows, cols, layers, per = sizes.rows, sizes.cols, sizes.layers, sizes.per
    q, cols_here, rows_here = sizes.quarter, sizes.cols_here, sizes.rows_here
    order = rows * rows_here
    height = per * q
    row_bits, layer_bits = bits_of(rows), bits_of(layers)
    f32 = jnp.float32
    strip_shape = shape(q, cols_here)

    striped = inv_root.reshape(per, layers, q, cols_here)
    l = lax.axis_index("layer")
    own = lax.dynamic_index_in_dim(striped, l, 1, keepdims=False).reshape(height, cols_here)
    slots = [own]
    right = left = own
    for s in range(1, cols):
        if s % 2:
            right = lax.ppermute(right, "col", [(i, (i + 1) % cols) for i in range(cols)])
        else:
            left = lax.ppermute(left, "col", [(i, (i - 1) % cols) for i in range(cols)])
        slots.append(right if s % 2 else left)

    def cross(piece):
        return lax.ppermute(piece, "layer", flip(layers, layer_bits[0]))

    top, low = layer_bits
    h_pattern, z_pattern, fetched = run(
        fetch_kernel,
        "fetch",
        [shape(*h_pattern.shape, jnp.int32)] * 2 + [shape(*hamiltonian.shape)],
        [h_pattern, z_pattern, hamiltonian],
    )
    h_pieces, h_table = [hamiltonian], [(0, 0)]
    for axis, bit in [("layer", top)] + [("row", b) for b in row_bits]:
        perm = flip(rows if axis == "row" else layers, bit)
        for piece, (dr, dl) in list(zip(h_pieces, h_table)):
            h_table.append((dr ^ bit, dl) if axis == "row" else (dr, dl ^ bit))
            if False:
                piece = pack([piece], [])
            h_pieces.append(lax.ppermute(piece, axis, perm))
    zm, *h_own = run(
        functools.partial(bring_kernel, sizes, h_table),
        "bring",
        [shape(height, order)] + [shape(cols_here, 2 * q)] * cols,
        [fetched, *h_pieces[1:], *slots[:-1]],
        smem=[h_pattern, z_pattern],
    )
    h_other = [lax.ppermute(block, "layer", flip(layers, low)) for block in h_own]
    product = run(
        functools.partial(first_kernel, sizes, top),
        "first_product",
        [shape(height, cols_here)],
        [zm, slots[-1], *h_own, *h_other],
        smem=[z_pattern],
        scratch=[pltpu.VMEM((height, order), jnp.bfloat16)],
    )[0]

    gathered = {0: product}
    for bit in row_bits:
        for dr, piece in list(gathered.items()):
            gathered[dr ^ bit] = lax.ppermute(piece, "row", flip(rows, bit))
    row_offsets = list(gathered)
    held, z_table = [inv_root], {}

    last = pack([slots[-1]], [product])
    last_top = cross(last)
    last_low = lax.ppermute(last, "layer", flip(layers, low))
    outgoing = run(
        functools.partial(route_kernel, sizes, row_offsets),
        "route",
        [shape(q, cols_here)] * cols,
        [gathered[o] for o in row_offsets],
        after=[last_low],
        scratch=[pltpu.VMEM((cols * q, cols_here), jnp.bfloat16)],
    )
    messages = [
        lax.ppermute(outgoing[d], "col", flip(cols, d)) for d in range(cols - 1, 0, -1)
    ]
    messages = [outgoing[0]] + messages[::-1]
    group = range(1, cols - 1)
    mine = pack([slots[s] for s in group])
    other = cross(mine)
    both = lax.ppermute(pack([mine, other], [outgoing[0]]), "layer", flip(layers, low))
    held, z_table = [inv_root, mine, other, both, last, last_low, last_top], {}
    for n, s in enumerate(group):
        row = n * height
        z_table[0, s], z_table[top, s], z_table[low, s] = (1, row), (2, row), (3, row)
        z_table[low ^ top, s] = (3, len(group) * height + row)
    for n, dl in enumerate((0, low, top)):
        z_table[dl, cols - 1] = (4 + n, 0)
    parts = run(split_kernel, "split", [strip_shape] * per, [last_top])
    parts = [lax.ppermute(part, "layer", flip(layers, low)) for part in parts]
    z_full = run(
        functools.partial(layers_kernel, sizes, z_table),
        "layers",
        [shape(rows_here, order)],
        held,
        smem=[z_pattern],
    )[0]
    early = [0, *range(cols - 1, cols // 2, -1)]
    late = range(cols // 2, 0, -1)
    total = run(
        functools.partial(second_kernel, sizes, early),
        "second_product",
        [shape(*hamiltonian.shape, f32)],
        [z_full, *[messages[d] for d in early]],
    )[0]
    return run(
        functools.partial(last_kernel, sizes, late, low ^ top),
        "last_product",
        [shape(*hamiltonian.shape)],
        [z_full, total, *[messages[d] for d in late], *parts],
        smem=[z_pattern],
        scratch=[pltpu.VMEM((rows_here, cols_here), jnp.bfloat16)],
    )[0]


def solution(mesh):
    rows, cols, layers = (mesh.shape[a] for a in ("row", "col", "layer"))

    def whole(hamiltonian, inv_root, h_pattern, z_pattern):
        order = hamiltonian.shape[0]
        cols_here = order // cols
        sizes = Sizes(
            rows, cols, layers, order // rows, cols_here, cols_here // layers, cols // rows
        )
        return jax.shard_map(
            functools.partial(local, sizes),
            mesh=mesh,
            in_specs=(P("row", ("col", "layer")), P("row", "col"), P(), P()),
            out_specs=P("row", ("col", "layer")),
            check_vma=False,
        )(hamiltonian, inv_root, h_pattern, z_pattern)

    return whole
```

```python
import functools
from typing import NamedTuple

import jax
import jax.numpy as jnp
from jax import lax
from jax.experimental import pallas as pl
from jax.experimental.pallas import tpu as pltpu
from jax.sharding import PartitionSpec as P

BS = 256
MARGIN = 4 * 1024 * 1024


class Sizes(NamedTuple):
    rows: int
    cols: int
    layers: int
    rows_here: int
    cols_here: int
    quarter: int
    per: int


def bits_of(size):
    return [1 << b for b in reversed(range(size.bit_length() - 1))]


def flip(size, bit):
    return [(i, i ^ bit) for i in range(size)]


def mod(a, n):
    return lax.rem(a + n, n)


def place():
    return lax.axis_index("row"), lax.axis_index("col"), lax.axis_index("layer")


def run(kernel, name, outs, arrays, smem=(), after=(), scratch=(), flops=0):
    size = sum(a.size * a.dtype.itemsize for a in arrays)
    size += sum(o.size * o.dtype.itemsize for o in outs)
    for kept in scratch:
        size += kept.shape[0] * kept.shape[1] * jnp.dtype(kept.dtype).itemsize
    skip = len(smem) + len(arrays)

    def body(*refs):
        kernel(*refs[:skip], *refs[skip + len(after) :])

    return pl.pallas_call(
        body,
        out_shape=list(outs),
        in_specs=[pl.BlockSpec(memory_space=pltpu.SMEM)] * len(smem)
        + [pl.BlockSpec(memory_space=pltpu.VMEM)] * len(arrays)
        + [pl.BlockSpec(memory_space=pl.ANY)] * len(after),
        out_specs=[pl.BlockSpec(memory_space=pltpu.VMEM)] * len(outs),
        scratch_shapes=list(scratch),
        compiler_params=pltpu.CompilerParams(vmem_limit_bytes=size + MARGIN),
        cost_estimate=pl.CostEstimate(flops=flops, bytes_accessed=size, transcendentals=0),
        name=name,
    )(*smem, *arrays, *after)


def shape(rows, columns, dtype=jnp.bfloat16):
    return jax.ShapeDtypeStruct((rows, columns), dtype)


def keep_block(pattern, i, j, block):
    return jnp.where(pattern[i, j] > 0, block, jnp.zeros_like(block))


def strip_start(l, half, sizes):
    return pl.multiple_of(half * sizes.cols_here + l * sizes.quarter, sizes.quarter)


def columns_of(cc, sizes):
    return pl.ds(pl.multiple_of(cc * sizes.cols_here, sizes.cols_here), sizes.cols_here)


def mask_strip(zp, r, l, half, cc, strip, sizes):
    block_row = (r * sizes.rows_here + half * sizes.cols_here + l * sizes.quarter) // BS
    first = cc * (sizes.cols_here // BS)
    return jnp.concatenate(
        [
            keep_block(zp, block_row, first + t, strip[:, t * BS : (t + 1) * BS])
            for t in range(sizes.cols_here // BS)
        ],
        axis=1,
    )


def mask_piece(zp, r, l, cc, piece, sizes):
    q = sizes.quarter
    return jnp.concatenate(
        [
            mask_strip(zp, r, l, half, cc, piece[half * q : (half + 1) * q, :], sizes)
            for half in range(sizes.per)
        ],
        axis=0,
    )


def pack_kernel(*refs):
    out, row = refs[-1], 0
    for ref in refs[:-1]:
        out[row : row + ref.shape[0], :] = ref[...]
        row += ref.shape[0]


def pack(pieces, after=()):
    height = sum(p.shape[0] for p in pieces)
    out = shape(height, pieces[0].shape[1])
    return run(pack_kernel, "pack", [out], pieces, after=after)[0]


def slot_column(c, s, cols):
    return mod(c - (s + 1) // 2 if s % 2 else c + s // 2, cols)


def mask_kernel(sizes, zp, *refs):
    slots, out = refs[:-1], refs[-1]
    r, c, l = place()
    out[...] = jnp.zeros_like(out)
    for s, slot in enumerate(slots):
        cc = slot_column(c, s, sizes.cols)
        out[:, columns_of(cc, sizes)] = mask_piece(zp, r, l, cc, slot[...], sizes)


def fetch_kernel(hp, zp, h, hp_out, zp_out, h_out):
    for ref, out in ((hp, hp_out), (zp, zp_out), (h, h_out)):
        out[...] = ref[...]


def bring_kernel(sizes, h_table, hp, zp, *refs):
    n = len(h_table)
    pieces, slots = refs[:n], refs[n : n + sizes.cols - 1]
    zm, sent, blocks = refs[n + sizes.cols - 1], refs[n + sizes.cols : 2 * n + sizes.cols - 1], refs[
        2 * n + sizes.cols - 1 :
    ]
    r, c, l = place()
    q, wide = sizes.quarter, blocks[0].shape[0]
    for h, (dr, dl) in zip(pieces, h_table):
        columns = slice(q, 2 * q) if dl else slice(0, q)
        block_col = (c * sizes.cols_here + (l ^ dl) * q) // BS
        for rr in range(sizes.rows):

            @pl.when((r ^ dr) == rr)
            def _(h=h, rr=rr, columns=columns, block_col=block_col):
                for first in range(0, sizes.rows_here, BS):
                    row = rr * sizes.rows_here + first
                    at = row % wide
                    blocks[row // wide][at : at + BS, columns] = keep_block(
                        hp, row // BS, block_col, h[first : first + BS, :]
                    )

    for (dr, dl), h, out in zip(h_table[1:], pieces[1:], sent):
        block_col = (c * sizes.cols_here + (l ^ dl) * q) // BS
        for first in range(0, sizes.rows_here, BS):
            j = ((r ^ dr) * sizes.rows_here + first) // BS
            out[first : first + BS, :] = keep_block(hp, j, block_col, h[first : first + BS, :])
    mask_kernel(sizes, zp, *slots, zm)


def first_kernel(sizes, top, h_table, hp, zp, zm, last, raw, *refs):
    cols, q, n = sizes.cols, sizes.quarter, len(h_table) - 1
    others, blocks, (out, zs, hs) = refs[:n], refs[n:-3], refs[-3:]
    r, c, l = place()
    cc = slot_column(c, cols - 1, cols)
    zs[...] = zm[...]
    zs[:, columns_of(cc, sizes)] = mask_piece(zp, r, l, cc, last[...], sizes)
    block_col = (c * sizes.cols_here + (l ^ 1) * q) // BS
    for first in range(0, sizes.rows_here, BS):
        j = (r * sizes.rows_here + first) // BS
        hs[first : first + BS, :] = keep_block(hp, j, block_col, raw[first : first + BS, :])
    width, acc = blocks[0].shape[0], None
    for n, block in enumerate(blocks):
        part = jnp.dot(
            zs[:, n * width : (n + 1) * width], block[...], preferred_element_type=jnp.float32
        )
        acc = part if acc is None else acc + part
    for n, ll in enumerate((l, l ^ top)):
        out[:, pl.ds(pl.multiple_of(ll * q, q), q)] = acc[:, n * q : (n + 1) * q].astype(out.dtype)
    for dl in (0, top):
        acc = None
        for (dr, there), h in zip(h_table, [hs, *others]):
            if there == dl:
                rows = pl.ds(
                    pl.multiple_of((r ^ dr) * sizes.rows_here, sizes.rows_here), sizes.rows_here
                )
                part = jnp.dot(zs[:, rows], h[...], preferred_element_type=jnp.float32)
                acc = part if acc is None else acc + part
        ll = l ^ 1 ^ dl
        out[:, pl.ds(pl.multiple_of(ll * q, q), q)] = acc.astype(out.dtype)


def route_kernel(sizes, row_offsets, *refs):
    n = len(row_offsets)
    pieces, outs, table = refs[:n], refs[n:-1], refs[-1]
    r, c, _ = place()
    q = sizes.quarter
    for dr, piece in zip(row_offsets, pieces):
        for half in range(sizes.per):
            start = pl.multiple_of(((r ^ dr) * sizes.per + half) * q, q)
            table[pl.ds(start, q), :] = piece[half * q : (half + 1) * q, :]
    for d, out in enumerate(outs):
        out[...] = table[pl.ds(pl.multiple_of((c ^ d) * q, q), q), :]


def split_kernel(*refs):
    pieces, outs = [], []
    for ref in refs:
        (pieces if ref.shape[0] > refs[-1].shape[0] else outs).append(ref)
    per, height = len(outs) // len(pieces), outs[0].shape[0]
    for n, out in enumerate(outs):
        first = n % per * height
        out[...] = pieces[n // per][first : first + height, :]


def layers_kernel(sizes, z_table, zp, *refs):
    cols, q = sizes.cols, sizes.quarter
    out, held = refs[-1], refs[:-1]
    r, c, l = place()
    for dl in range(sizes.layers):
        ll = l ^ dl
        for half in range(sizes.per):
            rows = pl.ds(strip_start(ll, half, sizes), q)
            for s in range(cols):
                cc = slot_column(c, s, cols)
                columns = columns_of(cc, sizes)
                if s and (dl, s) not in z_table:
                    out[rows, columns] = jnp.zeros((q, sizes.cols_here), out.dtype)
                    continue
                if s == 0:
                    strip = held[0][rows, :]
                else:
                    index, row = z_table[dl, s]
                    strip = held[index][row + half * q : row + (half + 1) * q, :]
                out[rows, columns] = mask_strip(zp, r, ll, half, cc, strip, sizes)


def turned_dot(left, right):
    return lax.dot_general(
        left, right, (((1,), (1,)), ((), ())), preferred_element_type=jnp.float32
    )


def second_kernel(sizes, part, z_full, *refs):
    messages, before, out = refs[: len(part)], refs[len(part) : -1], refs[-1]
    c = lax.axis_index("col")
    total = before[0][...] if before else None
    for d, message in zip(part, messages):
        added = turned_dot(z_full[:, columns_of(c ^ d, sizes)], message[...])
        total = added if total is None else total + added
    out[...] = total


def last_kernel(sizes, part, dl, zp, z_full, before, *refs):
    cols, q = sizes.cols, sizes.quarter
    messages, strips = refs[: len(part)], refs[len(part) : -2]
    out, zs = refs[-2:]
    r, c, l = place()
    far = c ^ (cols // 2)
    zs[...] = z_full[:, columns_of(far, sizes)]
    for n, strip in enumerate(strips):
        zs[pl.ds(strip_start(l ^ dl, n, sizes), q), :] = mask_strip(
            zp, r, l ^ dl, n, far, strip[...], sizes
        )
    total = before[...]
    for d, message in zip(part, messages):
        piece = zs[...] if d == cols // 2 else z_full[:, columns_of(c ^ d, sizes)]
        total += turned_dot(piece, message[...])
    out[...] = total.astype(out.dtype)


def local(sizes, hamiltonian, inv_root, h_pattern, z_pattern):
    rows, cols, layers, per = sizes.rows, sizes.cols, sizes.layers, sizes.per
    q, cols_here, rows_here = sizes.quarter, sizes.cols_here, sizes.rows_here
    order = rows * rows_here
    height = per * q
    row_bits, layer_bits = bits_of(rows), bits_of(layers)
    f32 = jnp.float32
    strip_shape = shape(q, cols_here)

    striped = inv_root.reshape(per, layers, q, cols_here)
    l = lax.axis_index("layer")
    own = lax.dynamic_index_in_dim(striped, l, 1, keepdims=False).reshape(height, cols_here)
    slots = [own]
    right = left = own
    for s in range(1, cols):
        if s % 2:
            right = lax.ppermute(right, "col", [(i, (i + 1) % cols) for i in range(cols)])
        else:
            left = lax.ppermute(left, "col", [(i, (i - 1) % cols) for i in range(cols)])
        slots.append(right if s % 2 else left)

    def cross(piece):
        return lax.ppermute(piece, "layer", flip(layers, layer_bits[0]))

    top, low = layer_bits
    h_pattern, z_pattern, fetched = run(
        fetch_kernel,
        "fetch",
        [shape(*h_pattern.shape, jnp.int32)] * 2 + [shape(*hamiltonian.shape)],
        [h_pattern, z_pattern, hamiltonian],
    )
    h_pieces, h_table = [hamiltonian], [(0, 0)]
    for axis, bit in [("layer", top)] + [("row", b) for b in row_bits]:
        perm = flip(rows if axis == "row" else layers, bit)
        for piece, (dr, dl) in list(zip(h_pieces, h_table)):
            h_table.append((dr ^ bit, dl) if axis == "row" else (dr, dl ^ bit))
            if False:
                piece = pack([piece], [])
            h_pieces.append(lax.ppermute(piece, axis, perm))
    raw = lax.ppermute(hamiltonian, "layer", flip(layers, low))
    group = range(1, cols - 1)
    mine = pack([slots[s] for s in group])
    other = cross(mine)
    n_sent = len(h_table) - 1
    zm, *h_own = run(
        functools.partial(bring_kernel, sizes, h_table),
        "bring",
        [shape(height, order)]
        + [shape(*hamiltonian.shape)] * n_sent
        + [shape(cols_here, 2 * q)] * cols,
        [fetched, *h_pieces[1:], *slots[:-1]],
        smem=[h_pattern, z_pattern],
        after=(),
    )
    sent, h_own = h_own[:n_sent], h_own[n_sent:]
    h_other = [lax.ppermute(piece, "layer", flip(layers, low)) for piece in sent]
    crossed = []
    product = run(
        functools.partial(first_kernel, sizes, top, h_table),
        "first_product",
        [shape(height, cols_here)],
        [zm, slots[-1], raw, *h_other, *h_own],
        smem=[h_pattern, z_pattern],
        scratch=[
            pltpu.VMEM((height, order), jnp.bfloat16),
            pltpu.VMEM(hamiltonian.shape, jnp.bfloat16),
        ],
    )[0]

    gathered = {0: product}
    for bit in row_bits:
        for dr, piece in list(gathered.items()):
            gathered[dr ^ bit] = lax.ppermute(piece, "row", flip(rows, bit))
    row_offsets = list(gathered)
    held, z_table = [inv_root], {}

    last = pack([slots[-1]], [product])
    last_top = cross(last)
    last_low = lax.ppermute(last, "layer", flip(layers, low))
    outgoing = run(
        functools.partial(route_kernel, sizes, row_offsets),
        "route",
        [shape(q, cols_here)] * cols,
        [gathered[o] for o in row_offsets],
        after=[last_low],
        scratch=[pltpu.VMEM((cols * q, cols_here), jnp.bfloat16)],
    )
    messages = [
        lax.ppermute(outgoing[d], "col", flip(cols, d)) for d in range(cols - 1, 0, -1)
    ]
    messages = [outgoing[0]] + messages[::-1]
    both = lax.ppermute(pack([mine, other], [outgoing[0]]), "layer", flip(layers, low))
    held, z_table = [inv_root, mine, other, both, last, last_low, last_top], {}
    for n, s in enumerate(group):
        row = n * height
        z_table[0, s], z_table[top, s], z_table[low, s] = (1, row), (2, row), (3, row)
        z_table[low ^ top, s] = (3, len(group) * height + row)
    for n, dl in enumerate((0, low, top)):
        z_table[dl, cols - 1] = (4 + n, 0)
    parts = run(split_kernel, "split", [strip_shape] * per, [last_top])
    parts = [lax.ppermute(part, "layer", flip(layers, low)) for part in parts]
    z_full = run(
        functools.partial(layers_kernel, sizes, z_table),
        "layers",
        [shape(rows_here, order)],
        held,
        smem=[z_pattern],
    )[0]
    early = [0, *range(cols - 1, cols // 2, -1)]
    late = range(cols // 2, 0, -1)
    total = run(
        functools.partial(second_kernel, sizes, early),
        "second_product",
        [shape(*hamiltonian.shape, f32)],
        [z_full, *[messages[d] for d in early]],
    )[0]
    return run(
        functools.partial(last_kernel, sizes, late, low ^ top),
        "last_product",
        [shape(*hamiltonian.shape)],
        [z_full, total, *[messages[d] for d in late], *parts],
        smem=[z_pattern],
        scratch=[pltpu.VMEM((rows_here, cols_here), jnp.bfloat16)],
    )[0]


def solution(mesh):
    rows, cols, layers = (mesh.shape[a] for a in ("row", "col", "layer"))

    def whole(hamiltonian, inv_root, h_pattern, z_pattern):
        order = hamiltonian.shape[0]
        cols_here = order // cols
        sizes = Sizes(
            rows, cols, layers, order // rows, cols_here, cols_here // layers, cols // rows
        )
        return jax.shard_map(
            functools.partial(local, sizes),
            mesh=mesh,
            in_specs=(P("row", ("col", "layer")), P("row", "col"), P(), P()),
            out_specs=P("row", ("col", "layer")),
            check_vma=False,
        )(hamiltonian, inv_root, h_pattern, z_pattern)

    return whole
```

```python
import functools
from typing import NamedTuple

import jax
import jax.numpy as jnp
from jax import lax
from jax.experimental import pallas as pl
from jax.experimental.pallas import tpu as pltpu
from jax.sharding import PartitionSpec as P

BS = 256
MARGIN = 4 * 1024 * 1024


class Sizes(NamedTuple):
    rows: int
    cols: int
    layers: int
    rows_here: int
    cols_here: int
    quarter: int
    per: int


def bits_of(size):
    return [1 << b for b in reversed(range(size.bit_length() - 1))]


def flip(size, bit):
    return [(i, i ^ bit) for i in range(size)]


def mod(a, n):
    return lax.rem(a + n, n)


def place():
    return lax.axis_index("row"), lax.axis_index("col"), lax.axis_index("layer")


def run(kernel, name, outs, arrays, smem=(), after=(), scratch=(), flops=0):
    size = sum(a.size * a.dtype.itemsize for a in arrays)
    size += sum(o.size * o.dtype.itemsize for o in outs)
    for kept in scratch:
        size += kept.shape[0] * kept.shape[1] * jnp.dtype(kept.dtype).itemsize
    skip = len(smem) + len(arrays)

    def body(*refs):
        kernel(*refs[:skip], *refs[skip + len(after) :])

    return pl.pallas_call(
        body,
        out_shape=list(outs),
        in_specs=[pl.BlockSpec(memory_space=pltpu.SMEM)] * len(smem)
        + [pl.BlockSpec(memory_space=pltpu.VMEM)] * len(arrays)
        + [pl.BlockSpec(memory_space=pl.ANY)] * len(after),
        out_specs=[pl.BlockSpec(memory_space=pltpu.VMEM)] * len(outs),
        scratch_shapes=list(scratch),
        compiler_params=pltpu.CompilerParams(vmem_limit_bytes=size + MARGIN),
        cost_estimate=pl.CostEstimate(flops=flops, bytes_accessed=size, transcendentals=0),
        name=name,
    )(*smem, *arrays, *after)


def shape(rows, columns, dtype=jnp.bfloat16):
    return jax.ShapeDtypeStruct((rows, columns), dtype)


def keep_block(pattern, i, j, block):
    return jnp.where(pattern[i, j] > 0, block, jnp.zeros_like(block))


def strip_start(l, half, sizes):
    return pl.multiple_of(half * sizes.cols_here + l * sizes.quarter, sizes.quarter)


def columns_of(cc, sizes):
    return pl.ds(pl.multiple_of(cc * sizes.cols_here, sizes.cols_here), sizes.cols_here)


def mask_strip(zp, r, l, half, cc, strip, sizes):
    block_row = (r * sizes.rows_here + half * sizes.cols_here + l * sizes.quarter) // BS
    first = cc * (sizes.cols_here // BS)
    return jnp.concatenate(
        [
            keep_block(zp, block_row, first + t, strip[:, t * BS : (t + 1) * BS])
            for t in range(sizes.cols_here // BS)
        ],
        axis=1,
    )


def mask_piece(zp, r, l, cc, piece, sizes):
    q = sizes.quarter
    return jnp.concatenate(
        [
            mask_strip(zp, r, l, half, cc, piece[half * q : (half + 1) * q, :], sizes)
            for half in range(sizes.per)
        ],
        axis=0,
    )


def pack_kernel(*refs):
    out, row = refs[-1], 0
    for ref in refs[:-1]:
        out[row : row + ref.shape[0], :] = ref[...]
        row += ref.shape[0]


def pack(pieces, after=()):
    height = sum(p.shape[0] for p in pieces)
    out = shape(height, pieces[0].shape[1])
    return run(pack_kernel, "pack", [out], pieces, after=after)[0]


def slot_column(c, s, cols):
    return mod(c - (s + 1) // 2 if s % 2 else c + s // 2, cols)


def mask_kernel(sizes, zp, *refs):
    slots, out = refs[:-1], refs[-1]
    r, c, l = place()
    out[...] = jnp.zeros_like(out)
    for s, slot in enumerate(slots):
        cc = slot_column(c, s, sizes.cols)
        out[:, columns_of(cc, sizes)] = mask_piece(zp, r, l, cc, slot[...], sizes)


def fetch_kernel(hp, zp, h, hp_out, zp_out, h_out):
    for ref, out in ((hp, hp_out), (zp, zp_out), (h, h_out)):
        out[...] = ref[...]


def bring_kernel(sizes, h_table, hp, zp, *refs):
    n = len(h_table)
    pieces, slots = refs[:n], refs[n : n + sizes.cols - 1]
    zm, sent, blocks = refs[n + sizes.cols - 1], refs[n + sizes.cols : 2 * n + sizes.cols - 1], refs[
        2 * n + sizes.cols - 1 :
    ]
    r, c, l = place()
    q, wide = sizes.quarter, blocks[0].shape[0]
    for h, (dr, dl) in zip(pieces, h_table):
        columns = slice(q, 2 * q) if dl else slice(0, q)
        block_col = (c * sizes.cols_here + (l ^ dl) * q) // BS
        for rr in range(sizes.rows):

            @pl.when((r ^ dr) == rr)
            def _(h=h, rr=rr, columns=columns, block_col=block_col):
                for first in range(0, sizes.rows_here, BS):
                    row = rr * sizes.rows_here + first
                    at = row % wide
                    blocks[row // wide][at : at + BS, columns] = keep_block(
                        hp, row // BS, block_col, h[first : first + BS, :]
                    )

    for (dr, dl), h, out in zip(h_table[1:], pieces[1:], sent):
        block_col = (c * sizes.cols_here + (l ^ dl) * q) // BS
        for first in range(0, sizes.rows_here, BS):
            j = ((r ^ dr) * sizes.rows_here + first) // BS
            out[first : first + BS, :] = keep_block(hp, j, block_col, h[first : first + BS, :])
    mask_kernel(sizes, zp, *slots, zm)


def first_kernel(sizes, top, h_table, hp, zp, zm, last, raw, *refs):
    cols, q, n = sizes.cols, sizes.quarter, len(h_table) - 1
    others, blocks, (out, zs, hs) = refs[:n], refs[n:-3], refs[-3:]
    r, c, l = place()
    cc = slot_column(c, cols - 1, cols)
    zs[...] = zm[...]
    zs[:, columns_of(cc, sizes)] = mask_piece(zp, r, l, cc, last[...], sizes)
    block_col = (c * sizes.cols_here + (l ^ 1) * q) // BS
    high = sizes.rows_here
    for (dr, dl), h in zip(h_table, [raw, *others]):
        columns = slice(q, 2 * q) if dl else slice(0, q)
        if dr or dl:
            hs[dr * high : (dr + 1) * high, columns] = h[...]
            continue
        for first in range(0, high, BS):
            j = (r * high + first) // BS
            hs[first : first + BS, columns] = keep_block(
                hp, j, block_col, h[first : first + BS, :]
            )
    width, acc = blocks[0].shape[0], None
    for n, block in enumerate(blocks):
        part = jnp.dot(
            zs[:, n * width : (n + 1) * width], block[...], preferred_element_type=jnp.float32
        )
        acc = part if acc is None else acc + part
    for n, ll in enumerate((l, l ^ top)):
        out[:, pl.ds(pl.multiple_of(ll * q, q), q)] = acc[:, n * q : (n + 1) * q].astype(out.dtype)
    acc = None
    for dr in range(sizes.rows):
        rows = pl.ds(pl.multiple_of((r ^ dr) * high, high), high)
        part = jnp.dot(
            zs[:, rows], hs[dr * high : (dr + 1) * high, :], preferred_element_type=jnp.float32
        )
        acc = part if acc is None else acc + part
    for n, ll in enumerate((l ^ 1, l ^ 1 ^ top)):
        out[:, pl.ds(pl.multiple_of(ll * q, q), q)] = acc[:, n * q : (n + 1) * q].astype(out.dtype)


def route_kernel(sizes, row_offsets, *refs):
    n = len(row_offsets)
    pieces, outs, table = refs[:n], refs[n:-1], refs[-1]
    r, c, _ = place()
    q = sizes.quarter
    for dr, piece in zip(row_offsets, pieces):
        for half in range(sizes.per):
            start = pl.multiple_of(((r ^ dr) * sizes.per + half) * q, q)
            table[pl.ds(start, q), :] = piece[half * q : (half + 1) * q, :]
    for d, out in enumerate(outs):
        out[...] = table[pl.ds(pl.multiple_of((c ^ d) * q, q), q), :]


def split_kernel(*refs):
    pieces, outs = [], []
    for ref in refs:
        (pieces if ref.shape[0] > refs[-1].shape[0] else outs).append(ref)
    per, height = len(outs) // len(pieces), outs[0].shape[0]
    for n, out in enumerate(outs):
        first = n % per * height
        out[...] = pieces[n // per][first : first + height, :]


def layers_kernel(sizes, z_table, zp, *refs):
    cols, q = sizes.cols, sizes.quarter
    out, held = refs[-1], refs[:-1]
    r, c, l = place()
    for dl in range(sizes.layers):
        ll = l ^ dl
        for half in range(sizes.per):
            rows = pl.ds(strip_start(ll, half, sizes), q)
            for s in range(cols):
                cc = slot_column(c, s, cols)
                columns = columns_of(cc, sizes)
                if s and (dl, s) not in z_table:
                    out[rows, columns] = jnp.zeros((q, sizes.cols_here), out.dtype)
                    continue
                if s == 0:
                    strip = held[0][rows, :]
                else:
                    index, row = z_table[dl, s]
                    strip = held[index][row + half * q : row + (half + 1) * q, :]
                out[rows, columns] = mask_strip(zp, r, ll, half, cc, strip, sizes)


def turned_dot(left, right):
    return lax.dot_general(
        left, right, (((1,), (1,)), ((), ())), preferred_element_type=jnp.float32
    )


def second_kernel(sizes, part, z_full, *refs):
    messages, before, out = refs[: len(part)], refs[len(part) : -1], refs[-1]
    c = lax.axis_index("col")
    total = before[0][...] if before else None
    for d, message in zip(part, messages):
        added = turned_dot(z_full[:, columns_of(c ^ d, sizes)], message[...])
        total = added if total is None else total + added
    out[...] = total


def last_kernel(sizes, part, dl, zp, z_full, before, *refs):
    cols, q = sizes.cols, sizes.quarter
    messages, strips = refs[: len(part)], refs[len(part) : -2]
    out, zs = refs[-2:]
    r, c, l = place()
    far = c ^ (cols // 2)
    zs[...] = z_full[:, columns_of(far, sizes)]
    for n, strip in enumerate(strips):
        zs[pl.ds(strip_start(l ^ dl, n, sizes), q), :] = mask_strip(
            zp, r, l ^ dl, n, far, strip[...], sizes
        )
    total = before[...]
    for d, message in zip(part, messages):
        piece = zs[...] if d == cols // 2 else z_full[:, columns_of(c ^ d, sizes)]
        total += turned_dot(piece, message[...])
    out[...] = total.astype(out.dtype)


def local(sizes, hamiltonian, inv_root, h_pattern, z_pattern):
    rows, cols, layers, per = sizes.rows, sizes.cols, sizes.layers, sizes.per
    q, cols_here, rows_here = sizes.quarter, sizes.cols_here, sizes.rows_here
    order = rows * rows_here
    height = per * q
    row_bits, layer_bits = bits_of(rows), bits_of(layers)
    f32 = jnp.float32
    strip_shape = shape(q, cols_here)

    striped = inv_root.reshape(per, layers, q, cols_here)
    l = lax.axis_index("layer")
    own = lax.dynamic_index_in_dim(striped, l, 1, keepdims=False).reshape(height, cols_here)
    slots = [own]
    right = left = own
    for s in range(1, cols):
        if s % 2:
            right = lax.ppermute(right, "col", [(i, (i + 1) % cols) for i in range(cols)])
        else:
            left = lax.ppermute(left, "col", [(i, (i - 1) % cols) for i in range(cols)])
        slots.append(right if s % 2 else left)

    def cross(piece):
        return lax.ppermute(piece, "layer", flip(layers, layer_bits[0]))

    top, low = layer_bits
    h_pattern, z_pattern, fetched = run(
        fetch_kernel,
        "fetch",
        [shape(*h_pattern.shape, jnp.int32)] * 2 + [shape(*hamiltonian.shape)],
        [h_pattern, z_pattern, hamiltonian],
    )
    h_pieces, h_table = [hamiltonian], [(0, 0)]
    for axis, bit in [("layer", top)] + [("row", b) for b in row_bits]:
        perm = flip(rows if axis == "row" else layers, bit)
        for piece, (dr, dl) in list(zip(h_pieces, h_table)):
            h_table.append((dr ^ bit, dl) if axis == "row" else (dr, dl ^ bit))
            if False:
                piece = pack([piece], [])
            h_pieces.append(lax.ppermute(piece, axis, perm))
    raw = lax.ppermute(hamiltonian, "layer", flip(layers, low))
    group = range(1, cols - 1)
    mine = pack([slots[s] for s in group])
    other = cross(mine)
    n_sent = len(h_table) - 1
    zm, *h_own = run(
        functools.partial(bring_kernel, sizes, h_table),
        "bring",
        [shape(height, order)]
        + [shape(*hamiltonian.shape)] * n_sent
        + [shape(cols_here, 2 * q)] * cols,
        [fetched, *h_pieces[1:], *slots[:-1]],
        smem=[h_pattern, z_pattern],
        after=(),
    )
    sent, h_own = h_own[:n_sent], h_own[n_sent:]
    h_other = [lax.ppermute(piece, "layer", flip(layers, low)) for piece in sent]
    crossed = []
    product = run(
        functools.partial(first_kernel, sizes, top, h_table),
        "first_product",
        [shape(height, cols_here)],
        [zm, slots[-1], raw, *h_other, *h_own],
        smem=[h_pattern, z_pattern],
        scratch=[
            pltpu.VMEM((height, order), jnp.bfloat16),
            pltpu.VMEM((order, 2 * q), jnp.bfloat16),
        ],
    )[0]

    gathered = {0: product}
    for bit in row_bits:
        for dr, piece in list(gathered.items()):
            gathered[dr ^ bit] = lax.ppermute(piece, "row", flip(rows, bit))
    row_offsets = list(gathered)
    held, z_table = [inv_root], {}

    last = pack([slots[-1]], [product])
    last_top = cross(last)
    last_low = lax.ppermute(last, "layer", flip(layers, low))
    outgoing = run(
        functools.partial(route_kernel, sizes, row_offsets),
        "route",
        [shape(q, cols_here)] * cols,
        [gathered[o] for o in row_offsets],
        after=[last_low],
        scratch=[pltpu.VMEM((cols * q, cols_here), jnp.bfloat16)],
    )
    messages = [
        lax.ppermute(outgoing[d], "col", flip(cols, d)) for d in range(cols - 1, 0, -1)
    ]
    messages = [outgoing[0]] + messages[::-1]
    both = lax.ppermute(pack([mine, other], [outgoing[0]]), "layer", flip(layers, low))
    held, z_table = [inv_root, mine, other, both, last, last_low, last_top], {}
    for n, s in enumerate(group):
        row = n * height
        z_table[0, s], z_table[top, s], z_table[low, s] = (1, row), (2, row), (3, row)
        z_table[low ^ top, s] = (3, len(group) * height + row)
    for n, dl in enumerate((0, low, top)):
        z_table[dl, cols - 1] = (4 + n, 0)
    parts = run(split_kernel, "split", [strip_shape] * per, [last_top])
    parts = [lax.ppermute(part, "layer", flip(layers, low)) for part in parts]
    z_full = run(
        functools.partial(layers_kernel, sizes, z_table),
        "layers",
        [shape(rows_here, order)],
        held,
        smem=[z_pattern],
    )[0]
    early = [0, *range(cols - 1, cols // 2, -1)]
    late = range(cols // 2, 0, -1)
    total = run(
        functools.partial(second_kernel, sizes, early),
        "second_product",
        [shape(*hamiltonian.shape, f32)],
        [z_full, *[messages[d] for d in early]],
    )[0]
    return run(
        functools.partial(last_kernel, sizes, late, low ^ top),
        "last_product",
        [shape(*hamiltonian.shape)],
        [z_full, total, *[messages[d] for d in late], *parts],
        smem=[z_pattern],
        scratch=[pltpu.VMEM((rows_here, cols_here), jnp.bfloat16)],
    )[0]


def solution(mesh):
    rows, cols, layers = (mesh.shape[a] for a in ("row", "col", "layer"))

    def whole(hamiltonian, inv_root, h_pattern, z_pattern):
        order = hamiltonian.shape[0]
        cols_here = order // cols
        sizes = Sizes(
            rows, cols, layers, order // rows, cols_here, cols_here // layers, cols // rows
        )
        return jax.shard_map(
            functools.partial(local, sizes),
            mesh=mesh,
            in_specs=(P("row", ("col", "layer")), P("row", "col"), P(), P()),
            out_specs=P("row", ("col", "layer")),
            check_vma=False,
        )(hamiltonian, inv_root, h_pattern, z_pattern)

    return whole
```
